128 devices in a mesh: span: 16 (over z, y), dp: 4 (over x_lo, core), mp: 2 (over x_hi).
Axes of the slice: x: 4 (x_hi: 2, x_lo: 2; x = x_hi * 2 + x_lo), y: 4, z: 4, core: 2. Of those that a mesh axis runs over, the one named last changes fastest.
Arguments:
- span_states: bfloat16 [8, 2048, 4096], P('dp', 'span', 'mp'), may hold values from -6 to 6
- queries: bfloat16 [8, 2048, 2048], P('dp', 'span', 'mp'), may hold values from -6 to 6
- out_grad: bfloat16 [8, 2048, 2048], P('dp', 'span', 'mp'), may hold values from -6 to 6
- neighbour_ids: int32 [8, 32, 2, 128], P('dp'), may hold values from 0 to 63999
- assignment: int32 [4, 16, 8, 1], P('dp'), may hold values from 0 to 15; in each aligned block of 8 rows (0 to 7, 8 to 15, ..., all dimensions but the last counted through in order) no two rows name the same one
- embed_table: bfloat16 [64000, 896], P('span'), may hold values from -6 to 6
- w_span_kv: bfloat16 [4096, 1792], P('mp'), may hold values from -0.09375 to 0.09375
- w_query_enc: bfloat16 [896, 896], P(None, 'mp'), may hold values from -0.1875 to 0.1875
- w_out_enc: bfloat16 [896, 896], P('mp'), may hold values from -0.1875 to 0.1875
- w_dec_kv: bfloat16 [896, 2, 2048], P(None, None, 'mp'), may hold values from -0.1875 to 0.1875
Outputs:
- cross_out: bfloat16 [8, 2048, 2048], P('dp', 'span', 'mp')
- attended: bfloat16 [4, 16, 16, 1, 128, 896], P('dp', 'span', None, None, None, 'mp')
- grad_query_enc: float32 [896, 896], P(('span', 'dp'), 'mp')
- grad_out_enc: float32 [896, 896], P('mp', ('span', 'dp'))
The draws below stay inside these ranges and needn't reach their ends.
Inputs may be any that keep to these rules, and one draw needn't show every extreme that they name: `assignment`: among the 8 rows of one span device, no encoder index appears more than 1 times, and in every draw some device names one encoder exactly 1 times.
All inputs are finite; a program needn't handle non-finite values.
Results may differ from the reference program's by a relative error of at most 0.033.
Values may be sent and summed in bfloat16 or wider, within the bound.
A program may use at most 128 MiB of HBM per device.

```python
import math
import jax
import jax.numpy as jnp
import numpy as np
from jax import lax

D = 4096
HEADS = 16
HD = 128
DE = 896
EHD = 64
EH = 14
VOCAB = 64000
R = 128
CH = 64
NB = 2
LOCAL = 2
SEQS = 2
SEQS_TOT = 8
NCH = 32
L = 2048
UNITS = 8
CAP = 1
ENCS = 16
GROUPS = 4
N_SPAN = 16
N_DP = 4
N_MP = 2


def with_ends(entries, key, smallest, top_value):
    place = [jax.random.randint(jax.random.fold_in(key, axis), (), 0, length) for axis, length in enumerate(entries.shape)]
    longest = entries.shape.index(max(entries.shape))
    beside = place[:longest] + [(place[longest] + 1) % entries.shape[longest]] + place[longest + 1:]
    return entries.at[tuple(place)].set(smallest).at[tuple(beside)].set(top_value)


def block_scale(key, extent, pieces, least, largest):
    loudness = 1.0
    for dim, parts in pieces:
        steps = jax.random.uniform(jax.random.fold_in(jax.random.fold_in(key, 6), dim), (parts,), jnp.float32, least / len(pieces), largest / len(pieces))
        loudness = loudness * jnp.repeat(jnp.exp(steps), extent[dim] // parts).reshape((-1,) + (1,) * (len(extent) - 1 - dim))
    return loudness


def rank_bounds(number_of, lean):
    weights = [(1 << 20) // math.isqrt(standing ** lean) + 1 for standing in range(1, number_of + 1)]
    scale = 1 + sum(weights) // (1 << 30)
    return np.cumsum(np.array([max(1, weight // scale) for weight in weights]))


def ranked(own_key, extent, number_of, lean):
    table = rank_bounds(number_of, lean)
    lot = jax.random.randint(jax.random.fold_in(own_key, 1), extent, 0, int(table[number_of - 1]))
    grade = jnp.searchsorted(jnp.asarray(table, jnp.int32), lot, side="right")
    return jax.random.permutation(jax.random.fold_in(own_key, 2), number_of)[grade].astype(jnp.int32)


def deal_out(key, own, number, rows, amount, top, limit, lean):
    sequence = jax.random.permutation(key, amount)
    crowded, usual = load_shares(amount, rows * top, limit, lean, True), load_shares(amount, rows * top, limit, lean, False)
    places = jnp.arange(amount)

    def named(tallies, rotation):
        used = int((tallies > 0).sum())
        fixed = max(1, used // 4)
        moved = fixed + (places - fixed + rotation * (used - fixed)) % max(1, amount - fixed)
        return jnp.zeros((amount,), jnp.int32).at[sequence[jnp.where(places < fixed, places, moved)]].set(jnp.asarray(tallies, jnp.int32))

    tallies = jnp.where(number % 4 == 0, named(crowded, number // 4), named(usual, number - number // 4 - 1))
    mixed = jax.random.permutation(jax.random.fold_in(own, 3), amount)
    giver, taker = mixed[0:amount // 2 * 2:2], mixed[1:amount // 2 * 2:2]
    slack = jnp.minimum(tallies[giver] - 1, limit - tallies[taker]) // 2
    slack = jnp.where((giver == sequence[0]) | (taker == sequence[0]) | (tallies[taker] == 0), 0, jnp.maximum(slack, 0))
    moved = jax.random.randint(jax.random.fold_in(own, 4), (amount // 2,), 0, 1 << 20) % (slack + 1)
    tallies = tallies.at[giver].add(-moved).at[taker].add(moved)
    items = jnp.searchsorted(jnp.cumsum(tallies), jnp.arange(rows * top), side="right").astype(jnp.int32)
    grid = items.reshape(top, rows).T
    grid = grid[jax.random.permutation(jax.random.fold_in(own, 1), rows)]
    rotation = jax.random.randint(jax.random.fold_in(own, 2), (rows, 1), 0, top)
    return jnp.take_along_axis(grid, (jnp.arange(top)[None, :] + rotation) % top, axis=1)


def load_shares(count, total, reach, lean, full):
    weights = [(1 << 20) // math.isqrt(rank ** lean) + 1 for rank in range(1, count + 1)]
    largest = reach if full else min(reach, max(-(-total // count), total * weights[0] // sum(weights)))
    least = 1 if total - largest >= count - 1 else 0
    counts, rest = [largest] + [least] * (count - 1), total - largest - least * (count - 1)
    while rest > 0:
        free = [i for i in range(1, count) if counts[i] < largest] or [i for i in range(1, count) if counts[i] < reach]
        whole, remaining = sum([weights[i] for i in free]), rest
        for i in free:
            more = min(reach - counts[i], max(1, remaining * weights[i] // whole), rest)
            counts[i] = counts[i] + more
            rest = rest - more
    return np.array(counts)


def noise(rng, shape, width, reach, split=(), kind=jnp.bfloat16):
    values = width * jax.random.normal(rng, shape, jnp.float32)
    if split:
        values = values * block_scale(rng, shape, split, -0.22, 0.18)
    return jnp.clip(values, -reach, reach).astype(kind)


def setup_inputs(seed: int = 0) -> dict:
    key_list = jax.random.split(jax.random.key(seed), 11)
    span_states = noise(key_list[0], (SEQS_TOT, L, D), 1.0, 6.0, ((0, 4), (1, 16), (2, 2)))
    queries = noise(key_list[1], (SEQS_TOT, L, HEADS * HD), 1.0, 6.0, ((0, 4), (1, 16), (2, 2)))
    out_grad = noise(key_list[2], (SEQS_TOT, L, HEADS * HD), 1.0, 6.0, ((0, 4), (1, 16), (2, 2)))
    neighbour_ids = with_ends(ranked(key_list[3], (SEQS_TOT, NCH, NB, R), VOCAB, 2), jax.random.fold_in(key_list[3], 3), 0, VOCAB - 1).astype(jnp.int32)
    assignment_keys = jax.random.split(jax.random.fold_in(key_list[4], 1), GROUPS * ENCS * UNITS // UNITS)
    assignment_turns = jax.random.permutation(jax.random.fold_in(key_list[4], 3), GROUPS * ENCS * UNITS // UNITS)
    assignment = jax.vmap(lambda own, number: deal_out(jax.random.fold_in(key_list[4], 2), own, number, UNITS, ENCS, 1, CAP, 0))(assignment_keys, assignment_turns).reshape((GROUPS, ENCS, UNITS, 1))
    embed_table = noise(key_list[5], (VOCAB, DE), 1.0, 6.0, ((0, 16),))
    w_span_kv = noise(key_list[6], (D, 2 * DE), D ** -0.5, 0.09375, ((0, 2),))
    w_query_enc = noise(key_list[7], (DE, DE), DE ** -0.5, 0.1875, ((1, 2),))
    w_out_enc = noise(key_list[8], (DE, DE), DE ** -0.5, 0.1875, ((0, 2),))
    w_dec_kv = noise(key_list[9], (DE, 2, HEADS * HD), DE ** -0.5, 0.1875, ((2, 2),))
    return {"span_states": span_states, "queries": queries, "out_grad": out_grad, "neighbour_ids": neighbour_ids, "assignment": assignment, "embed_table": embed_table, "w_span_kv": w_span_kv, "w_query_enc": w_query_enc, "w_out_enc": w_out_enc, "w_dec_kv": w_dec_kv}


def softmax_grad(probs_full, grad_probs, row_terms, scale):
    return (probs_full * (grad_probs - row_terms[..., None]) / scale).astype(jnp.bfloat16)

def reference(span_states, queries, out_grad, neighbour_ids, assignment, embed_table, w_span_kv, w_query_enc, w_out_enc, w_dec_kv):
    f32 = jnp.float32
    bf16 = jnp.bfloat16
    half_width = D // N_MP
    enc_cols = DE // N_MP
    dec_cols = HEADS * HD // N_MP
    head_group = HEADS // N_MP
    w_dec_flat = w_dec_kv.reshape(DE, 2 * HEADS * HD)

    def one_sequence(seq_item):
        states, query_seq, grad_seq, ids_seq = seq_item
        running = jnp.zeros((L, 2 * DE), f32)
        for group in range(N_MP):
            partial_value = jnp.dot(states[:, group * half_width:(group + 1) * half_width], w_span_kv[group * half_width:(group + 1) * half_width], preferred_element_type=f32).astype(bf16)
            running = running + partial_value.astype(f32)
        span_kv = running.astype(bf16).reshape(NCH, CH, 2, EH, EHD)
        key_rows = span_kv[:, :, 0].astype(f32)
        value_rows = span_kv[:, :, 1].astype(f32)
        embedded = embed_table[ids_seq].reshape(NCH * NB * R, DE)
        enc_query = jnp.dot(embedded, w_query_enc, preferred_element_type=f32).astype(bf16).reshape(NCH, NB, R, EH, EHD)
        scores = jnp.einsum('cnqhd,ckhd->cnhqk', enc_query.astype(f32), key_rows) / math.sqrt(EHD)
        enc_full = jax.nn.softmax(scores, axis=-1)
        enc_weights = enc_full.astype(bf16).astype(f32)
        attended = jnp.einsum('cnhqk,ckhd->cnqhd', enc_weights, value_rows).astype(bf16)
        att_flat = attended.reshape(NCH * NB * R, DE)
        running = jnp.zeros((NCH * NB * R, DE), f32)
        for group in range(N_MP):
            partial_value = (embedded.astype(f32) / N_MP + jnp.dot(att_flat[:, group * enc_cols:(group + 1) * enc_cols], w_out_enc[group * enc_cols:(group + 1) * enc_cols], preferred_element_type=f32)).astype(bf16)
            running = running + partial_value.astype(f32)
        encoded = running.astype(bf16)
        dec_kv = jnp.dot(encoded, w_dec_flat, preferred_element_type=f32).astype(bf16).reshape(NCH, NB * R, 2, HEADS, HD)
        dec_keys = dec_kv[:, :, 0].astype(f32)
        dec_values = dec_kv[:, :, 1].astype(f32)
        dec_query = query_seq.reshape(NCH, CH, HEADS, HD).astype(f32)
        dec_scores = jnp.einsum('cqhd,ckhd->chqk', dec_query, dec_keys) / math.sqrt(HD)
        dec_full = jax.nn.softmax(dec_scores, axis=-1)
        dec_weights = dec_full.astype(bf16).astype(f32)
        cross = jnp.einsum('chqk,ckhd->cqhd', dec_weights, dec_values).astype(bf16)
        grad_cross = grad_seq.reshape(NCH, CH, HEADS, HD).astype(f32)
        grad_values = jnp.einsum('chqk,cqhd->ckhd', dec_weights, grad_cross).astype(bf16)
        grad_probs = jnp.einsum('cqhd,ckhd->chqk', grad_cross, dec_values)
        row_terms = jnp.einsum('cqhd,cqhd->chq', grad_cross, cross.astype(f32))
        grad_scores = softmax_grad(dec_full, grad_probs, row_terms, math.sqrt(HD))
        grad_keys = jnp.einsum('chqk,cqhd->ckhd', grad_scores.astype(f32), dec_query).astype(bf16)
        grad_kv = jnp.stack([grad_keys, grad_values], axis=2)
        running = jnp.zeros((NCH * NB * R, DE), f32)
        for group in range(N_MP):
            grad_block = grad_kv[:, :, :, group * head_group:(group + 1) * head_group].reshape(NCH * NB * R, 2 * dec_cols)
            w_group = w_dec_kv[:, :, group * dec_cols:(group + 1) * dec_cols].reshape(DE, 2 * dec_cols)
            partial_value = jnp.dot(grad_block, w_group.T, preferred_element_type=f32).astype(bf16)
            running = running + partial_value.astype(f32)
        grad_encoded = running.astype(bf16)
        grad_out_w = jnp.dot(att_flat.T, grad_encoded, preferred_element_type=f32)
        grad_att = jnp.dot(grad_encoded, w_out_enc.T, preferred_element_type=f32).astype(bf16).reshape(NCH, NB, R, EH, EHD).astype(f32)
        enc_grad_probs = jnp.einsum('cnqhd,ckhd->cnhqk', grad_att, value_rows)
        enc_rows = jnp.einsum('cnqhd,cnqhd->cnhq', grad_att, attended.astype(f32))
        enc_grad_scores = softmax_grad(enc_full, enc_grad_probs, enc_rows, math.sqrt(EHD))
        grad_enc_query = jnp.einsum('cnhqk,ckhd->cnqhd', enc_grad_scores.astype(f32), key_rows).astype(bf16).reshape(NCH * NB * R, DE)
        grad_query_w = jnp.dot(embedded.T, grad_enc_query, preferred_element_type=f32)
        return (attended.reshape(NCH, NB, R, DE), cross.reshape(L, HEADS * HD), grad_query_w, grad_out_w)
    att_all, cross_all, grad_q_all, grad_o_all = lax.map(one_sequence, (span_states, queries, out_grad, neighbour_ids))
    att_units = att_all.reshape(N_DP, SEQS, N_SPAN, LOCAL, NB, R, DE)
    att_units = jnp.transpose(att_units, (0, 2, 1, 3, 4, 5, 6)).reshape(N_DP, N_SPAN, UNITS, R, DE)
    dest = assignment[..., 0]
    targets = jnp.arange(N_SPAN, dtype=jnp.int32)
    onehot = (dest[..., None] == targets).astype(jnp.int32)
    rank_rows = lax.optimization_barrier(jnp.sum(onehot * jnp.cumsum(onehot, axis=2), axis=3)) - 1
    slot_ids = jnp.arange(CAP, dtype=jnp.int32)

    def one_group(group_item):
        units_group, dest_group, rank_group = group_item
        select = ((dest_group[None, :, None, :] == targets[:, None, None, None]) & (rank_group[None, :, None, :] == slot_ids[None, None, :, None])).astype(f32)
        return jnp.einsum('eicu,iurx->eicrx', select, units_group.astype(f32)).astype(bf16)
    slots_all = lax.map(one_group, (att_units, dest, rank_rows))
    return (cross_all, slots_all, lax.optimization_barrier(jnp.sum(grad_q_all, axis=0)), lax.optimization_barrier(jnp.sum(grad_o_all, axis=0)))
```

```python
import math

import jax
import jax.numpy as jnp
from jax import lax
from jax.sharding import PartitionSpec as P

HD = 128
DE = 896
EHD = 64
R = 128
CH = 64
NB = 2
ROOM = 48


def softmax_grad(probs_full, grad_probs, row_terms, scale):
    return (probs_full * (grad_probs - row_terms[..., None]) / scale).astype(jnp.bfloat16)


def lists(ids_m, span_index, vocab_rows, n_span):
    tokens = ids_m.shape[1]
    t = jnp.arange(tokens, dtype=jnp.int32)
    same = ids_m[:, :, None] == ids_m[:, None, :]
    dup = jnp.any(same & (t[None, None, :] < t[None, :, None]), axis=2)
    uniq = jnp.logical_not(dup)
    src = ids_m // vocab_rows
    shards = jnp.arange(n_span, dtype=jnp.int32)
    counts = jnp.sum(
        (uniq[:, None, :] & (src[:, None, :] == shards[None, :, None])).astype(jnp.int32), axis=2
    )
    over = jnp.max(counts) > ROOM
    sel = uniq & (src == span_index)
    tri = (t[:, None] < t[None, :]).astype(jnp.bfloat16)
    rank = jnp.dot(sel.astype(jnp.bfloat16), tri, preferred_element_type=jnp.float32).astype(
        jnp.int32
    )
    room = jnp.arange(ROOM, dtype=jnp.int32)
    local = ids_m - span_index * vocab_rows
    rows = jnp.sum(
        jnp.where(
            (rank[:, None, :] == room[None, :, None]) & sel[:, None, :], local[:, None, :], 0
        ),
        axis=2,
    )
    own = lax.dynamic_index_in_dim(ids_m, span_index, 0, keepdims=False)
    own_src = own // vocab_rows
    own_same = own[:, None] == own[None, :]
    first = jnp.min(jnp.where(own_same, t[None, :], tokens), axis=1)
    own_uniq = first == t
    own_rank = jnp.sum(
        (
            own_uniq[None, :]
            & (own_src[:, None] == own_src[None, :])
            & (t[None, :] < first[:, None])
        ).astype(jnp.int32),
        axis=1,
    )
    return rows, own_src * ROOM + own_rank, over


def body(
    span_states,
    queries,
    out_grad,
    neighbour_ids,
    assignment,
    embed_table,
    w_span_kv,
    w_query_enc,
    w_out_enc,
    w_dec_kv,
):
    f32 = jnp.float32
    bf16 = jnp.bfloat16
    n_span = lax.axis_size("span")
    span_index = lax.axis_index("span")
    half_index = lax.axis_index("mp")
    seq_count, local_tokens, half_width = span_states.shape
    spans = local_tokens // CH
    units = spans * NB
    dec_cols = 2 * queries.shape[2]
    heads_dec = dec_cols // HD
    heads_enc = DE // EHD
    enc_cols = w_query_enc.shape[1]
    vocab_rows = embed_table.shape[0]
    tokens = units * R

    ids_m = lax.dynamic_index_in_dim(
        neighbour_ids.reshape(seq_count, n_span, tokens), half_index, 0, keepdims=False
    )
    rows, pos, over = lists(ids_m, span_index, vocab_rows, n_span)
    over = lax.pmax(over.astype(jnp.int32), ("dp", "mp"))
    sent = jnp.take(embed_table, rows.reshape(-1), axis=0).reshape(n_span, ROOM, DE)
    got = lax.all_to_all(sent, "span", split_axis=0, concat_axis=0, tiled=True)
    pick = (pos[:, None] == jnp.arange(n_span * ROOM, dtype=jnp.int32)[None, :]).astype(bf16)
    embedded = jnp.dot(pick, got.reshape(-1, DE), preferred_element_type=f32).astype(bf16)

    def whole_gather(_):
        shifted = ids_m.reshape(-1) - span_index * vocab_rows
        inside = (shifted >= 0) & (shifted < vocab_rows)
        found = jnp.take(embed_table, jnp.clip(shifted, 0, vocab_rows - 1), axis=0)
        return lax.psum_scatter(
            jnp.where(inside[:, None], found, jnp.zeros_like(found)),
            "span",
            scatter_dimension=0,
            tiled=True,
        )

    embedded = lax.cond(over > 0, whole_gather, lambda e: e, embedded)

    kv_part = jnp.dot(
        span_states.reshape(-1, half_width), w_span_kv, preferred_element_type=f32
    ).astype(bf16)
    kv_part = kv_part.reshape(seq_count, local_tokens, 2 * DE)
    kv_both = lax.all_to_all(kv_part, "mp", split_axis=0, concat_axis=0, tiled=True)
    kv = jnp.sum(kv_both.astype(f32), axis=0).astype(bf16)

    def swap_heads(x):
        both = lax.all_to_all(x, "mp", split_axis=0, concat_axis=0, tiled=True)
        return jnp.transpose(both, (1, 0, 2)).reshape(local_tokens, dec_cols)

    q = swap_heads(queries)
    og = swap_heads(out_grad)
    w_q = lax.all_gather(w_query_enc, "mp", axis=1, tiled=True)
    w_o = lax.all_gather(w_out_enc, "mp", axis=0, tiled=True)
    w_d = lax.all_gather(w_dec_kv, "mp", axis=2, tiled=True).reshape(DE, 2 * dec_cols)

    kv = kv.reshape(spans, CH, 2, heads_enc, EHD)
    keys, values = kv[:, :, 0], kv[:, :, 1]
    enc_query = (
        jnp.dot(embedded, w_q, preferred_element_type=f32)
        .astype(bf16)
        .reshape(spans, NB * R, heads_enc, EHD)
    )
    scores = jnp.einsum("cqhd,ckhd->chqk", enc_query, keys, preferred_element_type=f32) / math.sqrt(
        EHD
    )
    enc_full = jax.nn.softmax(scores, axis=-1)
    attended = jnp.einsum(
        "chqk,ckhd->cqhd", enc_full.astype(bf16), values, preferred_element_type=f32
    ).astype(bf16)
    att_flat = attended.reshape(tokens, DE)
    encoded = (embedded.astype(f32) + jnp.dot(att_flat, w_o, preferred_element_type=f32)).astype(
        bf16
    )

    halves = jnp.transpose(att_flat.reshape(units, R, 2, enc_cols), (2, 0, 1, 3))
    all_units = lax.all_to_all(halves, "mp", split_axis=0, concat_axis=0, tiled=True).reshape(
        seq_count * units, R, enc_cols
    )
    dest = lax.dynamic_index_in_dim(assignment[0, :, :, 0], span_index, 0, keepdims=False)
    placing = (dest[None, :] == jnp.arange(n_span, dtype=jnp.int32)[:, None]).astype(bf16)
    slots = jnp.einsum("eu,urd->erd", placing, all_units, preferred_element_type=f32).astype(bf16)
    attended_out = lax.all_to_all(slots, "span", split_axis=0, concat_axis=0, tiled=True)
    attended_out = attended_out.reshape(1, 1, n_span, 1, R, enc_cols)

    dec_kv = (
        jnp.dot(encoded, w_d, preferred_element_type=f32)
        .astype(bf16)
        .reshape(spans, NB * R, 2, heads_dec, HD)
    )
    dec_keys, dec_values = dec_kv[:, :, 0], dec_kv[:, :, 1]
    dec_query = q.reshape(spans, CH, heads_dec, HD)
    dec_scores = jnp.einsum(
        "cqhd,ckhd->chqk", dec_query, dec_keys, preferred_element_type=f32
    ) / math.sqrt(HD)
    dec_full = jax.nn.softmax(dec_scores, axis=-1)
    dec_weights = dec_full.astype(bf16)
    cross = jnp.einsum(
        "chqk,ckhd->cqhd", dec_weights, dec_values, preferred_element_type=f32
    ).astype(bf16)
    cross_halves = jnp.transpose(cross.reshape(local_tokens, 2, dec_cols // 2), (1, 0, 2))
    cross_out = lax.all_to_all(cross_halves, "mp", split_axis=0, concat_axis=0, tiled=True)
    grad_cross = og.reshape(spans, CH, heads_dec, HD)
    grad_values = jnp.einsum(
        "chqk,cqhd->ckhd", dec_weights, grad_cross, preferred_element_type=f32
    ).astype(bf16)
    grad_probs = jnp.einsum("cqhd,ckhd->chqk", grad_cross, dec_values, preferred_element_type=f32)
    row_terms = jnp.einsum("cqhd,cqhd->chq", grad_cross, cross, preferred_element_type=f32)
    grad_scores = softmax_grad(dec_full, grad_probs, row_terms, math.sqrt(HD))
    grad_keys = jnp.einsum(
        "chqk,cqhd->ckhd", grad_scores, dec_query, preferred_element_type=f32
    ).astype(bf16)
    grad_kv = jnp.stack([grad_keys, grad_values], axis=2).reshape(tokens, 2 * dec_cols)
    grad_encoded = lax.dot_general(
        grad_kv, w_d, (((1,), (1,)), ((), ())), preferred_element_type=f32
    ).astype(bf16)

    grad_out_part = lax.dot_general(
        att_flat, grad_encoded, (((0,), (0,)), ((), ())), preferred_element_type=f32
    )
    grad_att = (
        lax.dot_general(grad_encoded, w_o, (((1,), (1,)), ((), ())), preferred_element_type=f32)
        .astype(bf16)
        .reshape(spans, NB * R, heads_enc, EHD)
    )
    enc_grad_probs = jnp.einsum("cqhd,ckhd->chqk", grad_att, values, preferred_element_type=f32)
    enc_rows = jnp.einsum("cqhd,cqhd->chq", grad_att, attended, preferred_element_type=f32)
    enc_grad_scores = softmax_grad(enc_full, enc_grad_probs, enc_rows, math.sqrt(EHD))
    grad_enc_query = (
        jnp.einsum("chqk,ckhd->cqhd", enc_grad_scores, keys, preferred_element_type=f32)
        .astype(bf16)
        .reshape(tokens, DE)
    )
    grad_query_part = lax.dot_general(
        embedded, grad_enc_query, (((0,), (0,)), ((), ())), preferred_element_type=f32
    )
    gq = lax.psum_scatter(grad_query_part, "mp", scatter_dimension=1, tiled=True)
    go = lax.psum_scatter(grad_out_part, "mp", scatter_dimension=0, tiled=True)
    grad_query_enc, grad_out_enc = (
        lax.psum_scatter(gq, ("span", "dp"), scatter_dimension=0, tiled=True),
        lax.psum_scatter(go, ("span", "dp"), scatter_dimension=1, tiled=True),
    )
    return (cross_out, attended_out, grad_query_enc, grad_out_enc)


def solution(mesh):
    return jax.shard_map(
        body,
        mesh=mesh,
        in_specs=(
            P("dp", "span", "mp"),
            P("dp", "span", "mp"),
            P("dp", "span", "mp"),
            P("dp", None, None, None),
            P("dp", None, None, None),
            P("span", None),
            P("mp", None),
            P(None, "mp"),
            P("mp", None),
            P(None, None, "mp"),
        ),
        out_specs=(
            P("dp", "span", "mp"),
            P("dp", "span", None, None, None, "mp"),
            P(("span", "dp"), "mp"),
            P("mp", ("span", "dp")),
        ),
        check_vma=False,
    )
```

```python
import math

import jax
import jax.numpy as jnp
import numpy as np
from jax import lax
from jax.experimental import pallas as pl
from jax.experimental.pallas import tpu as pltpu
from jax.sharding import PartitionSpec as P

HD = 128
DE = 896
EHD = 64
R = 128
CH = 64
NB = 2
ROOM = 48


def lists(ids_m, span_index, vocab_rows, n_span):
    tokens = ids_m.shape[1]
    t = jnp.arange(tokens, dtype=jnp.int32)
    same = ids_m[:, :, None] == ids_m[:, None, :]
    dup = jnp.any(same & (t[None, None, :] < t[None, :, None]), axis=2)
    uniq = jnp.logical_not(dup)
    src = ids_m // vocab_rows
    shards = jnp.arange(n_span, dtype=jnp.int32)
    counts = jnp.sum(
        (uniq[:, None, :] & (src[:, None, :] == shards[None, :, None])).astype(jnp.int32), axis=2
    )
    over = jnp.max(counts) > ROOM
    sel = uniq & (src == span_index)
    tri = (t[:, None] < t[None, :]).astype(jnp.bfloat16)
    rank = jnp.dot(sel.astype(jnp.bfloat16), tri, preferred_element_type=jnp.float32).astype(
        jnp.int32
    )
    room = jnp.arange(ROOM, dtype=jnp.int32)
    local = ids_m - span_index * vocab_rows
    rows = jnp.sum(
        jnp.where(
            (rank[:, None, :] == room[None, :, None]) & sel[:, None, :], local[:, None, :], 0
        ),
        axis=2,
    )
    own = lax.dynamic_index_in_dim(ids_m, span_index, 0, keepdims=False)
    own_src = own // vocab_rows
    own_same = own[:, None] == own[None, :]
    first = jnp.min(jnp.where(own_same, t[None, :], tokens), axis=1)
    own_uniq = first == t
    own_rank = jnp.sum(
        (
            own_uniq[None, :]
            & (own_src[:, None] == own_src[None, :])
            & (t[None, :] < first[:, None])
        ).astype(jnp.int32),
        axis=1,
    )
    return rows, own_src * ROOM + own_rank, over


F32 = jnp.float32
BF16 = jnp.bfloat16
PAIR = 2 * EHD
HEADS_ENC = DE // EHD
PAIRS = HEADS_ENC // 2
TOK = 512
SPANS = 2
DEC = 2048
HALF = DE // 2
PADDED = 1024
PIECE = 14
TILES = ((0, 256), (256, 256), (512, 256), (768, 128))


def dot(a, b):
    return jnp.dot(a, b, preferred_element_type=F32)


def dot_nt(a, b):
    return lax.dot_general(a, b, (((1,), (1,)), ((), ())), preferred_element_type=F32)


def dot_tn(a, b):
    return lax.dot_general(a, b, (((0,), (0,)), ((), ())), preferred_element_type=F32)


def piece_rows():
    rows = np.full((2, PADDED), -1, np.int32)
    n = 0
    for core in range(2):
        for first in range(4):
            for second in range(4):
                for low in range(2):
                    for r in range(16):
                        if r < PIECE:
                            rows[0, n] = (((first * 4 + second) * 2 + low) * 2 + core) * PIECE + r
                            rows[1, n] = (((second * 4 + first) * 2 + low) * 2 + core) * PIECE + r
                        n += 1
    return rows


def pair_blocks(kv_ref, c, j, low, high):
    rows = pl.ds(pl.multiple_of(c * CH, CH), CH)
    k = kv_ref[rows, pl.ds(pl.multiple_of(j * PAIR, PAIR), PAIR)]
    v = kv_ref[rows, pl.ds(pl.multiple_of(DE + j * PAIR, PAIR), PAIR)]
    return (
        jnp.concatenate([k * low, k * high], axis=0),
        jnp.concatenate([v * low, v * high], axis=0),
    )


def middle(
    rows_ref,
    emb_ref,
    kv_ref,
    q_ref,
    og_ref,
    wq_ref,
    wo_ref,
    wd_own_ref,
    wd_oth_ref,
    att_own_ref,
    att_oth_ref,
    cross_ref,
    gq_ref,
    go_ref,
    eq_ref,
    att_ref,
    probs_ref,
    enc_ref,
    dkv_ref,
    gkv_ref,
    sum_ref,
    pad_ref,
):
    half = lax.axis_index("mp")
    lane = lax.broadcasted_iota(jnp.int32, (1, PAIR), 1)
    is_low = lane < EHD
    low = is_low.astype(F32).astype(BF16)
    high = (lane >= EHD).astype(F32).astype(BF16)

    for at, size in TILES:
        eq_ref[:, at : at + size] = dot(emb_ref[...], wq_ref[:, at : at + size]).astype(BF16)

    def forward(i, _):
        c, j = i // PAIRS, i % PAIRS
        rows = pl.ds(pl.multiple_of(c * NB * R, NB * R), NB * R)
        cols = pl.ds(pl.multiple_of(j * PAIR, PAIR), PAIR)
        kbd, vbd = pair_blocks(kv_ref, c, j, low, high)
        s = dot_nt(eq_ref[rows, cols], kbd) * (1.0 / math.sqrt(EHD))
        top0 = jnp.max(jnp.where(is_low, s, -jnp.inf), axis=1, keepdims=True)
        top1 = jnp.max(jnp.where(is_low, -jnp.inf, s), axis=1, keepdims=True)
        p = jnp.exp(s - jnp.where(is_low, top0, top1))
        sum0 = jnp.sum(jnp.where(is_low, p, 0.0), axis=1, keepdims=True)
        sum1 = jnp.sum(jnp.where(is_low, 0.0, p), axis=1, keepdims=True)
        p = p / jnp.where(is_low, sum0, sum1)
        probs_ref[i] = p
        att_ref[rows, cols] = dot(p.astype(BF16), vbd).astype(BF16)
        return 0

    lax.fori_loop(0, SPANS * PAIRS, forward, 0)

    for at, size in TILES:
        enc_ref[:, at : at + size] = (
            emb_ref[:, at : at + size].astype(F32) + dot(att_ref[...], wo_ref[:, at : at + size])
        ).astype(BF16)

    feature = lax.broadcasted_iota(jnp.int32, (DE, HALF), 0)
    column = lax.broadcasted_iota(jnp.int32, (DE, HALF), 1)
    for ref, which in ((att_own_ref, half), (att_oth_ref, 1 - half)):
        pick = (feature == column + which * HALF).astype(F32).astype(BF16)
        ref[...] = dot(att_ref[...], pick).astype(BF16)

    def project(i, _):
        cols = pl.ds(pl.multiple_of(i * 256, 256), 256)
        dkv_ref[0, :, cols] = dot(enc_ref[...], wd_own_ref[:, cols]).astype(BF16)
        dkv_ref[1, :, cols] = dot(enc_ref[...], wd_oth_ref[:, cols]).astype(BF16)
        return 0

    lax.fori_loop(0, DEC // 256, project, 0)
    scale = 1.0 / math.sqrt(HD)

    def decode(i, _):
        c, h = i // 8, i % 8
        few = pl.ds(pl.multiple_of(c * CH, CH), CH)
        rows = pl.ds(pl.multiple_of(c * NB * R, NB * R), NB * R)
        kcols = pl.ds(pl.multiple_of(h * HD, HD), HD)
        vcols = pl.ds(pl.multiple_of(DEC // 2 + h * HD, HD), HD)
        for g in range(2):
            cols = pl.ds(pl.multiple_of(g * (DEC // 2) + h * HD, HD), HD)
            q, og = q_ref[few, cols], og_ref[few, cols]
            k, v = dkv_ref[g, rows, kcols], dkv_ref[g, rows, vcols]
            s = dot_nt(q, k) * scale
            p = jnp.exp(s - jnp.max(s, axis=1, keepdims=True))
            p = p / jnp.sum(p, axis=1, keepdims=True)
            pb = p.astype(BF16)
            cross = dot(pb, v).astype(BF16)
            cross_ref[g, few, kcols] = cross
            gkv_ref[g, rows, vcols] = dot_tn(pb, og).astype(BF16)
            row = jnp.sum(og.astype(F32) * cross.astype(F32), axis=1, keepdims=True)
            ds = (p * (dot_nt(og, v) - row) * scale).astype(BF16)
            gkv_ref[g, rows, kcols] = dot_tn(ds, q).astype(BF16)
        return 0

    lax.fori_loop(0, SPANS * 8, decode, 0)
    sum_ref[...] = jnp.zeros_like(sum_ref)

    def collect(i, _):
        cols = pl.ds(pl.multiple_of(i * 256, 256), 256)
        sum_ref[...] += dot_nt(gkv_ref[0, :, cols], wd_own_ref[:, cols]) + dot_nt(
            gkv_ref[1, :, cols], wd_oth_ref[:, cols]
        )
        return 0

    lax.fori_loop(0, DEC // 256, collect, 0)
    enc_ref[...] = sum_ref[...].astype(BF16)

    def pad(ref, order):
        for at in range(0, PADDED, 256):
            spread = (
                lax.broadcasted_iota(jnp.int32, (DE, 256), 0)
                == rows_ref[order : order + 1, at : at + 256]
            )
            pad_ref[:, at : at + 256] = dot(ref[...], spread.astype(F32).astype(BF16)).astype(BF16)

    def outer(out_ref, ref):
        def tile(i, _):
            cols = pl.ds(pl.multiple_of(i * 256, 256), 256)
            out_ref[cols, :] = dot_tn(pad_ref[:, cols], ref[...]).astype(BF16)
            return 0

        lax.fori_loop(0, PADDED // 256, tile, 0)

    pad(enc_ref, 1)
    outer(go_ref, att_ref)
    for at, size in TILES:
        eq_ref[:, at : at + size] = dot_nt(enc_ref[...], wo_ref[at : at + size, :]).astype(BF16)

    def backward(i, _):
        c, j = i // PAIRS, i % PAIRS
        rows = pl.ds(pl.multiple_of(c * NB * R, NB * R), NB * R)
        cols = pl.ds(pl.multiple_of(j * PAIR, PAIR), PAIR)
        kbd, vbd = pair_blocks(kv_ref, c, j, low, high)
        ga = eq_ref[rows, cols]
        prod = ga.astype(F32) * att_ref[rows, cols].astype(F32)
        row0 = jnp.sum(jnp.where(is_low, prod, 0.0), axis=1, keepdims=True)
        row1 = jnp.sum(jnp.where(is_low, 0.0, prod), axis=1, keepdims=True)
        diff = dot_nt(ga, vbd) - jnp.where(is_low, row0, row1)
        ds = (probs_ref[i] * diff * (1.0 / math.sqrt(EHD))).astype(BF16)
        eq_ref[rows, cols] = dot(ds, kbd).astype(BF16)
        return 0

    lax.fori_loop(0, SPANS * PAIRS, backward, 0)
    pad(emb_ref, 0)
    outer(gq_ref, eq_ref)


def run_middle(embedded, kv, q, og, w_q, w_o, wd_own, wd_oth):
    vmem = pl.BlockSpec(memory_space=pltpu.VMEM)
    return pl.pallas_call(
        middle,
        out_shape=(
            jax.ShapeDtypeStruct((TOK, HALF), BF16),
            jax.ShapeDtypeStruct((TOK, HALF), BF16),
            jax.ShapeDtypeStruct((2, SPANS * CH, DEC // 2), BF16),
            jax.ShapeDtypeStruct((PADDED, DE), BF16),
            jax.ShapeDtypeStruct((PADDED, DE), BF16),
        ),
        in_specs=[vmem] * 9,
        out_specs=(vmem,) * 5,
        scratch_shapes=[
            pltpu.VMEM((TOK, DE), BF16),
            pltpu.VMEM((TOK, DE), BF16),
            pltpu.VMEM((SPANS * PAIRS, NB * R, PAIR), F32),
            pltpu.VMEM((TOK, DE), BF16),
            pltpu.VMEM((2, TOK, DEC), BF16),
            pltpu.VMEM((2, TOK, DEC), BF16),
            pltpu.VMEM((TOK, DE), F32),
            pltpu.VMEM((TOK, PADDED), BF16),
        ],
        compiler_params=pltpu.CompilerParams(vmem_limit_bytes=60 * 2**20),
        cost_estimate=pl.CostEstimate(
            flops=15 * 10**9, bytes_accessed=20 * 2**20, transcendentals=10**6
        ),
    )(jnp.asarray(piece_rows()), embedded, kv, q, og, w_q, w_o, wd_own, wd_oth)


def ending(
    slot_ref,
    own_ref,
    oth_ref,
    cross_ref,
    gq_ref,
    go_ref,
    att_out,
    cross_out,
    rq_ref,
    ro_ref,
    all_ref,
    slots_ref,
    core_ref,
    acc1_ref,
    first1_ref,
    first2_ref,
    acc2_ref,
    second1_ref,
    second2_ref,
    acc3_ref,
    last_ref,
    swap_sems,
    slot_sems,
    core_sems,
    ring_sems,
    last_sems,
    local_sem,
):
    span, dp, half = lax.axis_index("span"), lax.axis_index("dp"), lax.axis_index("mp")
    z, y, x_low, core = span // 4, span % 4, dp // 2, dp % 2
    partner = {"span": span, "dp": dp, "mp": 1 - half}
    peer = {"span": span, "dp": x_low * 2 + 1 - core, "mp": half}

    def in_span(k):
        return {"span": lax.rem(span + k, 16), "dp": dp, "mp": half}

    def along(axis, by):
        if axis == 0:
            return {"span": lax.rem(z + by + 4, 4) * 4 + y, "dp": dp, "mp": half}
        return {"span": z * 4 + lax.rem(y + by + 4, 4), "dp": dp, "mp": half}

    others = [
        {"span": span, "dp": (1 - x_low) * 2 + core, "mp": half},
        partner,
        {"span": span, "dp": (1 - x_low) * 2 + core, "mp": 1 - half},
    ]
    barrier = pltpu.get_barrier_semaphore()
    friends = [in_span(k) for k in range(1, 16)] + [peer] + others
    for friend in friends:
        pl.semaphore_signal(barrier, inc=1, device_id=friend, device_id_type=pl.DeviceIdType.MESH)
    pl.semaphore_wait(barrier, len(friends))

    def send(src, dst, sems, device):
        copy = pltpu.make_async_remote_copy(
            src_ref=src,
            dst_ref=dst,
            send_sem=sems.at[0],
            recv_sem=sems.at[1],
            device_id=device,
            device_id_type=pl.DeviceIdType.MESH,
        )
        copy.start()
        return copy

    waiting = []
    swap = send(oth_ref, all_ref.at[half], swap_sems.at[0], partner)
    cores = [
        send(ref.at[1 - core], core_ref.at[k], core_sems.at[k], peer)
        for k, ref in enumerate((gq_ref, go_ref))
    ]
    waiting.append(send(cross_ref.at[1], cross_out.at[half], swap_sems.at[1], partner))
    mine = pltpu.make_async_copy(cross_ref.at[0], cross_out.at[half], local_sem.at[0])
    mine.start()
    all_ref[half] = own_ref[...]

    def add(*parts):
        total = parts[0].astype(F32)
        for part in parts[1:]:
            total = total + part.astype(F32)
        return total

    for k, ref in enumerate((gq_ref, go_ref)):
        cores[k].wait()
        for i in range(4):
            acc1_ref[k, i] = add(ref[core, i], core_ref[k, i]).astype(BF16)

    where = (z, y)

    def ring(level, acc, got1, width):
        cut = width // 2
        copies = []
        for k in range(2):
            axis = k if level == 0 else 1 - k
            p = where[axis]
            far = lax.rem(p + 2, 4)
            copies.append(
                (
                    send(acc.at[k, far, pl.ds(0, cut)], got1.at[k, 0], ring_sems.at[level, k, 0], along(axis, 1)),
                    send(acc.at[k, far, pl.ds(cut, cut)], got1.at[k, 1], ring_sems.at[level, k, 1], along(axis, -1)),
                )
            )
        return copies

    def ring_next(level, copies, acc, got1, got2, width):
        cut = width // 2
        nexts = []
        for k in range(2):
            axis = k if level == 0 else 1 - k
            p = where[axis]
            up, down = lax.rem(p + 1, 4), lax.rem(p + 3, 4)
            for copy in copies[k]:
                copy.wait()
            acc[k, up, pl.ds(0, cut)] = add(acc[k, up, pl.ds(0, cut)], got1[k, 0]).astype(BF16)
            acc[k, down, pl.ds(cut, cut)] = add(acc[k, down, pl.ds(cut, cut)], got1[k, 1]).astype(BF16)
            nexts.append(
                (
                    send(acc.at[k, up], got2.at[k, 0], ring_sems.at[level, k, 2], along(axis, 1)),
                    send(acc.at[k, down], got2.at[k, 1], ring_sems.at[level, k, 3], along(axis, -1)),
                )
            )
        return nexts

    copies = ring(0, acc1_ref, first1_ref, 4)

    swap.wait()
    for e in range(16):
        unit, there = slot_ref[0, e], slot_ref[1, e]
        slots_ref[e] = all_ref[unit // 4, unit % 4] * there.astype(F32).astype(BF16)
    for k in range(1, 16):
        to = lax.rem(span + k, 16)
        waiting.append(send(slots_ref.at[to], att_out.at[span], slot_sems.at[k], in_span(k)))
    stay = pltpu.make_async_copy(slots_ref.at[span], att_out.at[span], local_sem.at[1])
    stay.start()

    nexts = ring_next(0, copies, acc1_ref, first1_ref, first2_ref, 4)
    for k in range(2):
        for copy in nexts[k]:
            copy.wait()
        acc2_ref[k] = add(acc1_ref[k, where[k]], first2_ref[k, 0], first2_ref[k, 1]).astype(BF16)
    copies = ring(1, acc2_ref, second1_ref, 2)
    nexts = ring_next(1, copies, acc2_ref, second1_ref, second2_ref, 2)
    for k in range(2):
        for copy in nexts[k]:
            copy.wait()
        acc3_ref[k] = add(acc2_ref[k, where[1 - k]], second2_ref[k, 0], second2_ref[k, 1]).astype(BF16)

    lasts = []
    for n, other in enumerate(others):
        low = x_low if n == 1 else 1 - x_low
        lasts.append(send(acc3_ref.at[:, low], last_ref.at[n], last_sems.at[n], other))
    for copy in lasts:
        copy.wait()
    for k, ref in enumerate((rq_ref, ro_ref)):
        ref[...] = add(acc3_ref[k, x_low], last_ref[0, k], last_ref[1, k], last_ref[2, k])
    for copy in waiting:
        copy.wait()
    mine.wait()
    stay.wait()


def run_ending(slot, own, oth, cross, gq, go):
    vmem = pl.BlockSpec(memory_space=pltpu.VMEM)
    anywhere = pl.BlockSpec(memory_space=pl.ANY)
    dma = pltpu.SemaphoreType.DMA
    return pl.pallas_call(
        ending,
        out_shape=(
            jax.ShapeDtypeStruct((16, R, HALF), BF16),
            jax.ShapeDtypeStruct((2, SPANS * CH, DEC // 2), BF16),
            jax.ShapeDtypeStruct((16, DE), F32),
            jax.ShapeDtypeStruct((16, DE), F32),
        ),
        in_specs=[pl.BlockSpec(memory_space=pltpu.SMEM)] + [vmem] * 5,
        out_specs=(anywhere, anywhere, vmem, vmem),
        scratch_shapes=[
            pltpu.VMEM((2, 4, R, HALF), BF16),
            pltpu.VMEM((16, R, HALF), BF16),
            pltpu.VMEM((2, 4, 4, 2, 16, DE), BF16),
            pltpu.VMEM((2, 4, 4, 2, 16, DE), BF16),
            pltpu.VMEM((2, 2, 2, 2, 16, DE), BF16),
            pltpu.VMEM((2, 2, 4, 2, 16, DE), BF16),
            pltpu.VMEM((2, 4, 2, 16, DE), BF16),
            pltpu.VMEM((2, 2, 1, 16, DE), BF16),
            pltpu.VMEM((2, 2, 2, 16, DE), BF16),
            pltpu.VMEM((2, 2, 16, DE), BF16),
            pltpu.VMEM((3, 2, 16, DE), BF16),
            dma((2, 2)),
            dma((16, 2)),
            dma((2, 2)),
            dma((2, 2, 4, 2)),
            dma((3, 2)),
            dma((2,)),
        ],
        compiler_params=pltpu.CompilerParams(
            vmem_limit_bytes=48 * 2**20, collective_id=1, has_side_effects=True
        ),
        cost_estimate=pl.CostEstimate(
            flops=10**7, bytes_accessed=10 * 2**20, transcendentals=0
        ),
    )(slot, own.reshape(4, R, HALF), oth.reshape(4, R, HALF), cross, gq.reshape(2, 4, 4, 2, 16, DE), go.reshape(2, 4, 4, 2, 16, DE))


def body(
    span_states,
    queries,
    out_grad,
    neighbour_ids,
    assignment,
    embed_table,
    w_span_kv,
    w_query_enc,
    w_out_enc,
    w_dec_kv,
):
    f32 = jnp.float32
    bf16 = jnp.bfloat16
    n_span = lax.axis_size("span")
    span_index = lax.axis_index("span")
    half_index = lax.axis_index("mp")
    seq_count, local_tokens, half_width = span_states.shape
    spans = local_tokens // CH
    units = spans * NB
    dec_cols = 2 * queries.shape[2]
    vocab_rows = embed_table.shape[0]
    tokens = units * R

    ids_m = lax.dynamic_index_in_dim(
        neighbour_ids.reshape(seq_count, n_span, tokens), half_index, 0, keepdims=False
    )
    rows, pos, over = lists(ids_m, span_index, vocab_rows, n_span)
    over = lax.pmax(over.astype(jnp.int32), ("dp", "mp"))
    sent = jnp.take(embed_table, rows.reshape(-1), axis=0).reshape(n_span, ROOM, DE)
    got = lax.all_to_all(sent, "span", split_axis=0, concat_axis=0, tiled=True)
    pick = (pos[:, None] == jnp.arange(n_span * ROOM, dtype=jnp.int32)[None, :]).astype(bf16)
    embedded = jnp.dot(pick, got.reshape(-1, DE), preferred_element_type=f32).astype(bf16)

    def whole_gather(_):
        shifted = ids_m.reshape(-1) - span_index * vocab_rows
        inside = (shifted >= 0) & (shifted < vocab_rows)
        found = jnp.take(embed_table, jnp.clip(shifted, 0, vocab_rows - 1), axis=0)
        return lax.psum_scatter(
            jnp.where(inside[:, None], found, jnp.zeros_like(found)),
            "span",
            scatter_dimension=0,
            tiled=True,
        )

    embedded = lax.cond(over > 0, whole_gather, lambda e: e, embedded)

    kv_part = jnp.dot(
        span_states.reshape(-1, half_width), w_span_kv, preferred_element_type=f32
    ).astype(bf16)
    kv_part = kv_part.reshape(seq_count, local_tokens, 2 * DE)
    kv_both = lax.all_to_all(kv_part, "mp", split_axis=0, concat_axis=0, tiled=True)
    kv = jnp.sum(kv_both.astype(f32), axis=0).astype(bf16)

    def swap_heads(x):
        both = lax.all_to_all(x, "mp", split_axis=0, concat_axis=0, tiled=True)
        own = lax.dynamic_index_in_dim(both, half_index, 0, keepdims=False)
        oth = lax.dynamic_index_in_dim(both, 1 - half_index, 0, keepdims=False)
        return jnp.concatenate([own, oth], axis=1)

    q = swap_heads(queries)
    og = swap_heads(out_grad)

    def other_half(w, rows):
        part = lax.dynamic_slice_in_dim(w, span_index * rows, rows, 0)
        part = lax.ppermute(part, "mp", [(0, 1), (1, 0)])
        return lax.all_gather(part, "span", axis=0, tiled=True)

    wd_own = w_dec_kv.reshape(DE, dec_cols)
    wq_oth = other_half(w_query_enc, DE // n_span)
    wo_oth = other_half(w_out_enc, 32)[:HALF]
    wd_oth = other_half(wd_own, DE // n_span)
    first = half_index == 0
    w_q = jnp.where(
        first,
        jnp.concatenate([w_query_enc, wq_oth], axis=1),
        jnp.concatenate([wq_oth, w_query_enc], axis=1),
    )
    w_o = jnp.where(
        first,
        jnp.concatenate([w_out_enc, wo_oth], axis=0),
        jnp.concatenate([wo_oth, w_out_enc], axis=0),
    )
    own, oth, cross, gq, go = run_middle(embedded, kv, q, og, w_q, w_o, wd_own, wd_oth)

    dest = lax.dynamic_index_in_dim(assignment[0, :, :, 0], span_index, 0, keepdims=False)
    at = dest[None, :] == jnp.arange(n_span, dtype=jnp.int32)[:, None]
    numbers = jnp.arange(seq_count * units, dtype=jnp.int32)
    slot = jnp.stack(
        [jnp.sum(jnp.where(at, numbers[None, :], 0), axis=1), jnp.sum(at.astype(jnp.int32), axis=1)]
    )
    attended_out, cross_out, rq, ro = run_ending(slot, own, oth, cross, gq, go)
    grad_query_enc = lax.dynamic_slice_in_dim(rq[:PIECE], half_index * HALF, HALF, 1)
    grad_out_enc = lax.dynamic_slice_in_dim(ro[:PIECE], half_index * HALF, HALF, 1).T
    return (
        cross_out,
        attended_out.reshape(1, 1, n_span, 1, R, HALF),
        grad_query_enc,
        grad_out_enc,
    )


def solution(mesh):
    return jax.shard_map(
        body,
        mesh=mesh,
        in_specs=(
            P("dp", "span", "mp"),
            P("dp", "span", "mp"),
            P("dp", "span", "mp"),
            P("dp", None, None, None),
            P("dp", None, None, None),
            P("span", None),
            P("mp", None),
            P(None, "mp"),
            P("mp", None),
            P(None, None, "mp"),
        ),
        out_specs=(
            P("dp", "span", "mp"),
            P("dp", "span", None, None, None, "mp"),
            P(("span", "dp"), "mp"),
            P("mp", ("span", "dp")),
        ),
        check_vma=False,
    )
```

```python
import math

import jax
import jax.numpy as jnp
import numpy as np
from jax import lax
from jax.experimental import pallas as pl
from jax.experimental.pallas import tpu as pltpu
from jax.sharding import PartitionSpec as P

HD = 128
DE = 896
EHD = 64
R = 128
CH = 64
NB = 2
ROOM = 48


def lists(ids_m, span_index, vocab_rows, n_span):
    tokens = ids_m.shape[1]
    t = jnp.arange(tokens, dtype=jnp.int32)
    same = ids_m[:, :, None] == ids_m[:, None, :]
    dup = jnp.any(same & (t[None, None, :] < t[None, :, None]), axis=2)
    uniq = jnp.logical_not(dup)
    src = ids_m // vocab_rows
    shards = jnp.arange(n_span, dtype=jnp.int32)
    counts = jnp.sum(
        (uniq[:, None, :] & (src[:, None, :] == shards[None, :, None])).astype(jnp.int32), axis=2
    )
    over = jnp.max(counts) > ROOM
    sel = uniq & (src == span_index)
    tri = (t[:, None] < t[None, :]).astype(jnp.bfloat16)
    rank = jnp.dot(sel.astype(jnp.bfloat16), tri, preferred_element_type=jnp.float32).astype(
        jnp.int32
    )
    room = jnp.arange(ROOM, dtype=jnp.int32)
    local = ids_m - span_index * vocab_rows
    rows = jnp.sum(
        jnp.where(
            (rank[:, None, :] == room[None, :, None]) & sel[:, None, :], local[:, None, :], 0
        ),
        axis=2,
    )
    own = lax.dynamic_index_in_dim(ids_m, span_index, 0, keepdims=False)
    own_src = own // vocab_rows
    own_same = own[:, None] == own[None, :]
    first = jnp.min(jnp.where(own_same, t[None, :], tokens), axis=1)
    own_uniq = first == t
    own_rank = jnp.sum(
        (
            own_uniq[None, :]
            & (own_src[:, None] == own_src[None, :])
            & (t[None, :] < first[:, None])
        ).astype(jnp.int32),
        axis=1,
    )
    return rows, own_src * ROOM + own_rank, over


F32 = jnp.float32
BF16 = jnp.bfloat16
PAIR = 2 * EHD
HEADS_ENC = DE // EHD
PAIRS = HEADS_ENC // 2
TOK = 512
SPANS = 2
DEC = 2048
HALF = DE // 2
PADDED = 1024
PIECE = 14
TILES = ((0, 256), (256, 256), (512, 256), (768, 128))


def dot(a, b):
    return jnp.dot(a, b, preferred_element_type=F32)


def dot_nt(a, b):
    return lax.dot_general(a, b, (((1,), (1,)), ((), ())), preferred_element_type=F32)


def dot_tn(a, b):
    return lax.dot_general(a, b, (((0,), (0,)), ((), ())), preferred_element_type=F32)


def piece_rows():
    rows = np.full((2, PADDED), -1, np.int32)
    n = 0
    for core in range(2):
        for first in range(4):
            for second in range(4):
                for low in range(2):
                    for r in range(16):
                        if r < PIECE:
                            rows[0, n] = (((first * 4 + second) * 2 + low) * 2 + core) * PIECE + r
                            rows[1, n] = (((second * 4 + first) * 2 + low) * 2 + core) * PIECE + r
                        n += 1
    return rows


def pair_blocks(kv_ref, c, j, low, high):
    rows = slice(c * CH, (c + 1) * CH)
    k = kv_ref[rows, pl.ds(pl.multiple_of(j * PAIR, PAIR), PAIR)]
    v = kv_ref[rows, pl.ds(pl.multiple_of(DE + j * PAIR, PAIR), PAIR)]
    return (
        jnp.concatenate([k * low, k * high], axis=0),
        jnp.concatenate([v * low, v * high], axis=0),
    )


def mega(
    slot_ref,
    rows_ref,
    pos_ref,
    alt_ref,
    sent_ref,
    states_ref,
    wspan_ref,
    q_ref,
    og_ref,
    wq_own_ref,
    wo_own_ref,
    wd_ref,
    wqo_ref,
    att_out,
    cross_out,
    rq_ref,
    ro_ref,
    got_ref,
    emb_ref,
    kvp_ref,
    kvg_ref,
    kv_ref,
    qo_ref,
    ogo_ref,
    wb_ref,
    sb_ref,
    wq_ref,
    wo_ref,
    eq_ref,
    att_ref,
    probs_ref,
    enc_ref,
    dkv_ref,
    gkv_ref,
    sum_ref,
    pad_ref,
    own_ref,
    cross_ref,
    all_ref,
    slots_ref,
    g_ref,
    core_ref,
    acc1_ref,
    first1_ref,
    first2_ref,
    acc2_ref,
    second1_ref,
    second2_ref,
    acc3_ref,
    last_ref,
    emb_sems,
    swap_sems,
    weight_sems,
    slot_sems,
    sum_sems,
    local_sems,
):
    span, dp, half = lax.axis_index("span"), lax.axis_index("dp"), lax.axis_index("mp")
    z, y, x_low, core = span // 4, span % 4, dp // 2, dp % 2
    partner = {"span": span, "dp": dp, "mp": 1 - half}
    peer = {"span": span, "dp": x_low * 2 + 1 - core, "mp": half}
    where = (z, y)

    def in_span(k):
        return {"span": lax.rem(span + k, 16), "dp": dp, "mp": half}

    def along(axis, by):
        if axis == 0:
            return {"span": lax.rem(z + by + 4, 4) * 4 + y, "dp": dp, "mp": half}
        return {"span": z * 4 + lax.rem(y + by + 4, 4), "dp": dp, "mp": half}

    others = [
        {"span": span, "dp": (1 - x_low) * 2 + core, "mp": half},
        partner,
        {"span": span, "dp": (1 - x_low) * 2 + core, "mp": 1 - half},
    ]
    spans_in = [
        pltpu.make_async_copy(
            wspan_ref.at[pl.ds(i * 512, 512)],
            (dkv_ref, gkv_ref)[i // 2].at[i % 2, :, pl.ds(0, 2 * DE)],
            local_sems.at[i],
        )
        for i in range(4)
    ]
    alt_in = pltpu.make_async_copy(alt_ref, eq_ref, local_sems.at[4])
    for copy in spans_in:
        copy.start()
    alt_in.start()

    barrier = pltpu.get_barrier_semaphore()
    friends = [in_span(k) for k in range(1, 16)] + [peer] + others
    for friend in friends:
        pl.semaphore_signal(barrier, inc=1, device_id=friend, device_id_type=pl.DeviceIdType.MESH)
    pl.semaphore_wait(barrier, len(friends))

    def send(src, dst, sems, device):
        copy = pltpu.make_async_remote_copy(
            src_ref=src,
            dst_ref=dst,
            send_sem=sems.at[0],
            recv_sem=sems.at[1],
            device_id=device,
            device_id_type=pl.DeviceIdType.MESH,
        )
        copy.start()
        return copy

    def add(*parts):
        total = parts[0].astype(F32)
        for part in parts[1:]:
            total = total + part.astype(F32)
        return total

    embs = [
        send(sent_ref.at[lax.rem(span + k, 16)], got_ref.at[span], emb_sems.at[k], in_span(k))
        for k in range(1, 16)
    ]
    def mod(v):
        return lax.rem(v + 4, 4)

    def wide_at(r, group, piece, count):
        n = core * 2 + r
        return wb_ref.at[
            pl.ds(pl.multiple_of(n * 224, 224), 224),
            pl.ds(pl.multiple_of(group * 512 + piece * 128, 128), count * 128),
        ]

    def small_at(r, group, piece, count):
        n = core * 2 + r
        return sb_ref.at[pl.ds(group * 4 + piece, count), pl.ds(pl.multiple_of(n * 112, 112), 112)]

    def share(r, sem, device, wide, small):
        return [
            send(wide, wide, weight_sems.at[r, sem], device),
            send(small, small, weight_sems.at[r, sem + 1], device),
        ]

    ranks = ((z, y), (y, z))
    weights = []
    for r in range(2):
        n = core * 2 + r
        p, s = ranks[r]
        weights.append(
            [
                send(
                    wd_ref.at[
                        pl.ds(pl.multiple_of(n * 224, 224), 224),
                        pl.ds(pl.multiple_of(s * 512 + p * 128, 128), 128),
                    ],
                    wide_at(r, s, p, 1),
                    weight_sems.at[r, 0],
                    others[2],
                ),
                send(wqo_ref.at[pl.ds(r, 1)], small_at(r, s, p, 1), weight_sems.at[r, 1], others[2]),
            ]
        )
    got_ref[span] = sent_ref[span]

    for copy in spans_in:
        copy.wait()

    def project_span(i, _):
        cols = pl.ds(pl.multiple_of(i * 256, 256), 256)
        total = jnp.zeros((2 * SPANS * CH, 256), F32)
        for n in range(4):
            total += dot(states_ref[:, n * 512 : (n + 1) * 512], (dkv_ref, gkv_ref)[n // 2][n % 2, :, cols])
        total = total.astype(BF16)
        kvp_ref[0, :, cols] = total[: SPANS * CH]
        kvp_ref[1, :, cols] = total[SPANS * CH :]
        return 0

    lax.fori_loop(0, 2 * DE // 256, project_span, 0)
    kv_swap = send(kvp_ref.at[1 - half], kvg_ref, swap_sems.at[0], partner)
    q_swap = send(q_ref.at[1 - half], qo_ref, swap_sems.at[1], partner)
    og_swap = send(og_ref.at[1 - half], ogo_ref, swap_sems.at[2], partner)

    def settle(r):
        for copy in weights[r]:
            copy.wait()

    for r in range(2):
        settle(r)
        p, s = ranks[r]
        weights[r] = []
        for i, by in enumerate((1, -1)):
            weights[r] += share(r, 2 + 2 * i, along(r, by), wide_at(r, s, p, 1), small_at(r, s, p, 1))
    for r in range(2):
        settle(r)
        p, s = ranks[r]
        weights[r] = []
        for i, by in enumerate((1, -1)):
            f = mod(p - by)
            wide, small = wide_at(r, s, f, 1), small_at(r, s, f, 1)
            weights[r] += share(
                r,
                6 + 2 * i,
                along(r, by),
                wide.at[pl.ds(112 * i, 112)],
                small.at[:, pl.ds(48 * i, 48 + 16 * i)],
            )
    for r in range(2):
        settle(r)
        p, s = ranks[r]
        weights[r] = []
        for i, by in enumerate((1, -1)):
            weights[r] += share(r, 10 + 2 * i, along(1 - r, by), wide_at(r, s, 0, 4), small_at(r, s, 0, 4))

    for copy in embs:
        copy.wait()
    alt_in.wait()
    slot_of = lax.broadcasted_iota(jnp.int32, (1, 16 * ROOM), 1)
    pick = (pos_ref[...] == slot_of).astype(F32).astype(BF16)
    over = slot_ref[2, 0] > 0
    for lane_at, size in TILES:
        cols = slice(lane_at, lane_at + size)
        rows = jnp.concatenate([got_ref[i, :, cols] for i in range(16)], axis=0)
        emb_ref[:, cols] = jnp.where(over, eq_ref[:, cols].astype(F32), dot(pick, rows)).astype(BF16)

    for r in range(2):
        settle(r)
        p, s = ranks[r]
        weights[r] = []
        for i, by in enumerate((1, -1)):
            f = mod(s - by)
            weights[r] += share(r, 14 + 2 * i, along(1 - r, by), wide_at(r, f, 2 * i, 2), small_at(r, f, 2 * i, 2))
    for r in range(2):
        settle(r)
        n = core * 2 + r
        weights[r] = share(
            r,
            18,
            peer,
            wb_ref.at[pl.ds(pl.multiple_of(n * 224, 224), 224)],
            sb_ref.at[:, pl.ds(pl.multiple_of(n * 112, 112), 112)],
        )
    kv_swap.wait()
    kv_ref[...] = add(kvp_ref[half], kvg_ref[...]).astype(BF16)
    for r in range(2):
        settle(r)

    place = lax.broadcasted_iota(jnp.int32, (HALF, 256), 0)
    wide = lax.broadcasted_iota(jnp.int32, (512, 256), 0)
    wide = jnp.where(wide < 384, wide, jnp.where(wide >= 448, wide - 64, -DE))
    col = lax.broadcasted_iota(jnp.int32, (HALF, 256), 1)
    wide_col = lax.broadcasted_iota(jnp.int32, (512, 256), 1)
    for lane_at, size in TILES:
        mine = (place + half * HALF == col + lane_at).astype(F32).astype(BF16)[:, :size]
        his = (wide + (1 - half) * HALF == wide_col + lane_at).astype(F32).astype(BF16)[:, :size]
        for up in range(2):
            rows = slice(up * HALF, (up + 1) * HALF)
            other = jnp.concatenate([sb_ref[up * 4 + i] for i in range(4)], axis=1)
            wq_ref[rows, lane_at : lane_at + size] = (dot(wq_own_ref[rows, :], mine) + dot(other, his)).astype(BF16)
    wo_ref[pl.ds(pl.multiple_of(half * HALF, HALF), HALF), :] = wo_own_ref[...]
    for i in range(7):
        wo_ref[pl.ds(pl.multiple_of((1 - half) * HALF, HALF), HALF), i * 128 : (i + 1) * 128] = sb_ref[8 + i]

    lane = lax.broadcasted_iota(jnp.int32, (1, PAIR), 1)
    is_low = lane < EHD
    low = is_low.astype(F32).astype(BF16)
    high = (lane >= EHD).astype(F32).astype(BF16)

    for lane_at, size in TILES:
        cols = slice(lane_at, lane_at + size)
        eq_ref[:, cols] = dot(emb_ref[...], wq_ref[:, cols]).astype(BF16)

    def forward(j, _):
        cols = pl.ds(pl.multiple_of(j * PAIR, PAIR), PAIR)
        for c in range(SPANS):
            rows = slice(c * NB * R, (c + 1) * NB * R)
            kbd, vbd = pair_blocks(kv_ref, c, j, low, high)
            s = dot_nt(eq_ref[rows, cols], kbd) * (1.0 / math.sqrt(EHD))
            top0 = jnp.max(jnp.where(is_low, s, -jnp.inf), axis=1, keepdims=True)
            top1 = jnp.max(jnp.where(is_low, -jnp.inf, s), axis=1, keepdims=True)
            p = jnp.exp(s - jnp.where(is_low, top0, top1))
            sum0 = jnp.sum(jnp.where(is_low, p, 0.0), axis=1, keepdims=True)
            sum1 = jnp.sum(jnp.where(is_low, 0.0, p), axis=1, keepdims=True)
            p = p * jnp.where(is_low, 1.0 / sum0, 1.0 / sum1)
            probs_ref[c, j] = p
            att_ref[rows, cols] = dot(p.astype(BF16), vbd).astype(BF16)
        return 0

    lax.fori_loop(0, PAIRS, forward, 0)

    feature = lax.broadcasted_iota(jnp.int32, (DE, HALF), 0)
    column = lax.broadcasted_iota(jnp.int32, (DE, HALF), 1)

    def half_of(which):
        chosen = (feature == column + which * HALF).astype(F32).astype(BF16)
        return dot(att_ref[...], chosen).astype(BF16)

    own_ref[...] = half_of(1 - half).reshape(4, R, HALF)
    att_swap = send(own_ref, all_ref.at[half], swap_sems.at[3], partner)
    all_ref[half] = half_of(half).reshape(4, R, HALF)

    for lane_at, size in TILES:
        cols = slice(lane_at, lane_at + size)
        enc_ref[:, cols] = (emb_ref[:, cols].astype(F32) + dot(att_ref[...], wo_ref[:, cols])).astype(BF16)

    def project(i, _):
        cols = pl.ds(pl.multiple_of(i * 256, 256), 256)
        dkv_ref[0, :, cols] = dot(enc_ref[...], wd_ref[:, cols]).astype(BF16)
        dkv_ref[1, :, cols] = dot(enc_ref[...], wb_ref[:, cols]).astype(BF16)
        return 0

    lax.fori_loop(0, DEC // 256, project, 0)

    att_swap.wait()
    for e in range(16):
        unit, there = slot_ref[0, e], slot_ref[1, e]
        slots_ref[e] = all_ref[unit // 4, unit % 4] * there.astype(F32).astype(BF16)
    waiting = [
        send(slots_ref.at[lax.rem(span + k, 16)], att_out.at[span], slot_sems.at[k], in_span(k))
        for k in range(1, 16)
    ]
    stay = pltpu.make_async_copy(slots_ref.at[span], att_out.at[span], local_sems.at[0])
    stay.start()
    q_swap.wait()
    og_swap.wait()
    scale = 1.0 / math.sqrt(HD)

    def decode(h, _):
        kcols = pl.ds(pl.multiple_of(h * HD, HD), HD)
        vcols = pl.ds(pl.multiple_of(DEC // 2 + h * HD, HD), HD)
        for g in range(2):
            for c in range(SPANS):
                few = slice(c * CH, (c + 1) * CH)
                rows = slice(c * NB * R, (c + 1) * NB * R)
                q = q_ref[half, few, kcols] if g == 0 else qo_ref[few, kcols]
                og = og_ref[half, few, kcols] if g == 0 else ogo_ref[few, kcols]
                k, v = dkv_ref[g, rows, kcols], dkv_ref[g, rows, vcols]
                s = dot_nt(q, k) * scale
                p = jnp.exp(s - jnp.max(s, axis=1, keepdims=True))
                p = p * (1.0 / jnp.sum(p, axis=1, keepdims=True))
                pb = p.astype(BF16)
                cross = dot(pb, v).astype(BF16)
                cross_ref[g, few, kcols] = cross
                gkv_ref[g, rows, vcols] = dot_tn(pb, og).astype(BF16)
                row = jnp.sum(og.astype(F32) * cross.astype(F32), axis=1, keepdims=True)
                ds = (p * (dot_nt(og, v) - row) * scale).astype(BF16)
                gkv_ref[g, rows, kcols] = dot_tn(ds, q).astype(BF16)
        return 0

    lax.fori_loop(0, 8, decode, 0)
    waiting.append(send(cross_ref.at[1], cross_out.at[half], swap_sems.at[4], partner))
    mine = pltpu.make_async_copy(cross_ref.at[0], cross_out.at[half], local_sems.at[1])
    mine.start()
    sum_ref[...] = jnp.zeros_like(sum_ref)

    def collect(i, _):
        cols = pl.ds(pl.multiple_of(i * 256, 256), 256)
        sum_ref[...] += dot_nt(gkv_ref[0, :, cols], wd_ref[:, cols]) + dot_nt(
            gkv_ref[1, :, cols], wb_ref[:, cols]
        )
        return 0

    lax.fori_loop(0, DEC // 256, collect, 0)
    enc_ref[...] = sum_ref[...].astype(BF16)

    def steps(k):
        sems = sum_sems.at[k]
        copies = [send(g_ref.at[k, 1 - core], core_ref.at[k], sems.at[0], peer)]
        yield
        copies[0].wait()
        for i in range(4):
            acc1_ref[k, i] = add(g_ref[k, core, i], core_ref[k, i]).astype(BF16)
        levels = ((acc1_ref, first1_ref, first2_ref, acc2_ref, 2, 1), (acc2_ref, second1_ref, second2_ref, acc3_ref, 1, 5))
        for level, (acc, got1, got2, out, cut, sem) in enumerate(levels):
            axis = k if level == 0 else 1 - k
            p = where[axis]
            far, up, down = mod(p + 2), mod(p + 1), mod(p - 1)
            one, two = pl.ds(0, cut), pl.ds(cut, cut)
            copies = [
                send(acc.at[k, far, one], got1.at[k, 0], sems.at[sem], along(axis, 1)),
                send(acc.at[k, far, two], got1.at[k, 1], sems.at[sem + 1], along(axis, -1)),
            ]
            yield
            for copy in copies:
                copy.wait()
            acc[k, up, one] = add(acc[k, up, one], got1[k, 0]).astype(BF16)
            acc[k, down, two] = add(acc[k, down, two], got1[k, 1]).astype(BF16)
            copies = [
                send(acc.at[k, up], got2.at[k, 0], sems.at[sem + 2], along(axis, 1)),
                send(acc.at[k, down], got2.at[k, 1], sems.at[sem + 3], along(axis, -1)),
            ]
            yield
            for copy in copies:
                copy.wait()
            out[k] = add(acc[k, p], got2[k, 0], got2[k, 1]).astype(BF16)
        copies = []
        for n, other in enumerate(others):
            to_low = x_low if n == 1 else 1 - x_low
            copies.append(send(acc3_ref.at[k, to_low], last_ref.at[k, n], sems.at[9 + n], other))
        yield
        for copy in copies:
            copy.wait()
        (rq_ref, ro_ref)[k][...] = add(acc3_ref[k, x_low], last_ref[k, 0], last_ref[k, 1], last_ref[k, 2])
        yield

    def pad(ref, order):
        for lane_at in range(0, PADDED, 256):
            spread = (
                lax.broadcasted_iota(jnp.int32, (DE, 256), 0)
                == rows_ref[order : order + 1, lane_at : lane_at + 256]
            )
            pad_ref[:, lane_at : lane_at + 256] = dot(ref[...], spread.astype(F32).astype(BF16)).astype(BF16)

    def outer(k, ref):
        def tile(i, _):
            cols = pl.ds(pl.multiple_of(i * 256, 256), 256)
            g_ref[k, i // 2, pl.ds((i % 2) * 2, 2)] = (
                dot_tn(pad_ref[:, cols], ref[...]).astype(BF16).reshape(2, 4, 2, 16, DE)
            )
            return 0

        lax.fori_loop(0, PADDED // 256, tile, 0)

    pad(enc_ref, 1)
    outer(1, att_ref)
    out_sum = steps(1)
    next(out_sum)
    for lane_at, size in TILES:
        cols = slice(lane_at, lane_at + size)
        eq_ref[:, cols] = dot_nt(enc_ref[...], wo_ref[cols, :]).astype(BF16)
    next(out_sum)

    def backward(j, _):
        cols = pl.ds(pl.multiple_of(j * PAIR, PAIR), PAIR)
        for c in range(SPANS):
            rows = slice(c * NB * R, (c + 1) * NB * R)
            kbd, vbd = pair_blocks(kv_ref, c, j, low, high)
            ga = eq_ref[rows, cols]
            prod = ga.astype(F32) * att_ref[rows, cols].astype(F32)
            row0 = jnp.sum(jnp.where(is_low, prod, 0.0), axis=1, keepdims=True)
            row1 = jnp.sum(jnp.where(is_low, 0.0, prod), axis=1, keepdims=True)
            diff = dot_nt(ga, vbd) - jnp.where(is_low, row0, row1)
            ds = (probs_ref[c, j] * diff * (1.0 / math.sqrt(EHD))).astype(BF16)
            eq_ref[rows, cols] = dot(ds, kbd).astype(BF16)
        return 0

    lax.fori_loop(0, PAIRS, backward, 0)
    next(out_sum)
    pad(emb_ref, 0)
    next(out_sum)
    outer(0, eq_ref)
    query_sum = steps(0)
    for _ in range(7):
        next(query_sum)
        next(out_sum, None)
    for copy in waiting:
        copy.wait()
    mine.wait()
    stay.wait()


def run(slot, pos, alt, sent, states, w_span, q, og, w_q, w_o, w_d, wqo):
    vmem = pl.BlockSpec(memory_space=pltpu.VMEM)
    anywhere = pl.BlockSpec(memory_space=pl.ANY)
    dma = pltpu.SemaphoreType.DMA
    return pl.pallas_call(
        mega,
        out_shape=(
            jax.ShapeDtypeStruct((16, R, HALF), BF16),
            jax.ShapeDtypeStruct((2, SPANS * CH, DEC // 2), BF16),
            jax.ShapeDtypeStruct((16, DE), F32),
            jax.ShapeDtypeStruct((16, DE), F32),
        ),
        in_specs=[pl.BlockSpec(memory_space=pltpu.SMEM), vmem, vmem, anywhere, vmem, vmem, anywhere]
        + [vmem] * 6,
        out_specs=(anywhere, anywhere, vmem, vmem),
        scratch_shapes=[
            pltpu.VMEM((16, ROOM, DE), BF16),
            pltpu.VMEM((TOK, DE), BF16),
            pltpu.VMEM((2, SPANS * CH, 2 * DE), BF16),
            pltpu.VMEM((SPANS * CH, 2 * DE), BF16),
            pltpu.VMEM((SPANS * CH, 2 * DE), BF16),
            pltpu.VMEM((SPANS * CH, DEC // 2), BF16),
            pltpu.VMEM((SPANS * CH, DEC // 2), BF16),
            pltpu.VMEM((DE, DEC), BF16),
            pltpu.VMEM((16, HALF, 128), BF16),
            pltpu.VMEM((DE, DE), BF16),
            pltpu.VMEM((DE, DE), BF16),
            pltpu.VMEM((TOK, DE), BF16),
            pltpu.VMEM((TOK, DE), BF16),
            pltpu.VMEM((SPANS, PAIRS, NB * R, PAIR), F32),
            pltpu.VMEM((TOK, DE), BF16),
            pltpu.VMEM((2, TOK, DEC), BF16),
            pltpu.VMEM((2, TOK, DEC), BF16),
            pltpu.VMEM((TOK, DE), F32),
            pltpu.VMEM((TOK, PADDED), BF16),
            pltpu.VMEM((4, R, HALF), BF16),
            pltpu.VMEM((2, SPANS * CH, DEC // 2), BF16),
            pltpu.VMEM((2, 4, R, HALF), BF16),
            pltpu.VMEM((16, R, HALF), BF16),
            pltpu.VMEM((2, 2, 4, 4, 2, 16, DE), BF16),
            pltpu.VMEM((2, 4, 4, 2, 16, DE), BF16),
            pltpu.VMEM((2, 4, 4, 2, 16, DE), BF16),
            pltpu.VMEM((2, 2, 2, 2, 16, DE), BF16),
            pltpu.VMEM((2, 2, 4, 2, 16, DE), BF16),
            pltpu.VMEM((2, 4, 2, 16, DE), BF16),
            pltpu.VMEM((2, 2, 1, 16, DE), BF16),
            pltpu.VMEM((2, 2, 2, 16, DE), BF16),
            pltpu.VMEM((2, 2, 16, DE), BF16),
            pltpu.VMEM((2, 3, 16, DE), BF16),
            dma((16, 2)),
            dma((5, 2)),
            dma((2, 20, 2)),
            dma((16, 2)),
            dma((2, 12, 2)),
            dma((5,)),
        ],
        compiler_params=pltpu.CompilerParams(
            vmem_limit_bytes=63 * 2**20, collective_id=1, has_side_effects=True
        ),
        cost_estimate=pl.CostEstimate(
            flops=16 * 10**9, bytes_accessed=30 * 2**20, transcendentals=10**6
        ),
    )(slot, jnp.asarray(piece_rows()), pos, alt, sent, states, w_span, q, og, w_q, w_o, w_d, wqo)


def body(
    span_states,
    queries,
    out_grad,
    neighbour_ids,
    assignment,
    embed_table,
    w_span_kv,
    w_query_enc,
    w_out_enc,
    w_dec_kv,
):
    bf16 = jnp.bfloat16
    n_span = lax.axis_size("span")
    span_index = lax.axis_index("span")
    half_index = lax.axis_index("mp")
    seq_count, local_tokens, half_width = span_states.shape
    spans = local_tokens // CH
    units = spans * NB
    dec_cols = 2 * queries.shape[2]
    vocab_rows = embed_table.shape[0]
    tokens = units * R

    ids_m = lax.dynamic_index_in_dim(
        neighbour_ids.reshape(seq_count, n_span, tokens), half_index, 0, keepdims=False
    )
    rows, pos, over = lists(ids_m, span_index, vocab_rows, n_span)
    sent = jnp.take(embed_table, rows.reshape(-1), axis=0).reshape(n_span, ROOM, DE)

    def whole_gather():
        shifted = ids_m.reshape(-1) - span_index * vocab_rows
        inside = (shifted >= 0) & (shifted < vocab_rows)
        found = jnp.take(embed_table, jnp.clip(shifted, 0, vocab_rows - 1), axis=0)
        found = jnp.where(inside[:, None], found, jnp.zeros_like(found))
        found = lax.all_to_all(
            found.reshape(n_span, tokens, DE), "span", split_axis=0, concat_axis=0, tiled=True
        )
        return jnp.sum(found.astype(F32), axis=0).astype(bf16)

    alt = lax.cond(over, whole_gather, lambda: jnp.zeros((tokens, DE), bf16))

    core = lax.axis_index("dp") % 2
    wqo = []
    for r in range(2):
        piece = (span_index % 4) * 4 + span_index // 4 if r == 0 else span_index
        start = (core * 2 + r) * 112
        from_q = lax.dynamic_slice(
            w_query_enc,
            ((piece // 4) * HALF + start, jnp.minimum((piece % 4) * 128, HALF - 128)),
            (112, 128),
        )
        from_o = lax.dynamic_slice(w_out_enc, (start, (piece - 8) * 128), (112, 128))
        wqo.append(jnp.where(piece < 8, from_q, from_o))
    wqo = jnp.stack(wqo)

    dest = lax.dynamic_index_in_dim(assignment[0, :, :, 0], span_index, 0, keepdims=False)
    at = dest[None, :] == jnp.arange(n_span, dtype=jnp.int32)[:, None]
    numbers = jnp.arange(seq_count * units, dtype=jnp.int32)
    slot = jnp.stack(
        [
            jnp.sum(jnp.where(at, numbers[None, :], 0), axis=1),
            jnp.sum(at.astype(jnp.int32), axis=1),
            jnp.full((n_span,), over.astype(jnp.int32)),
        ]
    )
    attended_out, cross_out, rq, ro = run(
        slot,
        pos[:, None],
        alt,
        sent,
        span_states.reshape(-1, half_width),
        w_span_kv,
        queries,
        out_grad,
        w_query_enc,
        w_out_enc,
        w_dec_kv.reshape(DE, dec_cols),
        wqo,
    )
    grad_query_enc = lax.dynamic_slice_in_dim(rq[:PIECE], half_index * HALF, HALF, 1)
    grad_out_enc = lax.dynamic_slice_in_dim(ro[:PIECE], half_index * HALF, HALF, 1).T
    return (
        cross_out,
        attended_out.reshape(1, 1, n_span, 1, R, HALF),
        grad_query_enc,
        grad_out_enc,
    )


def solution(mesh):
    return jax.shard_map(
        body,
        mesh=mesh,
        in_specs=(
            P("dp", "span", "mp"),
            P("dp", "span", "mp"),
            P("dp", "span", "mp"),
            P("dp", None, None, None),
            P("dp", None, None, None),
            P("span", None),
            P("mp", None),
            P(None, "mp"),
            P("mp", None),
            P(None, None, "mp"),
        ),
        out_specs=(
            P("dp", "span", "mp"),
            P("dp", "span", None, None, None, "mp"),
            P(("span", "dp"), "mp"),
            P("mp", ("span", "dp")),
        ),
        check_vma=False,
    )
```

```python
import math

import jax
import jax.numpy as jnp
import numpy as np
from jax import lax
from jax.experimental import pallas as pl
from jax.experimental.pallas import tpu as pltpu
from jax.sharding import PartitionSpec as P

HD = 128
DE = 896
EHD = 64
R = 128
CH = 64
NB = 2
ROOM = 48


def lists(ids_m, span_index, vocab_rows, n_span):
    tokens = ids_m.shape[1]
    t = jnp.arange(tokens, dtype=jnp.int32)
    same = ids_m[:, :, None] == ids_m[:, None, :]
    dup = jnp.any(same & (t[None, None, :] < t[None, :, None]), axis=2)
    uniq = jnp.logical_not(dup)
    src = ids_m // vocab_rows
    shards = jnp.arange(n_span, dtype=jnp.int32)
    counts = jnp.sum(
        (uniq[:, None, :] & (src[:, None, :] == shards[None, :, None])).astype(jnp.int32), axis=2
    )
    over = jnp.max(counts) > ROOM
    sel = uniq & (src == span_index)
    tri = (t[:, None] < t[None, :]).astype(jnp.bfloat16)
    rank = jnp.dot(sel.astype(jnp.bfloat16), tri, preferred_element_type=jnp.float32).astype(
        jnp.int32
    )
    room = jnp.arange(ROOM, dtype=jnp.int32)
    local = ids_m - span_index * vocab_rows
    rows = jnp.sum(
        jnp.where(
            (rank[:, None, :] == room[None, :, None]) & sel[:, None, :], local[:, None, :], 0
        ),
        axis=2,
    )
    own = lax.dynamic_index_in_dim(ids_m, span_index, 0, keepdims=False)
    own_src = own // vocab_rows
    own_same = own[:, None] == own[None, :]
    first = jnp.min(jnp.where(own_same, t[None, :], tokens), axis=1)
    own_uniq = first == t
    own_rank = jnp.sum(
        (
            own_uniq[None, :]
            & (own_src[:, None] == own_src[None, :])
            & (t[None, :] < first[:, None])
        ).astype(jnp.int32),
        axis=1,
    )
    return rows, own_src * ROOM + own_rank, over


F32 = jnp.float32
BF16 = jnp.bfloat16
PAIR = 2 * EHD
HEADS_ENC = DE // EHD
PAIRS = HEADS_ENC // 2
TOK = 512
SPANS = 2
DEC = 2048
HALF = DE // 2
PADDED = 1024
PIECE = 14
TILES = ((0, 256), (256, 256), (512, 256), (768, 128))


def dot(a, b):
    return jnp.dot(a, b, preferred_element_type=F32)


def dot_nt(a, b):
    return lax.dot_general(a, b, (((1,), (1,)), ((), ())), preferred_element_type=F32)


def dot_tn(a, b):
    return lax.dot_general(a, b, (((0,), (0,)), ((), ())), preferred_element_type=F32)


def piece_rows():
    rows = np.full((2, PADDED), -1, np.int32)
    n = 0
    for core in range(2):
        for first in range(4):
            for second in range(4):
                for low in range(2):
                    for r in range(16):
                        if r < PIECE:
                            rows[0, n] = (((first * 4 + second) * 2 + low) * 2 + core) * PIECE + r
                            rows[1, n] = (((second * 4 + first) * 2 + low) * 2 + core) * PIECE + r
                        n += 1
    return rows


def pair_blocks(kv_ref, c, j, low, high):
    rows = slice(c * CH, (c + 1) * CH)
    k = kv_ref[rows, pl.ds(pl.multiple_of(j * PAIR, PAIR), PAIR)]
    v = kv_ref[rows, pl.ds(pl.multiple_of(DE + j * PAIR, PAIR), PAIR)]
    return (
        jnp.concatenate([k * low, k * high], axis=0),
        jnp.concatenate([v * low, v * high], axis=0),
    )


def mega(
    slot_ref,
    rows_ref,
    pos_ref,
    alt_ref,
    list_ref,
    table_ref,
    states_ref,
    wspan_ref,
    q_ref,
    og_ref,
    wq_own_ref,
    wo_own_ref,
    wd_ref,
    wqo_ref,
    att_out,
    cross_out,
    rq_ref,
    ro_ref,
    picked_ref,
    sent_ref,
    got_ref,
    emb_ref,
    kvp_ref,
    kvg_ref,
    kv_ref,
    qo_ref,
    ogo_ref,
    wb_ref,
    sb_ref,
    wq_ref,
    wo_ref,
    eq_ref,
    att_ref,
    probs_ref,
    enc_ref,
    dkv_ref,
    gkv_ref,
    sum_ref,
    pad_ref,
    pad_emb_ref,
    cross_ref,
    all_ref,
    slots_ref,
    g_ref,
    core_ref,
    acc1_ref,
    first1_ref,
    first2_ref,
    acc2_ref,
    second_ref,
    acc3_ref,
    last_ref,
    emb_sems,
    swap_sems,
    weight_sems,
    slot_sems,
    sum_sems,
    local_sems,
):
    span, dp, half = lax.axis_index("span"), lax.axis_index("dp"), lax.axis_index("mp")
    z, y, x_low, core = span // 4, span % 4, dp // 2, dp % 2
    partner = {"span": span, "dp": dp, "mp": 1 - half}
    peer = {"span": span, "dp": x_low * 2 + 1 - core, "mp": half}
    where = (z, y)

    offsets = ((0, 1), (1, 0), (0, 3), (3, 0), (2, 1), (1, 2), (2, 3), (3, 2), (1, 1), (3, 3), (1, 3), (3, 1), (2, 0), (0, 2), (2, 2))

    def span_at(k):
        return lax.rem(z + offsets[k][0], 4) * 4 + lax.rem(y + offsets[k][1], 4)

    def in_span(k):
        return {"span": span_at(k), "dp": dp, "mp": half}

    def along(axis, by):
        if axis == 0:
            return {"span": lax.rem(z + by + 4, 4) * 4 + y, "dp": dp, "mp": half}
        return {"span": z * 4 + lax.rem(y + by + 4, 4), "dp": dp, "mp": half}

    others = [
        {"span": span, "dp": (1 - x_low) * 2 + core, "mp": half},
        partner,
        {"span": span, "dp": (1 - x_low) * 2 + core, "mp": 1 - half},
    ]
    def area(i):
        return (dkv_ref, gkv_ref)[i // 4].at[(i // 2) % 2, :, pl.ds((i % 2) * 1024, DE)]

    vocab = table_ref.shape[0]
    sizes = [min(512, vocab - at) for at in range(0, vocab, 512)]
    table_in = [
        pltpu.make_async_copy(
            table_ref.at[pl.ds(i * 512, size)], area(i).at[pl.ds(0, size)], local_sems.at[5 + i]
        )
        for i, size in enumerate(sizes)
    ]
    spans_in = [
        pltpu.make_async_copy(
            wspan_ref.at[pl.ds(i * 512, 512)],
            (dkv_ref, gkv_ref)[i // 2].at[i % 2, :, pl.ds(0, 2 * DE)],
            local_sems.at[i],
        )
        for i in range(4)
    ]
    alt_in = pltpu.make_async_copy(alt_ref, eq_ref, local_sems.at[4])
    for copy in table_in:
        copy.start()
    alt_in.start()

    barrier = pltpu.get_barrier_semaphore()
    friends = [in_span(k) for k in range(15)] + [peer] + others
    for friend in friends:
        pl.semaphore_signal(barrier, inc=1, device_id=friend, device_id_type=pl.DeviceIdType.MESH)
    pl.semaphore_wait(barrier, len(friends))

    def send(src, dst, sems, device):
        copy = pltpu.make_async_remote_copy(
            src_ref=src,
            dst_ref=dst,
            send_sem=sems.at[0],
            recv_sem=sems.at[1],
            device_id=device,
            device_id_type=pl.DeviceIdType.MESH,
        )
        copy.start()
        return copy

    def add(*parts):
        total = parts[0].astype(F32)
        for part in parts[1:]:
            total = total + part.astype(F32)
        return total

    def mod(v):
        return lax.rem(v + 4, 4)

    ranks = ((z, y), (y, z))

    def at(kind, r, group, piece, count):
        n = core * 2 + r
        if kind:
            return wb_ref.at[
                pl.ds(pl.multiple_of(n * 224, 224), 224),
                pl.ds(pl.multiple_of(group * 512 + piece * 128, 128), count * 128),
            ]
        return sb_ref.at[pl.ds(group * 4 + piece, count), pl.ds(pl.multiple_of(n * 112, 112), 112)]

    def weight_steps(kind):
        sems = weight_sems.at[kind]
        copies = []
        for r in range(2):
            s = ranks[r][1]
            n = core * 2 + r
            if kind:
                src = wd_ref.at[
                    pl.ds(pl.multiple_of(n * 224, 224), 224), pl.ds(pl.multiple_of(s * 512, 512), 512)
                ]
            else:
                src = wqo_ref.at[r]
            copies.append([send(src, at(kind, r, s, 0, 4), sems.at[r, 0], others[2])])
        yield
        for r in range(2):
            s = ranks[r][1]
            for copy in copies[r]:
                copy.wait()
            whole = at(kind, r, s, 0, 4)
            copies[r] = [
                send(whole, whole, sems.at[r, 1 + i], along(1 - r, by)) for i, by in enumerate((1, -1))
            ]
        yield
        for r in range(2):
            s = ranks[r][1]
            for copy in copies[r]:
                copy.wait()
            copies[r] = []
            for i, by in enumerate((1, -1)):
                part = at(kind, r, mod(s - by), 2 * i, 2)
                copies[r].append(send(part, part, sems.at[r, 3 + i], along(1 - r, by)))
        yield
        for r in range(2):
            for copy in copies[r]:
                copy.wait()
            n = core * 2 + r
            if kind:
                mine = wb_ref.at[pl.ds(pl.multiple_of(n * 224, 224), 224)]
            else:
                mine = sb_ref.at[:, pl.ds(pl.multiple_of(n * 112, 112), 112)]
            copies[r] = [send(mine, mine, sems.at[r, 5], peer)]
        yield
        for r in range(2):
            for copy in copies[r]:
                copy.wait()
        yield

    small_steps, wide_steps = weight_steps(0), weight_steps(1)
    next(small_steps)
    next(wide_steps)

    rank = lax.broadcasted_iota(jnp.int32, (1, 512), 1)
    for i, size in enumerate(sizes):
        table_in[i].wait()
        chosen = (list_ref[...] == rank + i * 512).astype(F32).astype(BF16)
        part = dot(chosen[:, :size], area(i)[:size, :])
        if i == 0:
            sum_ref[...], picked_ref[...] = part[:TOK], part[TOK:]
        else:
            sum_ref[...] += part[:TOK]
            picked_ref[...] += part[TOK:]
        if i == 4:
            next(small_steps)
    picked = jnp.concatenate([sum_ref[...], picked_ref[...]], axis=0)
    sent_ref[...] = picked.astype(BF16).reshape(16, ROOM, DE)
    for copy in spans_in:
        copy.start()
    embs = [
        send(sent_ref.at[span_at(k)], got_ref.at[span], emb_sems.at[k], in_span(k))
        for k in range(15)
    ]
    got_ref[span] = sent_ref[span]
    next(small_steps)
    next(wide_steps)

    for copy in spans_in:
        copy.wait()

    def project_span(i, _):
        cols = pl.ds(pl.multiple_of(i * 256, 256), 256)
        total = jnp.zeros((2 * SPANS * CH, 256), F32)
        for n in range(4):
            total += dot(states_ref[:, n * 512 : (n + 1) * 512], (dkv_ref, gkv_ref)[n // 2][n % 2, :, cols])
        total = total.astype(BF16)
        kvp_ref[0, :, cols] = total[: SPANS * CH]
        kvp_ref[1, :, cols] = total[SPANS * CH :]
        return 0

    lax.fori_loop(0, 2 * DE // 256, project_span, 0)
    kv_swap = send(kvp_ref.at[1 - half], kvg_ref, swap_sems.at[0], partner)
    q_swap = send(q_ref.at[1 - half], qo_ref, swap_sems.at[1], partner)
    og_swap = send(og_ref.at[1 - half], ogo_ref, swap_sems.at[2], partner)

    next(small_steps)
    next(small_steps)

    place = lax.broadcasted_iota(jnp.int32, (HALF, 256), 0)
    wide = lax.broadcasted_iota(jnp.int32, (512, 256), 0)
    wide = jnp.where(wide < 384, wide, jnp.where(wide >= 448, wide - 64, -DE))
    col = lax.broadcasted_iota(jnp.int32, (HALF, 256), 1)
    wide_col = lax.broadcasted_iota(jnp.int32, (512, 256), 1)
    for lane_at, size in TILES:
        mine = (place + half * HALF == col + lane_at).astype(F32).astype(BF16)[:, :size]
        his = (wide + (1 - half) * HALF == wide_col + lane_at).astype(F32).astype(BF16)[:, :size]
        for up in range(2):
            rows = slice(up * HALF, (up + 1) * HALF)
            other = jnp.concatenate([sb_ref[up * 4 + i] for i in range(4)], axis=1)
            wq_ref[rows, lane_at : lane_at + size] = (dot(wq_own_ref[rows, :], mine) + dot(other, his)).astype(BF16)
    wo_ref[pl.ds(pl.multiple_of(half * HALF, HALF), HALF), :] = wo_own_ref[...]
    for i in range(7):
        wo_ref[pl.ds(pl.multiple_of((1 - half) * HALF, HALF), HALF), i * 128 : (i + 1) * 128] = sb_ref[8 + i if i < 4 else 9 + i]

    for copy in embs:
        copy.wait()
    alt_in.wait()
    slot_of = lax.broadcasted_iota(jnp.int32, (1, 16 * ROOM), 1)
    pick = (pos_ref[...] == slot_of).astype(F32).astype(BF16)
    over = slot_ref[2, 0] > 0
    for lane_at, size in TILES:
        cols = slice(lane_at, lane_at + size)
        rows = jnp.concatenate([got_ref[i, :, cols] for i in range(16)], axis=0)
        emb_ref[:, cols] = jnp.where(over, eq_ref[:, cols].astype(F32), dot(pick, rows)).astype(BF16)

    next(wide_steps)
    lane = lax.broadcasted_iota(jnp.int32, (1, PAIR), 1)
    is_low = lane < EHD
    low = is_low.astype(F32).astype(BF16)
    high = (lane >= EHD).astype(F32).astype(BF16)

    def pad(to_ref, ref, order):
        for lane_at in range(0, PADDED, 256):
            spread = (
                lax.broadcasted_iota(jnp.int32, (DE, 256), 0)
                == rows_ref[order : order + 1, lane_at : lane_at + 256]
            )
            to_ref[:, lane_at : lane_at + 256] = dot(ref[...], spread.astype(F32).astype(BF16)).astype(BF16)

    for lane_at, size in TILES:
        cols = slice(lane_at, lane_at + size)
        eq_ref[:, cols] = dot(emb_ref[...], wq_ref[:, cols]).astype(BF16)

    def forward(j, _):
        cols = pl.ds(pl.multiple_of(j * PAIR, PAIR), PAIR)
        for c in range(SPANS):
            rows = slice(c * NB * R, (c + 1) * NB * R)
            kbd, vbd = pair_blocks(kv_ref, c, j, low, high)
            s = dot_nt(eq_ref[rows, cols], kbd) * (1.0 / math.sqrt(EHD))
            top0 = jnp.max(jnp.where(is_low, s, -jnp.inf), axis=1, keepdims=True)
            top1 = jnp.max(jnp.where(is_low, -jnp.inf, s), axis=1, keepdims=True)
            p = jnp.exp(s - jnp.where(is_low, top0, top1))
            sum0 = jnp.sum(jnp.where(is_low, p, 0.0), axis=1, keepdims=True)
            sum1 = jnp.sum(jnp.where(is_low, 0.0, p), axis=1, keepdims=True)
            p = p * jnp.where(is_low, 1.0 / sum0, 1.0 / sum1)
            probs_ref[c, j] = p
            att_ref[rows, cols] = dot(p.astype(BF16), vbd).astype(BF16)
        return 0

    kv_swap.wait()
    kv_ref[...] = add(kvp_ref[half], kvg_ref[...]).astype(BF16)
    lax.fori_loop(0, PAIRS, forward, 0)
    next(wide_steps)

    feature = lax.broadcasted_iota(jnp.int32, (DE, HALF), 0)
    column = lax.broadcasted_iota(jnp.int32, (DE, HALF), 1)

    def half_of(which):
        chosen = (feature == column + which * HALF).astype(F32).astype(BF16)
        return dot(att_ref[...], chosen).astype(BF16)

    slots_ref[0:4] = half_of(1 - half).reshape(4, R, HALF)
    att_swap = send(slots_ref.at[pl.ds(0, 4)], all_ref.at[half], swap_sems.at[3], partner)
    all_ref[half] = half_of(half).reshape(4, R, HALF)

    for lane_at, size in TILES:
        cols = slice(lane_at, lane_at + size)
        enc_ref[:, cols] = (emb_ref[:, cols].astype(F32) + dot(att_ref[...], wo_ref[:, cols])).astype(BF16)

    def project_own(i, _):
        cols = pl.ds(pl.multiple_of(i * 256, 256), 256)
        dkv_ref[0, :, cols] = dot(enc_ref[...], wd_ref[:, cols]).astype(BF16)
        return 0

    def project_other(i, _):
        cols = pl.ds(pl.multiple_of(i * 256, 256), 256)
        dkv_ref[1, :, cols] = dot(enc_ref[...], wb_ref[:, cols]).astype(BF16)
        return 0

    lax.fori_loop(0, DEC // 256, project_own, 0)
    pad(pad_emb_ref, emb_ref, 0)

    att_swap.wait()
    for e in range(16):
        unit, there = slot_ref[0, e], slot_ref[1, e]
        slots_ref[e] = all_ref[unit // 4, unit % 4] * there.astype(F32).astype(BF16)
    waiting = [
        send(slots_ref.at[span_at(k)], att_out.at[span], slot_sems.at[k], in_span(k))
        for k in range(15)
    ]
    stay = pltpu.make_async_copy(slots_ref.at[span], att_out.at[span], local_sems.at[0])
    stay.start()
    next(wide_steps)
    lax.fori_loop(0, DEC // 256, project_other, 0)
    q_swap.wait()
    og_swap.wait()
    scale = 1.0 / math.sqrt(HD)

    def decode(h, _):
        kcols = pl.ds(pl.multiple_of(h * HD, HD), HD)
        vcols = pl.ds(pl.multiple_of(DEC // 2 + h * HD, HD), HD)
        for g in range(2):
            for c in range(SPANS):
                few = slice(c * CH, (c + 1) * CH)
                rows = slice(c * NB * R, (c + 1) * NB * R)
                q = q_ref[half, few, kcols] if g == 0 else qo_ref[few, kcols]
                og = og_ref[half, few, kcols] if g == 0 else ogo_ref[few, kcols]
                k, v = dkv_ref[g, rows, kcols], dkv_ref[g, rows, vcols]
                s = dot_nt(q, k) * scale
                p = jnp.exp(s - jnp.max(s, axis=1, keepdims=True))
                p = p * (1.0 / jnp.sum(p, axis=1, keepdims=True))
                pb = p.astype(BF16)
                cross = dot(pb, v).astype(BF16)
                cross_ref[g, few, kcols] = cross
                gkv_ref[g, rows, vcols] = dot_tn(pb, og).astype(BF16)
                row = jnp.sum(og.astype(F32) * cross.astype(F32), axis=1, keepdims=True)
                ds = (p * (dot_nt(og, v) - row) * scale).astype(BF16)
                gkv_ref[g, rows, kcols] = dot_tn(ds, q).astype(BF16)
        return 0

    lax.fori_loop(0, 8, decode, 0)
    waiting.append(send(cross_ref.at[1], cross_out.at[half], swap_sems.at[4], partner))
    mine = pltpu.make_async_copy(cross_ref.at[0], cross_out.at[half], local_sems.at[1])
    mine.start()
    sum_ref[...] = jnp.zeros_like(sum_ref)

    def collect(i, _):
        cols = pl.ds(pl.multiple_of(i * 256, 256), 256)
        sum_ref[...] += dot_nt(gkv_ref[0, :, cols], wd_ref[:, cols]) + dot_nt(
            gkv_ref[1, :, cols], wb_ref[:, cols]
        )
        return 0

    lax.fori_loop(0, DEC // 256, collect, 0)
    enc_ref[...] = sum_ref[...].astype(BF16)

    def steps(k):
        sems = sum_sems.at[k]
        copies = [send(g_ref.at[k, 1 - core], core_ref.at[k], sems.at[0], peer)]
        yield
        copies[0].wait()
        for i in range(4):
            acc1_ref[k, i] = add(g_ref[k, core, i], core_ref[k, i]).astype(BF16)
        p, q = where[k], where[1 - k]
        far, up, down = mod(p + 2), mod(p + 1), mod(p - 1)
        one, two = pl.ds(0, 2), pl.ds(2, 2)
        copies = [
            send(acc1_ref.at[k, far, one], first1_ref.at[k, 0], sems.at[1], along(k, 1)),
            send(acc1_ref.at[k, far, two], first1_ref.at[k, 1], sems.at[2], along(k, -1)),
        ]
        yield
        for copy in copies:
            copy.wait()
        acc1_ref[k, up, one] = add(acc1_ref[k, up, one], first1_ref[k, 0]).astype(BF16)
        acc1_ref[k, down, two] = add(acc1_ref[k, down, two], first1_ref[k, 1]).astype(BF16)
        copies = [
            send(acc1_ref.at[k, up], first2_ref.at[k, 0], sems.at[3], along(k, 1)),
            send(acc1_ref.at[k, down], first2_ref.at[k, 1], sems.at[4], along(k, -1)),
        ]
        yield
        for copy in copies:
            copy.wait()
        acc2_ref[k] = add(acc1_ref[k, p], first2_ref[k, 0], first2_ref[k, 1]).astype(BF16)
        copies = [
            send(acc2_ref.at[k, mod(q + j)], second_ref.at[k, j - 1], sems.at[4 + j], along(1 - k, j))
            for j in range(1, 4)
        ]
        yield
        for copy in copies:
            copy.wait()
        acc3_ref[k] = add(acc2_ref[k, q], second_ref[k, 0], second_ref[k, 1], second_ref[k, 2]).astype(BF16)
        copies = []
        for n, other in enumerate(others):
            to_low = x_low if n == 1 else 1 - x_low
            copies.append(send(acc3_ref.at[k, to_low], last_ref.at[k, n], sems.at[8 + n], other))
        yield
        for copy in copies:
            copy.wait()
        (rq_ref, ro_ref)[k][...] = add(acc3_ref[k, x_low], last_ref[k, 0], last_ref[k, 1], last_ref[k, 2])
        yield

    def outer(k, padded_ref, ref):
        def tile(i, _):
            cols = pl.ds(pl.multiple_of(i * 256, 256), 256)
            g_ref[k, i // 2, pl.ds((i % 2) * 2, 2)] = (
                dot_tn(padded_ref[:, cols], ref[...]).astype(BF16).reshape(2, 4, 2, 16, DE)
            )
            return 0

        lax.fori_loop(0, PADDED // 256, tile, 0)

    pad(pad_ref, enc_ref, 1)
    outer(1, pad_ref, att_ref)
    out_sum = steps(1)
    next(out_sum)
    for lane_at, size in TILES:
        cols = slice(lane_at, lane_at + size)
        eq_ref[:, cols] = dot_nt(enc_ref[...], wo_ref[cols, :]).astype(BF16)
    next(out_sum)

    def backward(j, _):
        cols = pl.ds(pl.multiple_of(j * PAIR, PAIR), PAIR)
        for c in range(SPANS):
            rows = slice(c * NB * R, (c + 1) * NB * R)
            kbd, vbd = pair_blocks(kv_ref, c, j, low, high)
            ga = eq_ref[rows, cols]
            prod = ga.astype(F32) * att_ref[rows, cols].astype(F32)
            row0 = jnp.sum(jnp.where(is_low, prod, 0.0), axis=1, keepdims=True)
            row1 = jnp.sum(jnp.where(is_low, 0.0, prod), axis=1, keepdims=True)
            diff = dot_nt(ga, vbd) - jnp.where(is_low, row0, row1)
            ds = (probs_ref[c, j] * diff * (1.0 / math.sqrt(EHD))).astype(BF16)
            eq_ref[rows, cols] = dot(ds, kbd).astype(BF16)
        return 0

    lax.fori_loop(0, PAIRS, backward, 0)
    next(out_sum)
    next(out_sum)
    outer(0, pad_emb_ref, eq_ref)
    query_sum = steps(0)
    for _ in range(6):
        next(query_sum)
        next(out_sum, None)
    for copy in waiting:
        copy.wait()
    mine.wait()
    stay.wait()


def run(slot, pos, alt, rows, table, states, w_span, q, og, w_q, w_o, w_d, wqo):
    vmem = pl.BlockSpec(memory_space=pltpu.VMEM)
    anywhere = pl.BlockSpec(memory_space=pl.ANY)
    dma = pltpu.SemaphoreType.DMA
    return pl.pallas_call(
        mega,
        out_shape=(
            jax.ShapeDtypeStruct((16, R, HALF), BF16),
            jax.ShapeDtypeStruct((2, SPANS * CH, DEC // 2), BF16),
            jax.ShapeDtypeStruct((16, DE), F32),
            jax.ShapeDtypeStruct((16, DE), F32),
        ),
        in_specs=[pl.BlockSpec(memory_space=pltpu.SMEM), vmem, vmem, anywhere, vmem, anywhere, vmem, anywhere]
        + [vmem] * 6,
        out_specs=(anywhere, anywhere, vmem, vmem),
        scratch_shapes=[
            pltpu.VMEM((16 * ROOM - TOK, DE), F32),
            pltpu.VMEM((16, ROOM, DE), BF16),
            pltpu.VMEM((16, ROOM, DE), BF16),
            pltpu.VMEM((TOK, DE), BF16),
            pltpu.VMEM((2, SPANS * CH, 2 * DE), BF16),
            pltpu.VMEM((SPANS * CH, 2 * DE), BF16),
            pltpu.VMEM((SPANS * CH, 2 * DE), BF16),
            pltpu.VMEM((SPANS * CH, DEC // 2), BF16),
            pltpu.VMEM((SPANS * CH, DEC // 2), BF16),
            pltpu.VMEM((DE, DEC), BF16),
            pltpu.VMEM((16, HALF, 128), BF16),
            pltpu.VMEM((DE, DE), BF16),
            pltpu.VMEM((DE, DE), BF16),
            pltpu.VMEM((TOK, DE), BF16),
            pltpu.VMEM((TOK, DE), BF16),
            pltpu.VMEM((SPANS, PAIRS, NB * R, PAIR), F32),
            pltpu.VMEM((TOK, DE), BF16),
            pltpu.VMEM((2, TOK, DEC), BF16),
            pltpu.VMEM((2, TOK, DEC), BF16),
            pltpu.VMEM((TOK, DE), F32),
            pltpu.VMEM((TOK, PADDED), BF16),
            pltpu.VMEM((TOK, PADDED), BF16),
            pltpu.VMEM((2, SPANS * CH, DEC // 2), BF16),
            pltpu.VMEM((2, 4, R, HALF), BF16),
            pltpu.VMEM((16, R, HALF), BF16),
            pltpu.VMEM((2, 2, 4, 4, 2, 16, DE), BF16),
            pltpu.VMEM((2, 4, 4, 2, 16, DE), BF16),
            pltpu.VMEM((2, 4, 4, 2, 16, DE), BF16),
            pltpu.VMEM((2, 2, 2, 2, 16, DE), BF16),
            pltpu.VMEM((2, 2, 4, 2, 16, DE), BF16),
            pltpu.VMEM((2, 4, 2, 16, DE), BF16),
            pltpu.VMEM((2, 3, 2, 16, DE), BF16),
            pltpu.VMEM((2, 2, 16, DE), BF16),
            pltpu.VMEM((2, 3, 16, DE), BF16),
            dma((15, 2)),
            dma((5, 2)),
            dma((2, 2, 6, 2)),
            dma((15, 2)),
            dma((2, 11, 2)),
            dma((13,)),
        ],
        compiler_params=pltpu.CompilerParams(
            vmem_limit_bytes=63 * 2**20, collective_id=1, has_side_effects=True
        ),
        cost_estimate=pl.CostEstimate(
            flops=16 * 10**9, bytes_accessed=30 * 2**20, transcendentals=10**6
        ),
    )(slot, jnp.asarray(piece_rows()), pos, alt, rows, table, states, w_span, q, og, w_q, w_o, w_d, wqo)


def body(
    span_states,
    queries,
    out_grad,
    neighbour_ids,
    assignment,
    embed_table,
    w_span_kv,
    w_query_enc,
    w_out_enc,
    w_dec_kv,
):
    bf16 = jnp.bfloat16
    n_span = lax.axis_size("span")
    span_index = lax.axis_index("span")
    half_index = lax.axis_index("mp")
    seq_count, local_tokens, half_width = span_states.shape
    spans = local_tokens // CH
    units = spans * NB
    dec_cols = 2 * queries.shape[2]
    vocab_rows = embed_table.shape[0]
    tokens = units * R

    ids_m = lax.dynamic_index_in_dim(
        neighbour_ids.reshape(seq_count, n_span, tokens), half_index, 0, keepdims=False
    )
    rows, pos, over = lists(ids_m, span_index, vocab_rows, n_span)

    def whole_gather():
        shifted = ids_m.reshape(-1) - span_index * vocab_rows
        inside = (shifted >= 0) & (shifted < vocab_rows)
        found = jnp.take(embed_table, jnp.clip(shifted, 0, vocab_rows - 1), axis=0)
        found = jnp.where(inside[:, None], found, jnp.zeros_like(found))
        found = lax.all_to_all(
            found.reshape(n_span, tokens, DE), "span", split_axis=0, concat_axis=0, tiled=True
        )
        return jnp.sum(found.astype(F32), axis=0).astype(bf16)

    alt = lax.cond(over, whole_gather, lambda: jnp.zeros((tokens, DE), bf16))

    core = lax.axis_index("dp") % 2
    wqo = []
    for r in range(2):
        group = span_index % 4 if r == 0 else span_index // 4
        start = (core * 2 + r) * 112
        from_q = lax.dynamic_slice(w_query_enc, (group * HALF + start, 0), (112, HALF))
        from_o = lax.dynamic_slice(w_out_enc, (start, (group - 2) * 512), (112, 512))
        from_q = jnp.concatenate([from_q[:, :384], from_q[:, HALF - 128 :]], axis=1)
        wqo.append(jnp.where(group < 2, from_q, from_o))
    wqo = jnp.transpose(jnp.stack(wqo).reshape(2, 112, 4, 128), (0, 2, 1, 3))

    dest = lax.dynamic_index_in_dim(assignment[0, :, :, 0], span_index, 0, keepdims=False)
    at = dest[None, :] == jnp.arange(n_span, dtype=jnp.int32)[:, None]
    numbers = jnp.arange(seq_count * units, dtype=jnp.int32)
    slot = jnp.stack(
        [
            jnp.sum(jnp.where(at, numbers[None, :], 0), axis=1),
            jnp.sum(at.astype(jnp.int32), axis=1),
            jnp.full((n_span,), over.astype(jnp.int32)),
        ]
    )
    attended_out, cross_out, rq, ro = run(
        slot,
        pos[:, None],
        alt,
        rows.reshape(-1, 1),
        embed_table,
        span_states.reshape(-1, half_width),
        w_span_kv,
        queries,
        out_grad,
        w_query_enc,
        w_out_enc,
        w_dec_kv.reshape(DE, dec_cols),
        wqo,
    )
    grad_query_enc = lax.dynamic_slice_in_dim(rq[:PIECE], half_index * HALF, HALF, 1)
    grad_out_enc = lax.dynamic_slice_in_dim(ro[:PIECE], half_index * HALF, HALF, 1).T
    return (
        cross_out,
        attended_out.reshape(1, 1, n_span, 1, R, HALF),
        grad_query_enc,
        grad_out_enc,
    )


def solution(mesh):
    return jax.shard_map(
        body,
        mesh=mesh,
        in_specs=(
            P("dp", "span", "mp"),
            P("dp", "span", "mp"),
            P("dp", "span", "mp"),
            P("dp", None, None, None),
            P("dp", None, None, None),
            P("span", None),
            P("mp", None),
            P(None, "mp"),
            P("mp", None),
            P(None, None, "mp"),
        ),
        out_specs=(
            P("dp", "span", "mp"),
            P("dp", "span", None, None, None, "mp"),
            P(("span", "dp"), "mp"),
            P("mp", ("span", "dp")),
        ),
        check_vma=False,
    )
```

```python
import math

import jax
import jax.numpy as jnp
import numpy as np
from jax import lax
from jax.experimental import pallas as pl
from jax.experimental.pallas import tpu as pltpu
from jax.sharding import PartitionSpec as P

HD = 128
DE = 896
EHD = 64
R = 128
CH = 64
NB = 2
ROOM = 48


def lists(ids_m, span_index, vocab_rows, n_span):
    tokens = ids_m.shape[1]
    t = jnp.arange(tokens, dtype=jnp.int32)
    same = ids_m[:, :, None] == ids_m[:, None, :]
    dup = jnp.any(same & (t[None, None, :] < t[None, :, None]), axis=2)
    uniq = jnp.logical_not(dup)
    src = ids_m // vocab_rows
    shards = jnp.arange(n_span, dtype=jnp.int32)
    counts = jnp.sum(
        (uniq[:, None, :] & (src[:, None, :] == shards[None, :, None])).astype(jnp.int32), axis=2
    )
    over = jnp.max(counts) > ROOM
    sel = uniq & (src == span_index)
    tri = (t[:, None] < t[None, :]).astype(jnp.bfloat16)
    rank = jnp.dot(sel.astype(jnp.bfloat16), tri, preferred_element_type=jnp.float32).astype(
        jnp.int32
    )
    room = jnp.arange(ROOM, dtype=jnp.int32)
    local = ids_m - span_index * vocab_rows
    rows = jnp.sum(
        jnp.where(
            (rank[:, None, :] == room[None, :, None]) & sel[:, None, :], local[:, None, :], 0
        ),
        axis=2,
    )
    own = lax.dynamic_index_in_dim(ids_m, span_index, 0, keepdims=False)
    own_src = own // vocab_rows
    own_same = own[:, None] == own[None, :]
    first = jnp.min(jnp.where(own_same, t[None, :], tokens), axis=1)
    own_uniq = first == t
    own_rank = jnp.sum(
        (
            own_uniq[None, :]
            & (own_src[:, None] == own_src[None, :])
            & (t[None, :] < first[:, None])
        ).astype(jnp.int32),
        axis=1,
    )
    return rows, own_src * ROOM + own_rank, over


F32 = jnp.float32
BF16 = jnp.bfloat16
PAIR = 2 * EHD
HEADS_ENC = DE // EHD
PAIRS = HEADS_ENC // 2
TOK = 512
SPANS = 2
DEC = 2048
HALF = DE // 2
PADDED = 1024
PIECE = 14
TILES = ((0, 256), (256, 256), (512, 256), (768, 128))


def dot(a, b):
    return jnp.dot(a, b, preferred_element_type=F32)


def dot_nt(a, b):
    return lax.dot_general(a, b, (((1,), (1,)), ((), ())), preferred_element_type=F32)


def dot_tn(a, b):
    return lax.dot_general(a, b, (((0,), (0,)), ((), ())), preferred_element_type=F32)


def piece_rows():
    rows = np.full((2, PADDED), -1, np.int32)
    n = 0
    for core in range(2):
        for first in range(4):
            for second in range(4):
                for low in range(2):
                    for r in range(16):
                        if r < PIECE:
                            rows[0, n] = (((first * 4 + second) * 2 + low) * 2 + core) * PIECE + r
                            rows[1, n] = (((second * 4 + first) * 2 + low) * 2 + core) * PIECE + r
                        n += 1
    return rows


def pair_blocks(kv_ref, c, j, low, high):
    rows = slice(c * CH, (c + 1) * CH)
    k = kv_ref[rows, pl.ds(pl.multiple_of(j * PAIR, PAIR), PAIR)]
    v = kv_ref[rows, pl.ds(pl.multiple_of(DE + j * PAIR, PAIR), PAIR)]
    return (
        jnp.concatenate([k * low, k * high], axis=0),
        jnp.concatenate([v * low, v * high], axis=0),
    )


def mega(
    slot_ref,
    rows_ref,
    pos_ref,
    alt_ref,
    list_ref,
    table_ref,
    states_ref,
    wspan_ref,
    q_ref,
    og_ref,
    wq_own_ref,
    wo_own_ref,
    wd_ref,
    wqo_ref,
    att_out,
    cross_out,
    rq_ref,
    ro_ref,
    picked_ref,
    sent_ref,
    got_ref,
    emb_ref,
    kvp_ref,
    kvg_ref,
    kv_ref,
    qo_ref,
    ogo_ref,
    wb_ref,
    sb_ref,
    wq_ref,
    wo_ref,
    eq_ref,
    att_ref,
    probs_ref,
    enc_ref,
    dkv_ref,
    gkv_ref,
    sum_ref,
    pad_ref,
    pad_emb_ref,
    cross_ref,
    all_ref,
    slots_ref,
    g_ref,
    core_ref,
    acc1_ref,
    first_ref,
    acc2_ref,
    second_ref,
    acc3_ref,
    last_ref,
    emb_sems,
    swap_sems,
    weight_sems,
    slot_sems,
    sum_sems,
    local_sems,
):
    span, dp, half = lax.axis_index("span"), lax.axis_index("dp"), lax.axis_index("mp")
    z, y, x_low, core = span // 4, span % 4, dp // 2, dp % 2
    partner = {"span": span, "dp": dp, "mp": 1 - half}
    peer = {"span": span, "dp": x_low * 2 + 1 - core, "mp": half}
    where = (z, y)

    offsets = ((0, 1), (1, 0), (0, 3), (3, 0), (2, 1), (1, 2), (2, 3), (3, 2), (1, 1), (3, 3), (1, 3), (3, 1), (2, 0), (0, 2), (2, 2))

    def span_at(k):
        return lax.rem(z + offsets[k][0], 4) * 4 + lax.rem(y + offsets[k][1], 4)

    def in_span(k):
        return {"span": span_at(k), "dp": dp, "mp": half}

    def along(axis, by):
        if axis == 0:
            return {"span": lax.rem(z + by + 4, 4) * 4 + y, "dp": dp, "mp": half}
        return {"span": z * 4 + lax.rem(y + by + 4, 4), "dp": dp, "mp": half}

    others = [
        {"span": span, "dp": (1 - x_low) * 2 + core, "mp": half},
        partner,
        {"span": span, "dp": (1 - x_low) * 2 + core, "mp": 1 - half},
    ]
    def area(i):
        return (dkv_ref, gkv_ref)[i // 4].at[(i // 2) % 2, :, pl.ds((i % 2) * 1024, DE)]

    vocab = table_ref.shape[0]
    sizes = [min(512, vocab - at) for at in range(0, vocab, 512)]
    table_in = [
        pltpu.make_async_copy(
            table_ref.at[pl.ds(i * 512, size)], area(i).at[pl.ds(0, size)], local_sems.at[5 + i]
        )
        for i, size in enumerate(sizes)
    ]
    spans_in = [
        pltpu.make_async_copy(
            wspan_ref.at[pl.ds(i * 512, 512)],
            (dkv_ref, gkv_ref)[i // 2].at[i % 2, :, pl.ds(0, 2 * DE)],
            local_sems.at[i],
        )
        for i in range(4)
    ]
    alt_in = pltpu.make_async_copy(alt_ref, eq_ref, local_sems.at[4])
    for copy in table_in:
        copy.start()
    alt_in.start()

    barrier = pltpu.get_barrier_semaphore()
    friends = [in_span(k) for k in range(15)] + [peer] + others
    for friend in friends:
        pl.semaphore_signal(barrier, inc=1, device_id=friend, device_id_type=pl.DeviceIdType.MESH)
    pl.semaphore_wait(barrier, len(friends))

    def send(src, dst, sems, device):
        copy = pltpu.make_async_remote_copy(
            src_ref=src,
            dst_ref=dst,
            send_sem=sems.at[0],
            recv_sem=sems.at[1],
            device_id=device,
            device_id_type=pl.DeviceIdType.MESH,
        )
        copy.start()
        return copy

    def add(*parts):
        total = parts[0].astype(F32)
        for part in parts[1:]:
            total = total + part.astype(F32)
        return total

    def mod(v):
        return lax.rem(v + 4, 4)

    ranks = ((z, y), (y, z))

    def at(kind, r, group, piece, count):
        n = core * 2 + r
        if kind:
            return wb_ref.at[
                pl.ds(pl.multiple_of(n * 224, 224), 224),
                pl.ds(pl.multiple_of(group * 512 + piece * 128, 128), count * 128),
            ]
        return sb_ref.at[pl.ds(group * 4 + piece, count), pl.ds(pl.multiple_of(n * 112, 112), 112)]

    def weight_steps(kind):
        sems = weight_sems.at[kind]
        copies = []
        for r in range(2):
            s = ranks[r][1]
            n = core * 2 + r
            if kind:
                src = wd_ref.at[
                    pl.ds(pl.multiple_of(n * 224, 224), 224), pl.ds(pl.multiple_of(s * 512, 512), 512)
                ]
            else:
                src = wqo_ref.at[r]
            copies.append([send(src, at(kind, r, s, 0, 4), sems.at[r, 0], others[2])])
        yield
        for r in range(2):
            s = ranks[r][1]
            for copy in copies[r]:
                copy.wait()
            whole = at(kind, r, s, 0, 4)
            copies[r] = [
                send(whole, whole, sems.at[r, 1 + i], along(1 - r, by)) for i, by in enumerate((1, -1))
            ]
        yield
        for r in range(2):
            s = ranks[r][1]
            for copy in copies[r]:
                copy.wait()
            copies[r] = []
            for i, by in enumerate((1, -1)):
                part = at(kind, r, mod(s - by), 2 * i, 2)
                copies[r].append(send(part, part, sems.at[r, 3 + i], along(1 - r, by)))
        yield
        for r in range(2):
            for copy in copies[r]:
                copy.wait()
            n = core * 2 + r
            if kind:
                mine = wb_ref.at[pl.ds(pl.multiple_of(n * 224, 224), 224)]
            else:
                mine = sb_ref.at[:, pl.ds(pl.multiple_of(n * 112, 112), 112)]
            copies[r] = [send(mine, mine, sems.at[r, 5], peer)]
        yield
        for r in range(2):
            for copy in copies[r]:
                copy.wait()
        yield

    small_steps, wide_steps = weight_steps(0), weight_steps(1)
    next(small_steps)
    next(wide_steps)

    rank = lax.broadcasted_iota(jnp.int32, (1, 512), 1)
    for i, size in enumerate(sizes):
        table_in[i].wait()
        chosen = (list_ref[...] == rank + i * 512).astype(F32).astype(BF16)
        part = dot(chosen[:, :size], area(i)[:size, :])
        if i == 0:
            sum_ref[...], picked_ref[...] = part[:TOK], part[TOK:]
        else:
            sum_ref[...] += part[:TOK]
            picked_ref[...] += part[TOK:]
        if i == 4:
            next(small_steps)
    picked = jnp.concatenate([sum_ref[...], picked_ref[...]], axis=0)
    sent_ref[...] = picked.astype(BF16).reshape(16, ROOM, DE)
    for copy in spans_in:
        copy.start()
    embs = [
        send(sent_ref.at[span_at(k)], got_ref.at[span], emb_sems.at[k], in_span(k))
        for k in range(15)
    ]
    got_ref[span] = sent_ref[span]
    next(small_steps)
    next(wide_steps)

    for copy in spans_in:
        copy.wait()

    def project_span(i, _):
        cols = pl.ds(pl.multiple_of(i * 256, 256), 256)
        total = jnp.zeros((2 * SPANS * CH, 256), F32)
        for n in range(4):
            total += dot(states_ref[:, n * 512 : (n + 1) * 512], (dkv_ref, gkv_ref)[n // 2][n % 2, :, cols])
        total = total.astype(BF16)
        kvp_ref[0, :, cols] = total[: SPANS * CH]
        kvp_ref[1, :, cols] = total[SPANS * CH :]
        return 0

    lax.fori_loop(0, 2 * DE // 256, project_span, 0)
    kv_swap = send(kvp_ref.at[1 - half], kvg_ref, swap_sems.at[0], partner)
    q_swap = send(q_ref.at[1 - half], qo_ref, swap_sems.at[1], partner)
    og_swap = send(og_ref.at[1 - half], ogo_ref, swap_sems.at[2], partner)

    next(small_steps)
    next(small_steps)

    place = lax.broadcasted_iota(jnp.int32, (HALF, 256), 0)
    wide = lax.broadcasted_iota(jnp.int32, (512, 256), 0)
    wide = jnp.where(wide < 384, wide, jnp.where(wide >= 448, wide - 64, -DE))
    col = lax.broadcasted_iota(jnp.int32, (HALF, 256), 1)
    wide_col = lax.broadcasted_iota(jnp.int32, (512, 256), 1)
    for lane_at, size in TILES:
        mine = (place + half * HALF == col + lane_at).astype(F32).astype(BF16)[:, :size]
        his = (wide + (1 - half) * HALF == wide_col + lane_at).astype(F32).astype(BF16)[:, :size]
        for up in range(2):
            rows = slice(up * HALF, (up + 1) * HALF)
            other = jnp.concatenate([sb_ref[up * 4 + i] for i in range(4)], axis=1)
            wq_ref[rows, lane_at : lane_at + size] = (dot(wq_own_ref[rows, :], mine) + dot(other, his)).astype(BF16)
    wo_ref[pl.ds(pl.multiple_of(half * HALF, HALF), HALF), :] = wo_own_ref[...]
    for i in range(7):
        wo_ref[pl.ds(pl.multiple_of((1 - half) * HALF, HALF), HALF), i * 128 : (i + 1) * 128] = sb_ref[8 + i if i < 4 else 9 + i]

    for copy in embs:
        copy.wait()
    alt_in.wait()
    slot_of = lax.broadcasted_iota(jnp.int32, (1, 16 * ROOM), 1)
    pick = (pos_ref[...] == slot_of).astype(F32).astype(BF16)
    over = slot_ref[2, 0] > 0
    for lane_at, size in TILES:
        cols = slice(lane_at, lane_at + size)
        rows = jnp.concatenate([got_ref[i, :, cols] for i in range(16)], axis=0)
        emb_ref[:, cols] = jnp.where(over, eq_ref[:, cols].astype(F32), dot(pick, rows)).astype(BF16)

    next(wide_steps)
    lane = lax.broadcasted_iota(jnp.int32, (1, PAIR), 1)
    is_low = lane < EHD
    low = is_low.astype(F32).astype(BF16)
    high = (lane >= EHD).astype(F32).astype(BF16)

    def pad(to_ref, ref, order):
        for lane_at in range(0, PADDED, 256):
            spread = (
                lax.broadcasted_iota(jnp.int32, (DE, 256), 0)
                == rows_ref[order : order + 1, lane_at : lane_at + 256]
            )
            to_ref[:, lane_at : lane_at + 256] = dot(ref[...], spread.astype(F32).astype(BF16)).astype(BF16)

    for lane_at, size in TILES:
        cols = slice(lane_at, lane_at + size)
        eq_ref[:, cols] = dot(emb_ref[...], wq_ref[:, cols]).astype(BF16)

    def forward(j, _):
        cols = pl.ds(pl.multiple_of(j * PAIR, PAIR), PAIR)
        for c in range(SPANS):
            rows = slice(c * NB * R, (c + 1) * NB * R)
            kbd, vbd = pair_blocks(kv_ref, c, j, low, high)
            s = dot_nt(eq_ref[rows, cols], kbd) * (1.0 / math.sqrt(EHD))
            top0 = jnp.max(jnp.where(is_low, s, -jnp.inf), axis=1, keepdims=True)
            top1 = jnp.max(jnp.where(is_low, -jnp.inf, s), axis=1, keepdims=True)
            p = jnp.exp(s - jnp.where(is_low, top0, top1))
            sum0 = jnp.sum(jnp.where(is_low, p, 0.0), axis=1, keepdims=True)
            sum1 = jnp.sum(jnp.where(is_low, 0.0, p), axis=1, keepdims=True)
            p = p * jnp.where(is_low, 1.0 / sum0, 1.0 / sum1)
            probs_ref[c, j] = p
            att_ref[rows, cols] = dot(p.astype(BF16), vbd).astype(BF16)
        return 0

    kv_swap.wait()
    kv_ref[...] = add(kvp_ref[half], kvg_ref[...]).astype(BF16)
    lax.fori_loop(0, PAIRS, forward, 0)
    next(wide_steps)

    feature = lax.broadcasted_iota(jnp.int32, (DE, HALF), 0)
    column = lax.broadcasted_iota(jnp.int32, (DE, HALF), 1)

    def half_of(which):
        chosen = (feature == column + which * HALF).astype(F32).astype(BF16)
        return dot(att_ref[...], chosen).astype(BF16)

    slots_ref[0:4] = half_of(1 - half).reshape(4, R, HALF)
    att_swap = send(slots_ref.at[pl.ds(0, 4)], all_ref.at[half], swap_sems.at[3], partner)
    all_ref[half] = half_of(half).reshape(4, R, HALF)

    for lane_at, size in TILES:
        cols = slice(lane_at, lane_at + size)
        enc_ref[:, cols] = (emb_ref[:, cols].astype(F32) + dot(att_ref[...], wo_ref[:, cols])).astype(BF16)

    def project_own(i, _):
        cols = pl.ds(pl.multiple_of(i * 256, 256), 256)
        dkv_ref[0, :, cols] = dot(enc_ref[...], wd_ref[:, cols]).astype(BF16)
        return 0

    def project_other(i, _):
        cols = pl.ds(pl.multiple_of(i * 256, 256), 256)
        dkv_ref[1, :, cols] = dot(enc_ref[...], wb_ref[:, cols]).astype(BF16)
        return 0

    lax.fori_loop(0, DEC // 256, project_own, 0)
    pad(pad_emb_ref, emb_ref, 0)

    att_swap.wait()
    for e in range(16):
        unit, there = slot_ref[0, e], slot_ref[1, e]
        slots_ref[e] = all_ref[unit // 4, unit % 4] * there.astype(F32).astype(BF16)
    waiting = [
        send(slots_ref.at[span_at(k)], att_out.at[span], slot_sems.at[k], in_span(k))
        for k in range(15)
    ]
    stay = pltpu.make_async_copy(slots_ref.at[span], att_out.at[span], local_sems.at[0])
    stay.start()
    next(wide_steps)
    lax.fori_loop(0, DEC // 256, project_other, 0)
    q_swap.wait()
    og_swap.wait()
    scale = 1.0 / math.sqrt(HD)

    def decode(h, _):
        kcols = pl.ds(pl.multiple_of(h * HD, HD), HD)
        vcols = pl.ds(pl.multiple_of(DEC // 2 + h * HD, HD), HD)
        for g in range(2):
            for c in range(SPANS):
                few = slice(c * CH, (c + 1) * CH)
                rows = slice(c * NB * R, (c + 1) * NB * R)
                q = q_ref[half, few, kcols] if g == 0 else qo_ref[few, kcols]
                og = og_ref[half, few, kcols] if g == 0 else ogo_ref[few, kcols]
                k, v = dkv_ref[g, rows, kcols], dkv_ref[g, rows, vcols]
                s = dot_nt(q, k) * scale
                p = jnp.exp(s - jnp.max(s, axis=1, keepdims=True))
                p = p * (1.0 / jnp.sum(p, axis=1, keepdims=True))
                pb = p.astype(BF16)
                cross = dot(pb, v).astype(BF16)
                cross_ref[g, few, kcols] = cross
                gkv_ref[g, rows, vcols] = dot_tn(pb, og).astype(BF16)
                row = jnp.sum(og.astype(F32) * cross.astype(F32), axis=1, keepdims=True)
                ds = (p * (dot_nt(og, v) - row) * scale).astype(BF16)
                gkv_ref[g, rows, kcols] = dot_tn(ds, q).astype(BF16)
        return 0

    lax.fori_loop(0, 8, decode, 0)
    waiting.append(send(cross_ref.at[1], cross_out.at[half], swap_sems.at[4], partner))
    mine = pltpu.make_async_copy(cross_ref.at[0], cross_out.at[half], local_sems.at[1])
    mine.start()
    sum_ref[...] = jnp.zeros_like(sum_ref)

    def collect(i, _):
        cols = pl.ds(pl.multiple_of(i * 256, 256), 256)
        sum_ref[...] += dot_nt(gkv_ref[0, :, cols], wd_ref[:, cols]) + dot_nt(
            gkv_ref[1, :, cols], wb_ref[:, cols]
        )
        return 0

    lax.fori_loop(0, DEC // 256, collect, 0)
    enc_ref[...] = sum_ref[...].astype(BF16)

    def steps(job):
        k, lanes = ((0, slice(0, 512)), (0, slice(512, DE)), (1, slice(0, DE)))[job]
        wide = pl.ds(lanes.start, lanes.stop - lanes.start)
        axis = (0, 1, 1)[job]
        flip = job == 1
        p, q = where[axis], where[1 - axis]
        sems = sum_sems.at[job]
        copies = [
            send(g_ref.at[k, 1 - core, :, :, :, :, wide], core_ref.at[k, :, :, :, :, wide], sems.at[0], peer)
        ]
        yield
        copies[0].wait()
        for i in range(4):
            acc1_ref[k, i, :, :, :, lanes] = add(
                g_ref[k, core, i, :, :, :, lanes], core_ref[k, i, :, :, :, lanes]
            ).astype(BF16)
        copies = []
        for j in range(1, 4):
            to = mod(p + j)
            block = acc1_ref.at[k, :, to, :, :, wide] if flip else acc1_ref.at[k, to, :, :, :, wide]
            copies.append(send(block, first_ref.at[k, j - 1, :, :, :, wide], sems.at[j], along(axis, j)))
        yield
        for copy in copies:
            copy.wait()
        own = acc1_ref[k, :, p, :, :, lanes] if flip else acc1_ref[k, p, :, :, :, lanes]
        acc2_ref[k, :, :, :, lanes] = add(own, *[first_ref[k, j, :, :, :, lanes] for j in range(3)]).astype(BF16)
        copies = [
            send(
                acc2_ref.at[k, mod(q + j), :, :, wide],
                second_ref.at[k, j - 1, :, :, wide],
                sems.at[3 + j],
                along(1 - axis, j),
            )
            for j in range(1, 4)
        ]
        yield
        for copy in copies:
            copy.wait()
        acc3_ref[k, :, :, lanes] = add(
            acc2_ref[k, q, :, :, lanes], *[second_ref[k, j, :, :, lanes] for j in range(3)]
        ).astype(BF16)
        copies = []
        for n, other in enumerate(others):
            to_low = x_low if n == 1 else 1 - x_low
            copies.append(
                send(acc3_ref.at[k, to_low, :, wide], last_ref.at[k, n, :, wide], sems.at[7 + n], other)
            )
        yield
        for copy in copies:
            copy.wait()
        (rq_ref, ro_ref)[k][:, lanes] = add(
            acc3_ref[k, x_low, :, lanes], *[last_ref[k, n, :, lanes] for n in range(3)]
        )
        yield

    def outer(k, padded_ref, ref, lanes):
        def tile(i, _):
            cols = pl.ds(pl.multiple_of(i * 256, 256), 256)
            g_ref[k, i // 2, pl.ds((i % 2) * 2, 2), :, :, :, lanes] = (
                dot_tn(padded_ref[:, cols], ref[:, lanes]).astype(BF16).reshape(2, 4, 2, 16, -1)
            )
            return 0

        lax.fori_loop(0, PADDED // 256, tile, 0)

    pad(pad_ref, enc_ref, 1)
    outer(1, pad_ref, att_ref, slice(0, DE))
    out_sum = steps(2)
    next(out_sum)
    for lane_at, size in TILES:
        cols = slice(lane_at, lane_at + size)
        eq_ref[:, cols] = dot_nt(enc_ref[...], wo_ref[cols, :]).astype(BF16)
    next(out_sum)

    def backward(j, _):
        cols = pl.ds(pl.multiple_of(j * PAIR, PAIR), PAIR)
        for c in range(SPANS):
            rows = slice(c * NB * R, (c + 1) * NB * R)
            kbd, vbd = pair_blocks(kv_ref, c, j, low, high)
            ga = eq_ref[rows, cols]
            prod = ga.astype(F32) * att_ref[rows, cols].astype(F32)
            row0 = jnp.sum(jnp.where(is_low, prod, 0.0), axis=1, keepdims=True)
            row1 = jnp.sum(jnp.where(is_low, 0.0, prod), axis=1, keepdims=True)
            diff = dot_nt(ga, vbd) - jnp.where(is_low, row0, row1)
            ds = (probs_ref[c, j] * diff * (1.0 / math.sqrt(EHD))).astype(BF16)
            eq_ref[rows, cols] = dot(ds, kbd).astype(BF16)
        return 0

    lax.fori_loop(0, 4, backward, 0)
    outer(0, pad_emb_ref, eq_ref, slice(0, 512))
    low_sum = steps(0)
    next(low_sum)
    lax.fori_loop(4, PAIRS, backward, 0)
    next(low_sum)
    next(out_sum)
    outer(0, pad_emb_ref, eq_ref, slice(512, DE))
    high_sum = steps(1)
    next(high_sum)
    next(high_sum)
    next(low_sum)
    next(out_sum)
    next(high_sum)
    next(low_sum)
    next(out_sum)
    next(high_sum)
    next(low_sum)
    next(high_sum)
    for copy in waiting:
        copy.wait()
    mine.wait()
    stay.wait()


def run(slot, pos, alt, rows, table, states, w_span, q, og, w_q, w_o, w_d, wqo):
    vmem = pl.BlockSpec(memory_space=pltpu.VMEM)
    anywhere = pl.BlockSpec(memory_space=pl.ANY)
    dma = pltpu.SemaphoreType.DMA
    return pl.pallas_call(
        mega,
        out_shape=(
            jax.ShapeDtypeStruct((16, R, HALF), BF16),
            jax.ShapeDtypeStruct((2, SPANS * CH, DEC // 2), BF16),
            jax.ShapeDtypeStruct((16, DE), F32),
            jax.ShapeDtypeStruct((16, DE), F32),
        ),
        in_specs=[pl.BlockSpec(memory_space=pltpu.SMEM), vmem, vmem, anywhere, vmem, anywhere, vmem, anywhere]
        + [vmem] * 6,
        out_specs=(anywhere, anywhere, vmem, vmem),
        scratch_shapes=[
            pltpu.VMEM((16 * ROOM - TOK, DE), F32),
            pltpu.VMEM((16, ROOM, DE), BF16),
            pltpu.VMEM((16, ROOM, DE), BF16),
            pltpu.VMEM((TOK, DE), BF16),
            pltpu.VMEM((2, SPANS * CH, 2 * DE), BF16),
            pltpu.VMEM((SPANS * CH, 2 * DE), BF16),
            pltpu.VMEM((SPANS * CH, 2 * DE), BF16),
            pltpu.VMEM((SPANS * CH, DEC // 2), BF16),
            pltpu.VMEM((SPANS * CH, DEC // 2), BF16),
            pltpu.VMEM((DE, DEC), BF16),
            pltpu.VMEM((16, HALF, 128), BF16),
            pltpu.VMEM((DE, DE), BF16),
            pltpu.VMEM((DE, DE), BF16),
            pltpu.VMEM((TOK, DE), BF16),
            pltpu.VMEM((TOK, DE), BF16),
            pltpu.VMEM((SPANS, PAIRS, NB * R, PAIR), F32),
            pltpu.VMEM((TOK, DE), BF16),
            pltpu.VMEM((2, TOK, DEC), BF16),
            pltpu.VMEM((2, TOK, DEC), BF16),
            pltpu.VMEM((TOK, DE), F32),
            pltpu.VMEM((TOK, PADDED), BF16),
            pltpu.VMEM((TOK, PADDED), BF16),
            pltpu.VMEM((2, SPANS * CH, DEC // 2), BF16),
            pltpu.VMEM((2, 4, R, HALF), BF16),
            pltpu.VMEM((16, R, HALF), BF16),
            pltpu.VMEM((2, 2, 4, 4, 2, 16, DE), BF16),
            pltpu.VMEM((2, 4, 4, 2, 16, DE), BF16),
            pltpu.VMEM((2, 4, 4, 2, 16, DE), BF16),
            pltpu.VMEM((2, 3, 4, 2, 16, DE), BF16),
            pltpu.VMEM((2, 4, 2, 16, DE), BF16),
            pltpu.VMEM((2, 3, 2, 16, DE), BF16),
            pltpu.VMEM((2, 2, 16, DE), BF16),
            pltpu.VMEM((2, 3, 16, DE), BF16),
            dma((15, 2)),
            dma((5, 2)),
            dma((2, 2, 6, 2)),
            dma((15, 2)),
            dma((3, 10, 2)),
            dma((13,)),
        ],
        compiler_params=pltpu.CompilerParams(
            vmem_limit_bytes=63 * 2**20, collective_id=1, has_side_effects=True
        ),
        cost_estimate=pl.CostEstimate(
            flops=16 * 10**9, bytes_accessed=30 * 2**20, transcendentals=10**6
        ),
    )(slot, jnp.asarray(piece_rows()), pos, alt, rows, table, states, w_span, q, og, w_q, w_o, w_d, wqo)


def body(
    span_states,
    queries,
    out_grad,
    neighbour_ids,
    assignment,
    embed_table,
    w_span_kv,
    w_query_enc,
    w_out_enc,
    w_dec_kv,
):
    bf16 = jnp.bfloat16
    n_span = lax.axis_size("span")
    span_index = lax.axis_index("span")
    half_index = lax.axis_index("mp")
    seq_count, local_tokens, half_width = span_states.shape
    spans = local_tokens // CH
    units = spans * NB
    dec_cols = 2 * queries.shape[2]
    vocab_rows = embed_table.shape[0]
    tokens = units * R

    ids_m = lax.dynamic_index_in_dim(
        neighbour_ids.reshape(seq_count, n_span, tokens), half_index, 0, keepdims=False
    )
    rows, pos, over = lists(ids_m, span_index, vocab_rows, n_span)

    def whole_gather():
        shifted = ids_m.reshape(-1) - span_index * vocab_rows
        inside = (shifted >= 0) & (shifted < vocab_rows)
        found = jnp.take(embed_table, jnp.clip(shifted, 0, vocab_rows - 1), axis=0)
        found = jnp.where(inside[:, None], found, jnp.zeros_like(found))
        found = lax.all_to_all(
            found.reshape(n_span, tokens, DE), "span", split_axis=0, concat_axis=0, tiled=True
        )
        return jnp.sum(found.astype(F32), axis=0).astype(bf16)

    alt = lax.cond(over, whole_gather, lambda: jnp.zeros((tokens, DE), bf16))

    core = lax.axis_index("dp") % 2
    wqo = []
    for r in range(2):
        group = span_index % 4 if r == 0 else span_index // 4
        start = (core * 2 + r) * 112
        from_q = lax.dynamic_slice(w_query_enc, (group * HALF + start, 0), (112, HALF))
        from_o = lax.dynamic_slice(w_out_enc, (start, (group - 2) * 512), (112, 512))
        from_q = jnp.concatenate([from_q[:, :384], from_q[:, HALF - 128 :]], axis=1)
        wqo.append(jnp.where(group < 2, from_q, from_o))
    wqo = jnp.transpose(jnp.stack(wqo).reshape(2, 112, 4, 128), (0, 2, 1, 3))

    dest = lax.dynamic_index_in_dim(assignment[0, :, :, 0], span_index, 0, keepdims=False)
    at = dest[None, :] == jnp.arange(n_span, dtype=jnp.int32)[:, None]
    numbers = jnp.arange(seq_count * units, dtype=jnp.int32)
    slot = jnp.stack(
        [
            jnp.sum(jnp.where(at, numbers[None, :], 0), axis=1),
            jnp.sum(at.astype(jnp.int32), axis=1),
            jnp.full((n_span,), over.astype(jnp.int32)),
        ]
    )
    attended_out, cross_out, rq, ro = run(
        slot,
        pos[:, None],
        alt,
        rows.reshape(-1, 1),
        embed_table,
        span_states.reshape(-1, half_width),
        w_span_kv,
        queries,
        out_grad,
        w_query_enc,
        w_out_enc,
        jnp.concatenate([w_dec_kv[:, 0], w_dec_kv[:, 1]], axis=1),
        wqo,
    )
    grad_query_enc = lax.dynamic_slice_in_dim(rq[:PIECE], half_index * HALF, HALF, 1)
    grad_out_enc = lax.dynamic_slice_in_dim(ro[:PIECE], half_index * HALF, HALF, 1).T
    return (
        cross_out,
        attended_out.reshape(1, 1, n_span, 1, R, HALF),
        grad_query_enc,
        grad_out_enc,
    )


def solution(mesh):
    return jax.shard_map(
        body,
        mesh=mesh,
        in_specs=(
            P("dp", "span", "mp"),
            P("dp", "span", "mp"),
            P("dp", "span", "mp"),
            P("dp", None, None, None),
            P("dp", None, None, None),
            P("span", None),
            P("mp", None),
            P(None, "mp"),
            P("mp", None),
            P(None, None, "mp"),
        ),
        out_specs=(
            P("dp", "span", "mp"),
            P("dp", "span", None, None, None, "mp"),
            P(("span", "dp"), "mp"),
            P("mp", ("span", "dp")),
        ),
        check_vma=False,
    )
```

```python
import math

import jax
import jax.numpy as jnp
import numpy as np
from jax import lax
from jax.experimental import pallas as pl
from jax.experimental.pallas import tpu as pltpu
from jax.sharding import PartitionSpec as P

HD = 128
DE = 896
EHD = 64
R = 128
CH = 64
NB = 2
ROOM = 48


def lists(ids_m, span_index, vocab_rows, n_span):
    tokens = ids_m.shape[1]
    t = jnp.arange(tokens, dtype=jnp.int32)
    same = ids_m[:, :, None] == ids_m[:, None, :]
    dup = jnp.any(same & (t[None, None, :] < t[None, :, None]), axis=2)
    uniq = jnp.logical_not(dup)
    src = ids_m // vocab_rows
    shards = jnp.arange(n_span, dtype=jnp.int32)
    counts = jnp.sum(
        (uniq[:, None, :] & (src[:, None, :] == shards[None, :, None])).astype(jnp.int32), axis=2
    )
    over = jnp.max(counts) > ROOM
    sel = uniq & (src == span_index)
    tri = (t[:, None] < t[None, :]).astype(jnp.bfloat16)
    rank = jnp.dot(sel.astype(jnp.bfloat16), tri, preferred_element_type=jnp.float32).astype(
        jnp.int32
    )
    room = jnp.arange(ROOM, dtype=jnp.int32)
    local = ids_m - span_index * vocab_rows
    rows = jnp.sum(
        jnp.where(
            (rank[:, None, :] == room[None, :, None]) & sel[:, None, :], local[:, None, :], 0
        ),
        axis=2,
    )
    own = lax.dynamic_index_in_dim(ids_m, span_index, 0, keepdims=False)
    own_src = own // vocab_rows
    own_same = own[:, None] == own[None, :]
    first = jnp.min(jnp.where(own_same, t[None, :], tokens), axis=1)
    own_uniq = first == t
    own_rank = jnp.sum(
        (
            own_uniq[None, :]
            & (own_src[:, None] == own_src[None, :])
            & (t[None, :] < first[:, None])
        ).astype(jnp.int32),
        axis=1,
    )
    return rows, own_src * ROOM + own_rank, over


F32 = jnp.float32
BF16 = jnp.bfloat16
PAIR = 2 * EHD
HEADS_ENC = DE // EHD
PAIRS = HEADS_ENC // 2
TOK = 512
SPANS = 2
DEC = 2048
HALF = DE // 2
PADDED = 1024
PIECE = 14
TILES = ((0, 256), (256, 256), (512, 256), (768, 128))


def dot(a, b):
    return jnp.dot(a, b, preferred_element_type=F32)


def dot_nt(a, b):
    return lax.dot_general(a, b, (((1,), (1,)), ((), ())), preferred_element_type=F32)


def dot_tn(a, b):
    return lax.dot_general(a, b, (((0,), (0,)), ((), ())), preferred_element_type=F32)


def piece_rows():
    rows = np.full((2, PADDED), -1, np.int32)
    n = 0
    for core in range(2):
        for first in range(4):
            for second in range(4):
                for low in range(2):
                    for r in range(16):
                        if r < PIECE:
                            rows[0, n] = (((first * 4 + second) * 2 + low) * 2 + core) * PIECE + r
                            rows[1, n] = (((second * 4 + first) * 2 + low) * 2 + core) * PIECE + r
                        n += 1
    return rows


def pair_blocks(kv_ref, c, j, low, high):
    rows = slice(c * CH, (c + 1) * CH)
    k = kv_ref[rows, pl.ds(pl.multiple_of(j * PAIR, PAIR), PAIR)]
    v = kv_ref[rows, pl.ds(pl.multiple_of(DE + j * PAIR, PAIR), PAIR)]
    return (
        jnp.concatenate([k * low, k * high], axis=0),
        jnp.concatenate([v * low, v * high], axis=0),
    )


def mega(
    slot_ref,
    rows_ref,
    pos_ref,
    alt_ref,
    list_ref,
    table_ref,
    states_ref,
    wspan_ref,
    q_ref,
    og_ref,
    wq_own_ref,
    wo_own_ref,
    wd_ref,
    wqo_ref,
    att_out,
    cross_out,
    rq_ref,
    ro_ref,
    picked_ref,
    sent_ref,
    got_ref,
    emb_ref,
    kvp_ref,
    kvg_ref,
    kv_ref,
    qo_ref,
    ogo_ref,
    wb_ref,
    sb_ref,
    wq_ref,
    wo_ref,
    eq_ref,
    att_ref,
    probs_ref,
    enc_ref,
    dkv_ref,
    gkv_ref,
    sum_ref,
    pad_ref,
    pad_emb_ref,
    cross_ref,
    all_ref,
    slots_ref,
    g_ref,
    core_ref,
    acc1_ref,
    first_ref,
    acc2_ref,
    second_ref,
    acc3_ref,
    last_ref,
    emb_sems,
    swap_sems,
    weight_sems,
    slot_sems,
    sum_sems,
    local_sems,
):
    span, dp, half = lax.axis_index("span"), lax.axis_index("dp"), lax.axis_index("mp")
    z, y, x_low, core = span // 4, span % 4, dp // 2, dp % 2
    partner = {"span": span, "dp": dp, "mp": 1 - half}
    peer = {"span": span, "dp": x_low * 2 + 1 - core, "mp": half}
    where = (z, y)

    offsets = ((0, 1), (1, 0), (0, 3), (3, 0), (2, 1), (1, 2), (2, 3), (3, 2), (1, 1), (3, 3), (1, 3), (3, 1), (2, 0), (0, 2), (2, 2))

    def span_at(k):
        return lax.rem(z + offsets[k][0], 4) * 4 + lax.rem(y + offsets[k][1], 4)

    def in_span(k):
        return {"span": span_at(k), "dp": dp, "mp": half}

    def along(axis, by):
        if axis == 0:
            return {"span": lax.rem(z + by + 4, 4) * 4 + y, "dp": dp, "mp": half}
        return {"span": z * 4 + lax.rem(y + by + 4, 4), "dp": dp, "mp": half}

    others = [
        {"span": span, "dp": (1 - x_low) * 2 + core, "mp": half},
        partner,
        {"span": span, "dp": (1 - x_low) * 2 + core, "mp": 1 - half},
    ]
    def area(i):
        return (dkv_ref, gkv_ref)[i // 4].at[(i // 2) % 2, :, pl.ds((i % 2) * 1024, DE)]

    vocab = table_ref.shape[0]
    sizes = [min(512, vocab - at) for at in range(0, vocab, 512)]
    table_in = [
        pltpu.make_async_copy(
            table_ref.at[pl.ds(i * 512, size)], area(i).at[pl.ds(0, size)], local_sems.at[5 + i]
        )
        for i, size in enumerate(sizes)
    ]
    spans_in = [
        pltpu.make_async_copy(
            wspan_ref.at[pl.ds(i * 512, 512)],
            (dkv_ref, gkv_ref)[i // 2].at[i % 2, :, pl.ds(0, 2 * DE)],
            local_sems.at[i],
        )
        for i in range(4)
    ]
    alt_in = pltpu.make_async_copy(alt_ref, eq_ref, local_sems.at[4])
    for copy in table_in:
        copy.start()
    alt_in.start()

    barrier = pltpu.get_barrier_semaphore()
    friends = [in_span(k) for k in range(15)] + [peer] + others
    for friend in friends:
        pl.semaphore_signal(barrier, inc=1, device_id=friend, device_id_type=pl.DeviceIdType.MESH)
    pl.semaphore_wait(barrier, len(friends))

    def send(src, dst, sems, device):
        copy = pltpu.make_async_remote_copy(
            src_ref=src,
            dst_ref=dst,
            send_sem=sems.at[0],
            recv_sem=sems.at[1],
            device_id=device,
            device_id_type=pl.DeviceIdType.MESH,
        )
        copy.start()
        return copy

    def add(*parts):
        total = parts[0].astype(F32)
        for part in parts[1:]:
            total = total + part.astype(F32)
        return total

    def mod(v):
        return lax.rem(v + 4, 4)

    ranks = ((z, y), (y, z))

    def at(kind, r, group, piece, count):
        n = core * 2 + r
        if kind:
            return wb_ref.at[
                pl.ds(pl.multiple_of(n * 224, 224), 224),
                pl.ds(pl.multiple_of(group * 512 + piece * 128, 128), count * 128),
            ]
        return sb_ref.at[pl.ds(group * 4 + piece, count), pl.ds(pl.multiple_of(n * 112, 112), 112)]

    def weight_steps(kind):
        sems = weight_sems.at[kind]
        copies = []
        for r in range(2):
            s = ranks[r][1]
            n = core * 2 + r
            if kind:
                src = wd_ref.at[
                    pl.ds(pl.multiple_of(n * 224, 224), 224), pl.ds(pl.multiple_of(s * 512, 512), 512)
                ]
            else:
                src = wqo_ref.at[r]
            copies.append([send(src, at(kind, r, s, 0, 4), sems.at[r, 0], others[2])])
        yield
        for r in range(2):
            s = ranks[r][1]
            for copy in copies[r]:
                copy.wait()
            whole = at(kind, r, s, 0, 4)
            copies[r] = [
                send(whole, whole, sems.at[r, 1 + i], along(1 - r, by)) for i, by in enumerate((1, -1))
            ]
        yield
        for r in range(2):
            s = ranks[r][1]
            for copy in copies[r]:
                copy.wait()
            copies[r] = []
            for i, by in enumerate((1, -1)):
                part = at(kind, r, mod(s - by), 2 * i, 2)
                copies[r].append(send(part, part, sems.at[r, 3 + i], along(1 - r, by)))
        yield
        for r in range(2):
            for copy in copies[r]:
                copy.wait()
            n = core * 2 + r
            if kind:
                mine = wb_ref.at[pl.ds(pl.multiple_of(n * 224, 224), 224)]
            else:
                mine = sb_ref.at[:, pl.ds(pl.multiple_of(n * 112, 112), 112)]
            copies[r] = [send(mine, mine, sems.at[r, 5], peer)]
        yield
        for r in range(2):
            for copy in copies[r]:
                copy.wait()
        yield

    small_steps, wide_steps = weight_steps(0), weight_steps(1)
    next(small_steps)
    next(wide_steps)
    q_swap = send(q_ref.at[1 - half], qo_ref, swap_sems.at[1], partner)
    og_swap = send(og_ref.at[1 - half], ogo_ref, swap_sems.at[2], partner)

    rank = lax.broadcasted_iota(jnp.int32, (1, 512), 1)
    for i, size in enumerate(sizes):
        table_in[i].wait()
        chosen = (list_ref[...] == rank + i * 512).astype(F32).astype(BF16)
        part = dot(chosen[:, :size], area(i)[:size, :])
        if i == 0:
            sum_ref[...], picked_ref[...] = part[:TOK], part[TOK:]
        else:
            sum_ref[...] += part[:TOK]
            picked_ref[...] += part[TOK:]
        if i == 4:
            next(small_steps)
    picked = jnp.concatenate([sum_ref[...], picked_ref[...]], axis=0)
    sent_ref[...] = picked.astype(BF16).reshape(16, ROOM, DE)
    for copy in spans_in:
        copy.start()
    embs = [
        send(sent_ref.at[span_at(k)], got_ref.at[span], emb_sems.at[k], in_span(k))
        for k in range(15)
    ]
    got_ref[span] = sent_ref[span]
    next(small_steps)

    for copy in spans_in:
        copy.wait()

    def project_span(i, _):
        cols = pl.ds(pl.multiple_of(i * 256, 256), 256)
        total = jnp.zeros((2 * SPANS * CH, 256), F32)
        for n in range(4):
            total += dot(states_ref[:, n * 512 : (n + 1) * 512], (dkv_ref, gkv_ref)[n // 2][n % 2, :, cols])
        total = total.astype(BF16)
        kvp_ref[0, :, cols] = total[: SPANS * CH]
        kvp_ref[1, :, cols] = total[SPANS * CH :]
        return 0

    lax.fori_loop(0, 2 * DE // 256, project_span, 0)
    kv_swap = send(kvp_ref.at[1 - half], kvg_ref, swap_sems.at[0], partner)

    next(small_steps)
    next(small_steps)

    place = lax.broadcasted_iota(jnp.int32, (HALF, 256), 0)
    wide = lax.broadcasted_iota(jnp.int32, (512, 256), 0)
    wide = jnp.where(wide < 384, wide, jnp.where(wide >= 448, wide - 64, -DE))
    col = lax.broadcasted_iota(jnp.int32, (HALF, 256), 1)
    wide_col = lax.broadcasted_iota(jnp.int32, (512, 256), 1)
    for lane_at, size in TILES:
        mine = (place + half * HALF == col + lane_at).astype(F32).astype(BF16)[:, :size]
        his = (wide + (1 - half) * HALF == wide_col + lane_at).astype(F32).astype(BF16)[:, :size]
        for up in range(2):
            rows = slice(up * HALF, (up + 1) * HALF)
            other = jnp.concatenate([sb_ref[up * 4 + i] for i in range(4)], axis=1)
            wq_ref[rows, lane_at : lane_at + size] = (dot(wq_own_ref[rows, :], mine) + dot(other, his)).astype(BF16)
    wo_ref[pl.ds(pl.multiple_of(half * HALF, HALF), HALF), :] = wo_own_ref[...]
    for i in range(7):
        wo_ref[pl.ds(pl.multiple_of((1 - half) * HALF, HALF), HALF), i * 128 : (i + 1) * 128] = sb_ref[8 + i if i < 4 else 9 + i]

    for copy in embs:
        copy.wait()
    next(wide_steps)
    alt_in.wait()
    slot_of = lax.broadcasted_iota(jnp.int32, (1, 16 * ROOM), 1)
    pick = (pos_ref[...] == slot_of).astype(F32).astype(BF16)
    over = slot_ref[2, 0] > 0
    for lane_at, size in TILES:
        cols = slice(lane_at, lane_at + size)
        rows = jnp.concatenate([got_ref[i, :, cols] for i in range(16)], axis=0)
        emb_ref[:, cols] = jnp.where(over, eq_ref[:, cols].astype(F32), dot(pick, rows)).astype(BF16)

    lane = lax.broadcasted_iota(jnp.int32, (1, PAIR), 1)
    is_low = lane < EHD
    low = is_low.astype(F32).astype(BF16)
    high = (lane >= EHD).astype(F32).astype(BF16)

    def pad(to_ref, ref, order):
        for lane_at in range(0, PADDED, 256):
            spread = (
                lax.broadcasted_iota(jnp.int32, (DE, 256), 0)
                == rows_ref[order : order + 1, lane_at : lane_at + 256]
            )
            to_ref[:, lane_at : lane_at + 256] = dot(ref[...], spread.astype(F32).astype(BF16)).astype(BF16)

    for lane_at, size in TILES:
        cols = slice(lane_at, lane_at + size)
        eq_ref[:, cols] = dot(emb_ref[...], wq_ref[:, cols]).astype(BF16)
    next(wide_steps)

    def forward(j, _):
        cols = pl.ds(pl.multiple_of(j * PAIR, PAIR), PAIR)
        for c in range(SPANS):
            rows = slice(c * NB * R, (c + 1) * NB * R)
            kbd, vbd = pair_blocks(kv_ref, c, j, low, high)
            s = dot_nt(eq_ref[rows, cols], kbd) * (1.0 / math.sqrt(EHD))
            top0 = jnp.max(jnp.where(is_low, s, -jnp.inf), axis=1, keepdims=True)
            top1 = jnp.max(jnp.where(is_low, -jnp.inf, s), axis=1, keepdims=True)
            p = jnp.exp(s - jnp.where(is_low, top0, top1))
            sum0 = jnp.sum(jnp.where(is_low, p, 0.0), axis=1, keepdims=True)
            sum1 = jnp.sum(jnp.where(is_low, 0.0, p), axis=1, keepdims=True)
            p = p * jnp.where(is_low, 1.0 / sum0, 1.0 / sum1)
            probs_ref[c, j] = p
            att_ref[rows, cols] = dot(p.astype(BF16), vbd).astype(BF16)
        return 0

    kv_swap.wait()
    kv_ref[...] = add(kvp_ref[half], kvg_ref[...]).astype(BF16)
    lax.fori_loop(0, PAIRS, forward, 0)
    next(wide_steps)

    feature = lax.broadcasted_iota(jnp.int32, (DE, HALF), 0)
    column = lax.broadcasted_iota(jnp.int32, (DE, HALF), 1)

    def half_of(which):
        chosen = (feature == column + which * HALF).astype(F32).astype(BF16)
        return dot(att_ref[...], chosen).astype(BF16)

    slots_ref[0:4] = half_of(1 - half).reshape(4, R, HALF)
    att_swap = send(slots_ref.at[pl.ds(0, 4)], all_ref.at[half], swap_sems.at[3], partner)
    all_ref[half] = half_of(half).reshape(4, R, HALF)

    for lane_at, size in TILES:
        cols = slice(lane_at, lane_at + size)
        enc_ref[:, cols] = (emb_ref[:, cols].astype(F32) + dot(att_ref[...], wo_ref[:, cols])).astype(BF16)

    def project_own(i, _):
        cols = pl.ds(pl.multiple_of(i * 256, 256), 256)
        dkv_ref[0, :, cols] = dot(enc_ref[...], wd_ref[:, cols]).astype(BF16)
        return 0

    def project_other(i, _):
        cols = pl.ds(pl.multiple_of(i * 256, 256), 256)
        dkv_ref[1, :, cols] = dot(enc_ref[...], wb_ref[:, cols]).astype(BF16)
        return 0

    lax.fori_loop(0, DEC // 256, project_own, 0)
    pad(pad_emb_ref, emb_ref, 0)
    next(wide_steps)
    lax.fori_loop(0, DEC // 256, project_other, 0)

    att_swap.wait()
    for e in range(16):
        unit, there = slot_ref[0, e], slot_ref[1, e]
        slots_ref[e] = all_ref[unit // 4, unit % 4] * there.astype(F32).astype(BF16)
    waiting = [
        send(slots_ref.at[span_at(k)], att_out.at[span], slot_sems.at[k], in_span(k))
        for k in range(15)
    ]
    stay = pltpu.make_async_copy(slots_ref.at[span], att_out.at[span], local_sems.at[0])
    stay.start()
    q_swap.wait()
    og_swap.wait()
    scale = 1.0 / math.sqrt(HD)

    def decode(h, _):
        kcols = pl.ds(pl.multiple_of(h * HD, HD), HD)
        vcols = pl.ds(pl.multiple_of(DEC // 2 + h * HD, HD), HD)
        for g in range(2):
            for c in range(SPANS):
                few = slice(c * CH, (c + 1) * CH)
                rows = slice(c * NB * R, (c + 1) * NB * R)
                q = q_ref[half, few, kcols] if g == 0 else qo_ref[few, kcols]
                og = og_ref[half, few, kcols] if g == 0 else ogo_ref[few, kcols]
                k, v = dkv_ref[g, rows, kcols], dkv_ref[g, rows, vcols]
                s = dot_nt(q, k) * scale
                p = jnp.exp(s - jnp.max(s, axis=1, keepdims=True))
                p = p * (1.0 / jnp.sum(p, axis=1, keepdims=True))
                pb = p.astype(BF16)
                cross = dot(pb, v).astype(BF16)
                cross_ref[g, few, kcols] = cross
                gkv_ref[g, rows, vcols] = dot_tn(pb, og).astype(BF16)
                row = jnp.sum(og.astype(F32) * cross.astype(F32), axis=1, keepdims=True)
                ds = (p * (dot_nt(og, v) - row) * scale).astype(BF16)
                gkv_ref[g, rows, kcols] = dot_tn(ds, q).astype(BF16)
        return 0

    lax.fori_loop(0, 8, decode, 0)
    waiting.append(send(cross_ref.at[1], cross_out.at[half], swap_sems.at[4], partner))
    mine = pltpu.make_async_copy(cross_ref.at[0], cross_out.at[half], local_sems.at[1])
    mine.start()
    sum_ref[...] = jnp.zeros_like(sum_ref)

    def collect(i, _):
        cols = pl.ds(pl.multiple_of(i * 256, 256), 256)
        sum_ref[...] += dot_nt(gkv_ref[0, :, cols], wd_ref[:, cols]) + dot_nt(
            gkv_ref[1, :, cols], wb_ref[:, cols]
        )
        return 0

    lax.fori_loop(0, DEC // 256, collect, 0)
    enc_ref[...] = sum_ref[...].astype(BF16)

    def steps(job):
        k, lanes = ((0, slice(0, 512)), (0, slice(512, DE)), (1, slice(0, DE)))[job]
        wide = pl.ds(lanes.start, lanes.stop - lanes.start)
        axis = (0, 1, 1)[job]
        flip = job == 1
        p, q = where[axis], where[1 - axis]
        sems = sum_sems.at[job]
        copies = [
            send(g_ref.at[k, 1 - core, :, :, :, :, wide], core_ref.at[k, :, :, :, :, wide], sems.at[0], peer)
        ]
        yield
        copies[0].wait()
        for i in range(4):
            acc1_ref[k, i, :, :, :, lanes] = add(
                g_ref[k, core, i, :, :, :, lanes], core_ref[k, i, :, :, :, lanes]
            ).astype(BF16)
        copies = []
        for j in range(1, 4):
            to = mod(p + j)
            block = acc1_ref.at[k, :, to, :, :, wide] if flip else acc1_ref.at[k, to, :, :, :, wide]
            copies.append(send(block, first_ref.at[k, j - 1, :, :, :, wide], sems.at[j], along(axis, j)))
        yield
        for copy in copies:
            copy.wait()
        own = acc1_ref[k, :, p, :, :, lanes] if flip else acc1_ref[k, p, :, :, :, lanes]
        acc2_ref[k, :, :, :, lanes] = add(own, *[first_ref[k, j, :, :, :, lanes] for j in range(3)]).astype(BF16)
        copies = [
            send(
                acc2_ref.at[k, mod(q + j), :, :, wide],
                second_ref.at[k, j - 1, :, :, wide],
                sems.at[3 + j],
                along(1 - axis, j),
            )
            for j in range(1, 4)
        ]
        yield
        for copy in copies:
            copy.wait()
        acc3_ref[k, :, :, lanes] = add(
            acc2_ref[k, q, :, :, lanes], *[second_ref[k, j, :, :, lanes] for j in range(3)]
        ).astype(BF16)
        copies = []
        for n, other in enumerate(others):
            to_low = x_low if n == 1 else 1 - x_low
            copies.append(
                send(acc3_ref.at[k, to_low, :, wide], last_ref.at[k, n, :, wide], sems.at[7 + n], other)
            )
        yield
        for copy in copies:
            copy.wait()
        (rq_ref, ro_ref)[k][:, lanes] = add(
            acc3_ref[k, x_low, :, lanes], *[last_ref[k, n, :, lanes] for n in range(3)]
        )
        yield

    def outer(k, padded_ref, ref, lanes):
        def tile(i, _):
            cols = pl.ds(pl.multiple_of(i * 256, 256), 256)
            g_ref[k, i // 2, pl.ds((i % 2) * 2, 2), :, :, :, lanes] = (
                dot_tn(padded_ref[:, cols], ref[:, lanes]).astype(BF16).reshape(2, 4, 2, 16, -1)
            )
            return 0

        lax.fori_loop(0, PADDED // 256, tile, 0)

    pad(pad_ref, enc_ref, 1)
    outer(1, pad_ref, att_ref, slice(0, DE))
    out_sum = steps(2)
    next(out_sum)
    for lane_at, size in TILES:
        cols = slice(lane_at, lane_at + size)
        eq_ref[:, cols] = dot_nt(enc_ref[...], wo_ref[cols, :]).astype(BF16)
    next(out_sum)

    def backward(j, _):
        cols = pl.ds(pl.multiple_of(j * PAIR, PAIR), PAIR)
        for c in range(SPANS):
            rows = slice(c * NB * R, (c + 1) * NB * R)
            kbd, vbd = pair_blocks(kv_ref, c, j, low, high)
            ga = eq_ref[rows, cols]
            prod = ga.astype(F32) * att_ref[rows, cols].astype(F32)
            row0 = jnp.sum(jnp.where(is_low, prod, 0.0), axis=1, keepdims=True)
            row1 = jnp.sum(jnp.where(is_low, 0.0, prod), axis=1, keepdims=True)
            diff = dot_nt(ga, vbd) - jnp.where(is_low, row0, row1)
            ds = (probs_ref[c, j] * diff * (1.0 / math.sqrt(EHD))).astype(BF16)
            eq_ref[rows, cols] = dot(ds, kbd).astype(BF16)
        return 0

    lax.fori_loop(0, 4, backward, 0)
    outer(0, pad_emb_ref, eq_ref, slice(0, 512))
    low_sum = steps(0)
    next(low_sum)
    lax.fori_loop(4, PAIRS, backward, 0)
    next(low_sum)
    next(out_sum)
    outer(0, pad_emb_ref, eq_ref, slice(512, DE))
    high_sum = steps(1)
    next(high_sum)
    next(high_sum)
    next(low_sum)
    next(out_sum)
    next(high_sum)
    next(low_sum)
    next(out_sum)
    next(high_sum)
    next(low_sum)
    next(high_sum)
    for copy in waiting:
        copy.wait()
    mine.wait()
    stay.wait()


def run(slot, pos, alt, rows, table, states, w_span, q, og, w_q, w_o, w_d, wqo):
    vmem = pl.BlockSpec(memory_space=pltpu.VMEM)
    anywhere = pl.BlockSpec(memory_space=pl.ANY)
    dma = pltpu.SemaphoreType.DMA
    return pl.pallas_call(
        mega,
        out_shape=(
            jax.ShapeDtypeStruct((16, R, HALF), BF16),
            jax.ShapeDtypeStruct((2, SPANS * CH, DEC // 2), BF16),
            jax.ShapeDtypeStruct((16, DE), F32),
            jax.ShapeDtypeStruct((16, DE), F32),
        ),
        in_specs=[pl.BlockSpec(memory_space=pltpu.SMEM), vmem, vmem, anywhere, vmem, anywhere, vmem, anywhere]
        + [vmem] * 6,
        out_specs=(anywhere, anywhere, vmem, vmem),
        scratch_shapes=[
            pltpu.VMEM((16 * ROOM - TOK, DE), F32),
            pltpu.VMEM((16, ROOM, DE), BF16),
            pltpu.VMEM((16, ROOM, DE), BF16),
            pltpu.VMEM((TOK, DE), BF16),
            pltpu.VMEM((2, SPANS * CH, 2 * DE), BF16),
            pltpu.VMEM((SPANS * CH, 2 * DE), BF16),
            pltpu.VMEM((SPANS * CH, 2 * DE), BF16),
            pltpu.VMEM((SPANS * CH, DEC // 2), BF16),
            pltpu.VMEM((SPANS * CH, DEC // 2), BF16),
            pltpu.VMEM((DE, DEC), BF16),
            pltpu.VMEM((16, HALF, 128), BF16),
            pltpu.VMEM((DE, DE), BF16),
            pltpu.VMEM((DE, DE), BF16),
            pltpu.VMEM((TOK, DE), BF16),
            pltpu.VMEM((TOK, DE), BF16),
            pltpu.VMEM((SPANS, PAIRS, NB * R, PAIR), F32),
            pltpu.VMEM((TOK, DE), BF16),
            pltpu.VMEM((2, TOK, DEC), BF16),
            pltpu.VMEM((2, TOK, DEC), BF16),
            pltpu.VMEM((TOK, DE), F32),
            pltpu.VMEM((TOK, PADDED), BF16),
            pltpu.VMEM((TOK, PADDED), BF16),
            pltpu.VMEM((2, SPANS * CH, DEC // 2), BF16),
            pltpu.VMEM((2, 4, R, HALF), BF16),
            pltpu.VMEM((16, R, HALF), BF16),
            pltpu.VMEM((2, 2, 4, 4, 2, 16, DE), BF16),
            pltpu.VMEM((2, 4, 4, 2, 16, DE), BF16),
            pltpu.VMEM((2, 4, 4, 2, 16, DE), BF16),
            pltpu.VMEM((2, 3, 4, 2, 16, DE), BF16),
            pltpu.VMEM((2, 4, 2, 16, DE), BF16),
            pltpu.VMEM((2, 3, 2, 16, DE), BF16),
            pltpu.VMEM((2, 2, 16, DE), BF16),
            pltpu.VMEM((2, 3, 16, DE), BF16),
            dma((15, 2)),
            dma((5, 2)),
            dma((2, 2, 6, 2)),
            dma((15, 2)),
            dma((3, 10, 2)),
            dma((13,)),
        ],
        compiler_params=pltpu.CompilerParams(
            vmem_limit_bytes=63 * 2**20, collective_id=1, has_side_effects=True
        ),
        cost_estimate=pl.CostEstimate(
            flops=16 * 10**9, bytes_accessed=30 * 2**20, transcendentals=10**6
        ),
    )(slot, jnp.asarray(piece_rows()), pos, alt, rows, table, states, w_span, q, og, w_q, w_o, w_d, wqo)


def body(
    span_states,
    queries,
    out_grad,
    neighbour_ids,
    assignment,
    embed_table,
    w_span_kv,
    w_query_enc,
    w_out_enc,
    w_dec_kv,
):
    bf16 = jnp.bfloat16
    n_span = lax.axis_size("span")
    span_index = lax.axis_index("span")
    half_index = lax.axis_index("mp")
    seq_count, local_tokens, half_width = span_states.shape
    spans = local_tokens // CH
    units = spans * NB
    dec_cols = 2 * queries.shape[2]
    vocab_rows = embed_table.shape[0]
    tokens = units * R

    ids_m = lax.dynamic_index_in_dim(
        neighbour_ids.reshape(seq_count, n_span, tokens), half_index, 0, keepdims=False
    )
    rows, pos, over = lists(ids_m, span_index, vocab_rows, n_span)

    def whole_gather():
        shifted = ids_m.reshape(-1) - span_index * vocab_rows
        inside = (shifted >= 0) & (shifted < vocab_rows)
        found = jnp.take(embed_table, jnp.clip(shifted, 0, vocab_rows - 1), axis=0)
        found = jnp.where(inside[:, None], found, jnp.zeros_like(found))
        found = lax.all_to_all(
            found.reshape(n_span, tokens, DE), "span", split_axis=0, concat_axis=0, tiled=True
        )
        return jnp.sum(found.astype(F32), axis=0).astype(bf16)

    alt = lax.cond(over, whole_gather, lambda: jnp.zeros((tokens, DE), bf16))

    core = lax.axis_index("dp") % 2
    wqo = []
    for r in range(2):
        group = span_index % 4 if r == 0 else span_index // 4
        start = (core * 2 + r) * 112
        from_q = lax.dynamic_slice(w_query_enc, (group * HALF + start, 0), (112, HALF))
        from_o = lax.dynamic_slice(w_out_enc, (start, (group - 2) * 512), (112, 512))
        from_q = jnp.concatenate([from_q[:, :384], from_q[:, HALF - 128 :]], axis=1)
        wqo.append(jnp.where(group < 2, from_q, from_o))
    wqo = jnp.transpose(jnp.stack(wqo).reshape(2, 112, 4, 128), (0, 2, 1, 3))

    dest = lax.dynamic_index_in_dim(assignment[0, :, :, 0], span_index, 0, keepdims=False)
    at = dest[None, :] == jnp.arange(n_span, dtype=jnp.int32)[:, None]
    numbers = jnp.arange(seq_count * units, dtype=jnp.int32)
    slot = jnp.stack(
        [
            jnp.sum(jnp.where(at, numbers[None, :], 0), axis=1),
            jnp.sum(at.astype(jnp.int32), axis=1),
            jnp.full((n_span,), over.astype(jnp.int32)),
        ]
    )
    attended_out, cross_out, rq, ro = run(
        slot,
        pos[:, None],
        alt,
        rows.reshape(-1, 1),
        embed_table,
        span_states.reshape(-1, half_width),
        w_span_kv,
        queries,
        out_grad,
        w_query_enc,
        w_out_enc,
        w_dec_kv.reshape(DE, dec_cols),
        wqo,
    )
    grad_query_enc = lax.dynamic_slice_in_dim(rq[:PIECE], half_index * HALF, HALF, 1)
    grad_out_enc = lax.dynamic_slice_in_dim(ro[:PIECE], half_index * HALF, HALF, 1).T
    return (
        cross_out,
        attended_out.reshape(1, 1, n_span, 1, R, HALF),
        grad_query_enc,
        grad_out_enc,
    )


def solution(mesh):
    return jax.shard_map(
        body,
        mesh=mesh,
        in_specs=(
            P("dp", "span", "mp"),
            P("dp", "span", "mp"),
            P("dp", "span", "mp"),
            P("dp", None, None, None),
            P("dp", None, None, None),
            P("span", None),
            P("mp", None),
            P(None, "mp"),
            P("mp", None),
            P(None, None, "mp"),
        ),
        out_specs=(
            P("dp", "span", "mp"),
            P("dp", "span", None, None, None, "mp"),
            P(("span", "dp"), "mp"),
            P("mp", ("span", "dp")),
        ),
        check_vma=False,
    )
```

```python
import math

import jax
import jax.numpy as jnp
import numpy as np
from jax import lax
from jax.experimental import pallas as pl
from jax.experimental.pallas import tpu as pltpu
from jax.sharding import PartitionSpec as P

HD = 128
DE = 896
EHD = 64
R = 128
CH = 64
NB = 2
ROOM = 48


def lists(ids_m, span_index, vocab_rows, n_span):
    tokens = ids_m.shape[1]
    t = jnp.arange(tokens, dtype=jnp.int32)
    same = ids_m[:, :, None] == ids_m[:, None, :]
    dup = jnp.any(same & (t[None, None, :] < t[None, :, None]), axis=2)
    uniq = jnp.logical_not(dup)
    src = ids_m // vocab_rows
    shards = jnp.arange(n_span, dtype=jnp.int32)
    counts = jnp.sum(
        (uniq[:, None, :] & (src[:, None, :] == shards[None, :, None])).astype(jnp.int32), axis=2
    )
    over = jnp.max(counts) > ROOM
    sel = uniq & (src == span_index)
    tri = (t[:, None] < t[None, :]).astype(jnp.bfloat16)
    rank = jnp.dot(sel.astype(jnp.bfloat16), tri, preferred_element_type=jnp.float32).astype(
        jnp.int32
    )
    room = jnp.arange(ROOM, dtype=jnp.int32)
    local = ids_m - span_index * vocab_rows
    rows = jnp.sum(
        jnp.where(
            (rank[:, None, :] == room[None, :, None]) & sel[:, None, :], local[:, None, :], 0
        ),
        axis=2,
    )
    own = lax.dynamic_index_in_dim(ids_m, span_index, 0, keepdims=False)
    own_src = own // vocab_rows
    own_same = own[:, None] == own[None, :]
    first = jnp.min(jnp.where(own_same, t[None, :], tokens), axis=1)
    own_uniq = first == t
    own_rank = jnp.sum(
        (
            own_uniq[None, :]
            & (own_src[:, None] == own_src[None, :])
            & (t[None, :] < first[:, None])
        ).astype(jnp.int32),
        axis=1,
    )
    return rows, own_src * ROOM + own_rank, over


F32 = jnp.float32
BF16 = jnp.bfloat16
PAIR = 2 * EHD
HEADS_ENC = DE // EHD
PAIRS = HEADS_ENC // 2
TOK = 512
SPANS = 2
DEC = 2048
HALF = DE // 2
PADDED = 1024
PIECE = 14
TILES = ((0, 256), (256, 256), (512, 256), (768, 128))


def dot(a, b):
    return jnp.dot(a, b, preferred_element_type=F32)


def dot_nt(a, b):
    return lax.dot_general(a, b, (((1,), (1,)), ((), ())), preferred_element_type=F32)


def dot_tn(a, b):
    return lax.dot_general(a, b, (((0,), (0,)), ((), ())), preferred_element_type=F32)


def piece_rows():
    rows = np.full((2, PADDED), -1, np.int32)
    n = 0
    for core in range(2):
        for first in range(4):
            for second in range(4):
                for low in range(2):
                    for r in range(16):
                        if r < PIECE:
                            rows[0, n] = (((first * 4 + second) * 2 + low) * 2 + core) * PIECE + r
                            rows[1, n] = (((second * 4 + first) * 2 + low) * 2 + core) * PIECE + r
                        n += 1
    return rows


def pair_blocks(kv_ref, c, j, low, high):
    rows = slice(c * CH, (c + 1) * CH)
    k = kv_ref[rows, pl.ds(pl.multiple_of(j * PAIR, PAIR), PAIR)]
    v = kv_ref[rows, pl.ds(pl.multiple_of(DE + j * PAIR, PAIR), PAIR)]
    return (
        jnp.concatenate([k * low, k * high], axis=0),
        jnp.concatenate([v * low, v * high], axis=0),
    )


def mega(
    slot_ref,
    rows_ref,
    pos_ref,
    alt_ref,
    list_ref,
    table_ref,
    states_ref,
    wspan_ref,
    q_ref,
    og_ref,
    wq_own_ref,
    wo_own_ref,
    wd_ref,
    wqo_ref,
    att_out,
    cross_out,
    rq_ref,
    ro_ref,
    picked_ref,
    sent_ref,
    got_ref,
    emb_ref,
    kvp_ref,
    kvg_ref,
    kv_ref,
    qo_ref,
    ogo_ref,
    wb_ref,
    sb_ref,
    wq_ref,
    wo_ref,
    eq_ref,
    att_ref,
    probs_ref,
    enc_ref,
    dkv_ref,
    gkv_ref,
    sum_ref,
    pad_ref,
    pad_emb_ref,
    cross_ref,
    all_ref,
    slots_ref,
    g_ref,
    core_ref,
    acc1_ref,
    first_ref,
    acc2_ref,
    second_ref,
    acc3_ref,
    last_ref,
    emb_sems,
    swap_sems,
    weight_sems,
    slot_sems,
    sum_sems,
    local_sems,
):
    span, dp, half = lax.axis_index("span"), lax.axis_index("dp"), lax.axis_index("mp")
    z, y, x_low, core = span // 4, span % 4, dp // 2, dp % 2
    partner = {"span": span, "dp": dp, "mp": 1 - half}
    peer = {"span": span, "dp": x_low * 2 + 1 - core, "mp": half}
    where = (z, y)

    offsets = ((0, 1), (1, 0), (0, 3), (3, 0), (2, 1), (1, 2), (2, 3), (3, 2), (1, 1), (3, 3), (1, 3), (3, 1), (2, 0), (0, 2), (2, 2))

    def span_at(k):
        return lax.rem(z + offsets[k][0], 4) * 4 + lax.rem(y + offsets[k][1], 4)

    def in_span(k):
        return {"span": span_at(k), "dp": dp, "mp": half}

    def along(axis, by):
        if axis == 0:
            return {"span": lax.rem(z + by + 4, 4) * 4 + y, "dp": dp, "mp": half}
        return {"span": z * 4 + lax.rem(y + by + 4, 4), "dp": dp, "mp": half}

    others = [
        {"span": span, "dp": (1 - x_low) * 2 + core, "mp": half},
        partner,
        {"span": span, "dp": (1 - x_low) * 2 + core, "mp": 1 - half},
    ]
    def area(i):
        return (dkv_ref, gkv_ref)[i // 4].at[(i // 2) % 2, :, pl.ds((i % 2) * 1024, DE)]

    vocab = table_ref.shape[0]
    sizes = [min(512, vocab - at) for at in range(0, vocab, 512)]
    table_in = [
        pltpu.make_async_copy(
            table_ref.at[pl.ds(i * 512, size)], area(i).at[pl.ds(0, size)], local_sems.at[5 + i]
        )
        for i, size in enumerate(sizes)
    ]
    spans_in = [
        pltpu.make_async_copy(
            wspan_ref.at[pl.ds(i * 512, 512)],
            (dkv_ref, gkv_ref)[i // 2].at[i % 2, :, pl.ds(0, 2 * DE)],
            local_sems.at[i],
        )
        for i in range(4)
    ]
    alt_in = pltpu.make_async_copy(alt_ref, eq_ref, local_sems.at[4])
    for copy in table_in:
        copy.start()
    alt_in.start()

    barrier = pltpu.get_barrier_semaphore()
    friends = [in_span(k) for k in range(15)] + [peer] + others
    for friend in friends:
        pl.semaphore_signal(barrier, inc=1, device_id=friend, device_id_type=pl.DeviceIdType.MESH)
    pl.semaphore_wait(barrier, len(friends))

    def send(src, dst, sems, device):
        copy = pltpu.make_async_remote_copy(
            src_ref=src,
            dst_ref=dst,
            send_sem=sems.at[0],
            recv_sem=sems.at[1],
            device_id=device,
            device_id_type=pl.DeviceIdType.MESH,
        )
        copy.start()
        return copy

    def add(*parts):
        total = parts[0].astype(F32)
        for part in parts[1:]:
            total = total + part.astype(F32)
        return total

    def mod(v):
        return lax.rem(v + 4, 4)

    ranks = ((z, y), (y, z))

    def at(kind, r, group, piece, count):
        n = core * 2 + r
        if kind:
            return wb_ref.at[
                pl.ds(pl.multiple_of(n * 224, 224), 224),
                pl.ds(pl.multiple_of(group * 512 + piece * 128, 128), count * 128),
            ]
        return sb_ref.at[pl.ds(group * 4 + piece, count), pl.ds(pl.multiple_of(n * 112, 112), 112)]

    def weight_steps(kind):
        sems = weight_sems.at[kind]
        copies = []
        for r in range(2):
            s = ranks[r][1]
            n = core * 2 + r
            if kind:
                src = wd_ref.at[
                    pl.ds(pl.multiple_of(n * 224, 224), 224), pl.ds(pl.multiple_of(s * 512, 512), 512)
                ]
            else:
                src = wqo_ref.at[r]
            copies.append([send(src, at(kind, r, s, 0, 4), sems.at[r, 0], others[2])])
        yield
        for r in range(2):
            s = ranks[r][1]
            for copy in copies[r]:
                copy.wait()
            whole = at(kind, r, s, 0, 4)
            copies[r] = [
                send(whole, whole, sems.at[r, 1 + i], along(1 - r, by)) for i, by in enumerate((1, -1))
            ]
        yield
        for r in range(2):
            s = ranks[r][1]
            for copy in copies[r]:
                copy.wait()
            copies[r] = []
            for i, by in enumerate((1, -1)):
                part = at(kind, r, mod(s - by), 2 * i, 2)
                copies[r].append(send(part, part, sems.at[r, 3 + i], along(1 - r, by)))
        yield
        for r in range(2):
            for copy in copies[r]:
                copy.wait()
            n = core * 2 + r
            if kind:
                mine = wb_ref.at[pl.ds(pl.multiple_of(n * 224, 224), 224)]
            else:
                mine = sb_ref.at[:, pl.ds(pl.multiple_of(n * 112, 112), 112)]
            copies[r] = [send(mine, mine, sems.at[r, 5], peer)]
        yield
        for r in range(2):
            for copy in copies[r]:
                copy.wait()
        yield

    small_steps, wide_steps = weight_steps(0), weight_steps(1)
    next(small_steps)
    next(wide_steps)

    rank = lax.broadcasted_iota(jnp.int32, (1, 512), 1)
    for i, size in enumerate(sizes):
        table_in[i].wait()
        chosen = (list_ref[...] == rank + i * 512).astype(F32).astype(BF16)
        part = dot(chosen[:, :size], area(i)[:size, :])
        if i == 0:
            sum_ref[...], picked_ref[...] = part[:TOK], part[TOK:]
        else:
            sum_ref[...] += part[:TOK]
            picked_ref[...] += part[TOK:]
        if i == 4:
            next(small_steps)
    picked = jnp.concatenate([sum_ref[...], picked_ref[...]], axis=0)
    sent_ref[...] = picked.astype(BF16).reshape(16, ROOM, DE)
    for copy in spans_in:
        copy.start()
    embs = [
        send(sent_ref.at[span_at(k)], got_ref.at[span], emb_sems.at[k], in_span(k))
        for k in range(15)
    ]
    got_ref[span] = sent_ref[span]
    next(small_steps)
    next(wide_steps)

    for copy in spans_in:
        copy.wait()

    def project_span(i, _):
        cols = pl.ds(pl.multiple_of(i * 256, 256), 256)
        total = jnp.zeros((2 * SPANS * CH, 256), F32)
        for n in range(4):
            total += dot(states_ref[:, n * 512 : (n + 1) * 512], (dkv_ref, gkv_ref)[n // 2][n % 2, :, cols])
        total = total.astype(BF16)
        kvp_ref[0, :, cols] = total[: SPANS * CH]
        kvp_ref[1, :, cols] = total[SPANS * CH :]
        return 0

    lax.fori_loop(0, 2 * DE // 256, project_span, 0)
    kv_swap = send(kvp_ref.at[1 - half], kvg_ref, swap_sems.at[0], partner)
    q_swap = send(q_ref.at[1 - half], qo_ref, swap_sems.at[1], partner)
    og_swap = send(og_ref.at[1 - half], ogo_ref, swap_sems.at[2], partner)

    next(small_steps)
    next(small_steps)

    place = lax.broadcasted_iota(jnp.int32, (HALF, 256), 0)
    wide = lax.broadcasted_iota(jnp.int32, (512, 256), 0)
    wide = jnp.where(wide < 384, wide, jnp.where(wide >= 448, wide - 64, -DE))
    col = lax.broadcasted_iota(jnp.int32, (HALF, 256), 1)
    wide_col = lax.broadcasted_iota(jnp.int32, (512, 256), 1)
    for lane_at, size in TILES:
        mine = (place + half * HALF == col + lane_at).astype(F32).astype(BF16)[:, :size]
        his = (wide + (1 - half) * HALF == wide_col + lane_at).astype(F32).astype(BF16)[:, :size]
        for up in range(2):
            rows = slice(up * HALF, (up + 1) * HALF)
            other = jnp.concatenate([sb_ref[up * 4 + i] for i in range(4)], axis=1)
            wq_ref[rows, lane_at : lane_at + size] = (dot(wq_own_ref[rows, :], mine) + dot(other, his)).astype(BF16)
    wo_ref[pl.ds(pl.multiple_of(half * HALF, HALF), HALF), :] = wo_own_ref[...]
    for i in range(7):
        wo_ref[pl.ds(pl.multiple_of((1 - half) * HALF, HALF), HALF), i * 128 : (i + 1) * 128] = sb_ref[8 + i if i < 4 else 9 + i]

    for copy in embs:
        copy.wait()
    alt_in.wait()
    slot_of = lax.broadcasted_iota(jnp.int32, (1, 16 * ROOM), 1)
    pick = (pos_ref[...] == slot_of).astype(F32).astype(BF16)
    over = slot_ref[2, 0] > 0
    for lane_at, size in TILES:
        cols = slice(lane_at, lane_at + size)
        rows = jnp.concatenate([got_ref[i, :, cols] for i in range(16)], axis=0)
        emb_ref[:, cols] = jnp.where(over, eq_ref[:, cols].astype(F32), dot(pick, rows)).astype(BF16)

    next(wide_steps)
    lane = lax.broadcasted_iota(jnp.int32, (1, PAIR), 1)
    is_low = lane < EHD
    low = is_low.astype(F32).astype(BF16)
    high = (lane >= EHD).astype(F32).astype(BF16)

    def pad(to_ref, ref, order):
        for lane_at in range(0, PADDED, 256):
            spread = (
                lax.broadcasted_iota(jnp.int32, (DE, 256), 0)
                == rows_ref[order : order + 1, lane_at : lane_at + 256]
            )
            to_ref[:, lane_at : lane_at + 256] = dot(ref[...], spread.astype(F32).astype(BF16)).astype(BF16)

    for lane_at, size in TILES:
        cols = slice(lane_at, lane_at + size)
        eq_ref[:, cols] = dot(emb_ref[...], wq_ref[:, cols]).astype(BF16)

    def forward(j, _):
        cols = pl.ds(pl.multiple_of(j * PAIR, PAIR), PAIR)
        for c in range(SPANS):
            rows = slice(c * NB * R, (c + 1) * NB * R)
            kbd, vbd = pair_blocks(kv_ref, c, j, low, high)
            s = dot_nt(eq_ref[rows, cols], kbd) * (1.0 / math.sqrt(EHD))
            top0 = jnp.max(jnp.where(is_low, s, -jnp.inf), axis=1, keepdims=True)
            top1 = jnp.max(jnp.where(is_low, -jnp.inf, s), axis=1, keepdims=True)
            p = jnp.exp(s - jnp.where(is_low, top0, top1))
            sum0 = jnp.sum(jnp.where(is_low, p, 0.0), axis=1, keepdims=True)
            sum1 = jnp.sum(jnp.where(is_low, 0.0, p), axis=1, keepdims=True)
            p = p * jnp.where(is_low, 1.0 / sum0, 1.0 / sum1)
            probs_ref[c, j] = p
            att_ref[rows, cols] = dot(p.astype(BF16), vbd).astype(BF16)
        return 0

    kv_swap.wait()
    kv_ref[...] = add(kvp_ref[half], kvg_ref[...]).astype(BF16)
    lax.fori_loop(0, PAIRS, forward, 0)
    next(wide_steps)

    feature = lax.broadcasted_iota(jnp.int32, (DE, HALF), 0)
    column = lax.broadcasted_iota(jnp.int32, (DE, HALF), 1)

    def half_of(which):
        chosen = (feature == column + which * HALF).astype(F32).astype(BF16)
        return dot(att_ref[...], chosen).astype(BF16)

    slots_ref[0:4] = half_of(1 - half).reshape(4, R, HALF)
    att_swap = send(slots_ref.at[pl.ds(0, 4)], all_ref.at[half], swap_sems.at[3], partner)
    all_ref[half] = half_of(half).reshape(4, R, HALF)

    for lane_at, size in TILES:
        cols = slice(lane_at, lane_at + size)
        enc_ref[:, cols] = (emb_ref[:, cols].astype(F32) + dot(att_ref[...], wo_ref[:, cols])).astype(BF16)

    def project_own(i, _):
        cols = pl.ds(pl.multiple_of(i * 256, 256), 256)
        dkv_ref[0, :, cols] = dot(enc_ref[...], wd_ref[:, cols]).astype(BF16)
        return 0

    def project_other(i, _):
        cols = pl.ds(pl.multiple_of(i * 256, 256), 256)
        dkv_ref[1, :, cols] = dot(enc_ref[...], wb_ref[:, cols]).astype(BF16)
        return 0

    lax.fori_loop(0, DEC // 256, project_own, 0)
    pad(pad_emb_ref, emb_ref, 0)
    next(wide_steps)
    lax.fori_loop(0, DEC // 256, project_other, 0)

    att_swap.wait()
    for e in range(16):
        unit, there = slot_ref[0, e], slot_ref[1, e]
        slots_ref[e] = all_ref[unit // 4, unit % 4] * there.astype(F32).astype(BF16)
    waiting = [
        send(slots_ref.at[span_at(k)], att_out.at[span], slot_sems.at[k], in_span(k))
        for k in range(15)
    ]
    stay = pltpu.make_async_copy(slots_ref.at[span], att_out.at[span], local_sems.at[0])
    stay.start()
    q_swap.wait()
    og_swap.wait()
    scale = 1.0 / math.sqrt(HD)

    def decode(h, _):
        kcols = pl.ds(pl.multiple_of(h * HD, HD), HD)
        vcols = pl.ds(pl.multiple_of(DEC // 2 + h * HD, HD), HD)
        for g in range(2):
            for c in range(SPANS):
                few = slice(c * CH, (c + 1) * CH)
                rows = slice(c * NB * R, (c + 1) * NB * R)
                q = q_ref[half, few, kcols] if g == 0 else qo_ref[few, kcols]
                og = og_ref[half, few, kcols] if g == 0 else ogo_ref[few, kcols]
                k, v = dkv_ref[g, rows, kcols], dkv_ref[g, rows, vcols]
                s = dot_nt(q, k) * scale
                p = jnp.exp(s - jnp.max(s, axis=1, keepdims=True))
                p = p * (1.0 / jnp.sum(p, axis=1, keepdims=True))
                pb = p.astype(BF16)
                cross = dot(pb, v).astype(BF16)
                cross_ref[g, few, kcols] = cross
                gkv_ref[g, rows, vcols] = dot_tn(pb, og).astype(BF16)
                row = jnp.sum(og.astype(F32) * cross.astype(F32), axis=1, keepdims=True)
                ds = (p * (dot_nt(og, v) - row) * scale).astype(BF16)
                gkv_ref[g, rows, kcols] = dot_tn(ds, q).astype(BF16)
        return 0

    lax.fori_loop(0, 8, decode, 0)
    waiting.append(send(cross_ref.at[1], cross_out.at[half], swap_sems.at[4], partner))
    mine = pltpu.make_async_copy(cross_ref.at[0], cross_out.at[half], local_sems.at[1])
    mine.start()
    sum_ref[...] = jnp.zeros_like(sum_ref)

    def collect(i, _):
        cols = pl.ds(pl.multiple_of(i * 256, 256), 256)
        sum_ref[...] += dot_nt(gkv_ref[0, :, cols], wd_ref[:, cols]) + dot_nt(
            gkv_ref[1, :, cols], wb_ref[:, cols]
        )
        return 0

    lax.fori_loop(0, DEC // 256, collect, 0)
    enc_ref[...] = sum_ref[...].astype(BF16)

    def steps(job):
        k, lanes = ((0, slice(0, 512)), (0, slice(512, DE)), (1, slice(0, DE)))[job]
        wide = pl.ds(lanes.start, lanes.stop - lanes.start)
        axis = (0, 1, 1)[job]
        flip = job == 1
        p, q = where[axis], where[1 - axis]
        sems = sum_sems.at[job]
        copies = [
            send(g_ref.at[k, 1 - core, :, :, :, :, wide], core_ref.at[k, :, :, :, :, wide], sems.at[0], peer)
        ]
        yield
        copies[0].wait()
        for i in range(4):
            acc1_ref[k, i, :, :, :, lanes] = add(
                g_ref[k, core, i, :, :, :, lanes], core_ref[k, i, :, :, :, lanes]
            ).astype(BF16)
        copies = []
        for j in range(1, 4):
            to = mod(p + j)
            block = acc1_ref.at[k, :, to, :, :, wide] if flip else acc1_ref.at[k, to, :, :, :, wide]
            copies.append(send(block, first_ref.at[k, j - 1, :, :, :, wide], sems.at[j], along(axis, j)))
        yield
        for copy in copies:
            copy.wait()
        own = acc1_ref[k, :, p, :, :, lanes] if flip else acc1_ref[k, p, :, :, :, lanes]
        acc2_ref[k, :, :, :, lanes] = add(own, *[first_ref[k, j, :, :, :, lanes] for j in range(3)]).astype(BF16)
        copies = [
            send(
                acc2_ref.at[k, mod(q + j), :, :, wide],
                second_ref.at[k, j - 1, :, :, wide],
                sems.at[3 + j],
                along(1 - axis, j),
            )
            for j in range(1, 4)
        ]
        yield
        for copy in copies:
            copy.wait()
        acc3_ref[k, :, :, lanes] = add(
            acc2_ref[k, q, :, :, lanes], *[second_ref[k, j, :, :, lanes] for j in range(3)]
        ).astype(BF16)
        copies = []
        for n, other in enumerate(others):
            to_low = x_low if n == 1 else 1 - x_low
            copies.append(
                send(acc3_ref.at[k, to_low, :, wide], last_ref.at[k, n, :, wide], sems.at[7 + n], other)
            )
        yield
        for copy in copies:
            copy.wait()
        (rq_ref, ro_ref)[k][:, lanes] = add(
            acc3_ref[k, x_low, :, lanes], *[last_ref[k, n, :, lanes] for n in range(3)]
        )
        yield

    def outer(k, padded_ref, ref, lanes):
        def tile(i, _):
            cols = pl.ds(pl.multiple_of(i * 256, 256), 256)
            g_ref[k, i // 2, pl.ds((i % 2) * 2, 2), :, :, :, lanes] = (
                dot_tn(padded_ref[:, cols], ref[:, lanes]).astype(BF16).reshape(2, 4, 2, 16, -1)
            )
            return 0

        lax.fori_loop(0, PADDED // 256, tile, 0)

    pad(pad_ref, enc_ref, 1)
    outer(1, pad_ref, att_ref, slice(0, DE))
    out_sum = steps(2)
    next(out_sum)
    for lane_at, size in TILES:
        cols = slice(lane_at, lane_at + size)
        eq_ref[:, cols] = dot_nt(enc_ref[...], wo_ref[cols, :]).astype(BF16)
    next(out_sum)

    def backward(j, _):
        cols = pl.ds(pl.multiple_of(j * PAIR, PAIR), PAIR)
        for c in range(SPANS):
            rows = slice(c * NB * R, (c + 1) * NB * R)
            kbd, vbd = pair_blocks(kv_ref, c, j, low, high)
            ga = eq_ref[rows, cols]
            prod = ga.astype(F32) * att_ref[rows, cols].astype(F32)
            row0 = jnp.sum(jnp.where(is_low, prod, 0.0), axis=1, keepdims=True)
            row1 = jnp.sum(jnp.where(is_low, 0.0, prod), axis=1, keepdims=True)
            diff = dot_nt(ga, vbd) - jnp.where(is_low, row0, row1)
            ds = (probs_ref[c, j] * diff * (1.0 / math.sqrt(EHD))).astype(BF16)
            eq_ref[rows, cols] = dot(ds, kbd).astype(BF16)
        return 0

    lax.fori_loop(0, 4, backward, 0)
    outer(0, pad_emb_ref, eq_ref, slice(0, 512))
    low_sum = steps(0)
    next(low_sum)
    lax.fori_loop(4, PAIRS, backward, 0)
    next(low_sum)
    next(out_sum)
    outer(0, pad_emb_ref, eq_ref, slice(512, DE))
    high_sum = steps(1)
    next(high_sum)
    next(high_sum)
    next(low_sum)
    next(out_sum)
    next(high_sum)
    next(low_sum)
    next(out_sum)
    next(high_sum)
    next(low_sum)
    next(high_sum)
    for copy in waiting:
        copy.wait()
    mine.wait()
    stay.wait()


def run(slot, pos, alt, rows, table, states, w_span, q, og, w_q, w_o, w_d, wqo):
    vmem = pl.BlockSpec(memory_space=pltpu.VMEM)
    anywhere = pl.BlockSpec(memory_space=pl.ANY)
    dma = pltpu.SemaphoreType.DMA
    return pl.pallas_call(
        mega,
        out_shape=(
            jax.ShapeDtypeStruct((16, R, HALF), BF16),
            jax.ShapeDtypeStruct((2, SPANS * CH, DEC // 2), BF16),
            jax.ShapeDtypeStruct((16, DE), F32),
            jax.ShapeDtypeStruct((16, DE), F32),
        ),
        in_specs=[pl.BlockSpec(memory_space=pltpu.SMEM), vmem, vmem, anywhere, vmem, anywhere, vmem, anywhere]
        + [vmem] * 6,
        out_specs=(anywhere, anywhere, vmem, vmem),
        scratch_shapes=[
            pltpu.VMEM((16 * ROOM - TOK, DE), F32),
            pltpu.VMEM((16, ROOM, DE), BF16),
            pltpu.VMEM((16, ROOM, DE), BF16),
            pltpu.VMEM((TOK, DE), BF16),
            pltpu.VMEM((2, SPANS * CH, 2 * DE), BF16),
            pltpu.VMEM((SPANS * CH, 2 * DE), BF16),
            pltpu.VMEM((SPANS * CH, 2 * DE), BF16),
            pltpu.VMEM((SPANS * CH, DEC // 2), BF16),
            pltpu.VMEM((SPANS * CH, DEC // 2), BF16),
            pltpu.VMEM((DE, DEC), BF16),
            pltpu.VMEM((16, HALF, 128), BF16),
            pltpu.VMEM((DE, DE), BF16),
            pltpu.VMEM((DE, DE), BF16),
            pltpu.VMEM((TOK, DE), BF16),
            pltpu.VMEM((TOK, DE), BF16),
            pltpu.VMEM((SPANS, PAIRS, NB * R, PAIR), F32),
            pltpu.VMEM((TOK, DE), BF16),
            pltpu.VMEM((2, TOK, DEC), BF16),
            pltpu.VMEM((2, TOK, DEC), BF16),
            pltpu.VMEM((TOK, DE), F32),
            pltpu.VMEM((TOK, PADDED), BF16),
            pltpu.VMEM((TOK, PADDED), BF16),
            pltpu.VMEM((2, SPANS * CH, DEC // 2), BF16),
            pltpu.VMEM((2, 4, R, HALF), BF16),
            pltpu.VMEM((16, R, HALF), BF16),
            pltpu.VMEM((2, 2, 4, 4, 2, 16, DE), BF16),
            pltpu.VMEM((2, 4, 4, 2, 16, DE), BF16),
            pltpu.VMEM((2, 4, 4, 2, 16, DE), BF16),
            pltpu.VMEM((2, 3, 4, 2, 16, DE), BF16),
            pltpu.VMEM((2, 4, 2, 16, DE), BF16),
            pltpu.VMEM((2, 3, 2, 16, DE), BF16),
            pltpu.VMEM((2, 2, 16, DE), BF16),
            pltpu.VMEM((2, 3, 16, DE), BF16),
            dma((15, 2)),
            dma((5, 2)),
            dma((2, 2, 6, 2)),
            dma((15, 2)),
            dma((3, 10, 2)),
            dma((13,)),
        ],
        compiler_params=pltpu.CompilerParams(
            vmem_limit_bytes=63 * 2**20, collective_id=1, has_side_effects=True
        ),
        cost_estimate=pl.CostEstimate(
            flops=16 * 10**9, bytes_accessed=30 * 2**20, transcendentals=10**6
        ),
    )(slot, jnp.asarray(piece_rows()), pos, alt, rows, table, states, w_span, q, og, w_q, w_o, w_d, wqo)


def body(
    span_states,
    queries,
    out_grad,
    neighbour_ids,
    assignment,
    embed_table,
    w_span_kv,
    w_query_enc,
    w_out_enc,
    w_dec_kv,
):
    bf16 = jnp.bfloat16
    n_span = lax.axis_size("span")
    span_index = lax.axis_index("span")
    half_index = lax.axis_index("mp")
    seq_count, local_tokens, half_width = span_states.shape
    spans = local_tokens // CH
    units = spans * NB
    dec_cols = 2 * queries.shape[2]
    vocab_rows = embed_table.shape[0]
    tokens = units * R

    ids_m = lax.dynamic_index_in_dim(
        neighbour_ids.reshape(seq_count, n_span, tokens), half_index, 0, keepdims=False
    )
    rows, pos, over = lists(ids_m, span_index, vocab_rows, n_span)

    def whole_gather():
        shifted = ids_m.reshape(-1) - span_index * vocab_rows
        inside = (shifted >= 0) & (shifted < vocab_rows)
        found = jnp.take(embed_table, jnp.clip(shifted, 0, vocab_rows - 1), axis=0)
        found = jnp.where(inside[:, None], found, jnp.zeros_like(found))
        found = lax.all_to_all(
            found.reshape(n_span, tokens, DE), "span", split_axis=0, concat_axis=0, tiled=True
        )
        return jnp.sum(found.astype(F32), axis=0).astype(bf16)

    alt = lax.cond(over, whole_gather, lambda: jnp.zeros((tokens, DE), bf16))

    core = lax.axis_index("dp") % 2
    wqo = []
    for r in range(2):
        group = span_index % 4 if r == 0 else span_index // 4
        start = (core * 2 + r) * 112
        from_q = lax.dynamic_slice(w_query_enc, (group * HALF + start, 0), (112, HALF))
        from_o = lax.dynamic_slice(w_out_enc, (start, (group - 2) * 512), (112, 512))
        from_q = jnp.concatenate([from_q[:, :384], from_q[:, HALF - 128 :]], axis=1)
        wqo.append(jnp.where(group < 2, from_q, from_o))
    wqo = jnp.transpose(jnp.stack(wqo).reshape(2, 112, 4, 128), (0, 2, 1, 3))

    dest = lax.dynamic_index_in_dim(assignment[0, :, :, 0], span_index, 0, keepdims=False)
    at = dest[None, :] == jnp.arange(n_span, dtype=jnp.int32)[:, None]
    numbers = jnp.arange(seq_count * units, dtype=jnp.int32)
    slot = jnp.stack(
        [
            jnp.sum(jnp.where(at, numbers[None, :], 0), axis=1),
            jnp.sum(at.astype(jnp.int32), axis=1),
            jnp.full((n_span,), over.astype(jnp.int32)),
        ]
    )
    attended_out, cross_out, rq, ro = run(
        slot,
        pos[:, None],
        alt,
        rows.reshape(-1, 1),
        embed_table,
        span_states.reshape(-1, half_width),
        w_span_kv,
        queries,
        out_grad,
        w_query_enc,
        w_out_enc,
        w_dec_kv.reshape(DE, dec_cols),
        wqo,
    )
    grad_query_enc = lax.dynamic_slice_in_dim(rq[:PIECE], half_index * HALF, HALF, 1)
    grad_out_enc = lax.dynamic_slice_in_dim(ro[:PIECE], half_index * HALF, HALF, 1).T
    return (
        cross_out,
        attended_out.reshape(1, 1, n_span, 1, R, HALF),
        grad_query_enc,
        grad_out_enc,
    )


def solution(mesh):
    return jax.shard_map(
        body,
        mesh=mesh,
        in_specs=(
            P("dp", "span", "mp"),
            P("dp", "span", "mp"),
            P("dp", "span", "mp"),
            P("dp", None, None, None),
            P("dp", None, None, None),
            P("span", None),
            P("mp", None),
            P(None, "mp"),
            P("mp", None),
            P(None, None, "mp"),
        ),
        out_specs=(
            P("dp", "span", "mp"),
            P("dp", "span", None, None, None, "mp"),
            P(("span", "dp"), "mp"),
            P("mp", ("span", "dp")),
        ),
        check_vma=False,
    )
```

```python
import math

import jax
import jax.numpy as jnp
import numpy as np
from jax import lax
from jax.experimental import pallas as pl
from jax.experimental.pallas import tpu as pltpu
from jax.sharding import PartitionSpec as P

HD = 128
DE = 896
EHD = 64
R = 128
CH = 64
NB = 2
ROOM = 48


def lists(ids_m, span_index, vocab_rows, n_span):
    tokens = ids_m.shape[1]
    t = jnp.arange(tokens, dtype=jnp.int32)
    same = ids_m[:, :, None] == ids_m[:, None, :]
    dup = jnp.any(same & (t[None, None, :] < t[None, :, None]), axis=2)
    uniq = jnp.logical_not(dup)
    src = ids_m // vocab_rows
    shards = jnp.arange(n_span, dtype=jnp.int32)
    counts = jnp.sum(
        (uniq[:, None, :] & (src[:, None, :] == shards[None, :, None])).astype(jnp.int32), axis=2
    )
    over = jnp.max(counts) > ROOM
    sel = uniq & (src == span_index)
    tri = (t[:, None] < t[None, :]).astype(jnp.bfloat16)
    rank = jnp.dot(sel.astype(jnp.bfloat16), tri, preferred_element_type=jnp.float32).astype(
        jnp.int32
    )
    room = jnp.arange(ROOM, dtype=jnp.int32)
    local = ids_m - span_index * vocab_rows
    rows = jnp.sum(
        jnp.where(
            (rank[:, None, :] == room[None, :, None]) & sel[:, None, :], local[:, None, :], 0
        ),
        axis=2,
    )
    own = lax.dynamic_index_in_dim(ids_m, span_index, 0, keepdims=False)
    own_src = own // vocab_rows
    own_same = own[:, None] == own[None, :]
    first = jnp.min(jnp.where(own_same, t[None, :], tokens), axis=1)
    own_uniq = first == t
    own_rank = jnp.sum(
        (
            own_uniq[None, :]
            & (own_src[:, None] == own_src[None, :])
            & (t[None, :] < first[:, None])
        ).astype(jnp.int32),
        axis=1,
    )
    return rows, own_src * ROOM + own_rank, over


F32 = jnp.float32
BF16 = jnp.bfloat16
PAIR = 2 * EHD
HEADS_ENC = DE // EHD
PAIRS = HEADS_ENC // 2
TOK = 512
SPANS = 2
DEC = 2048
HALF = DE // 2
PADDED = 1024
PIECE = 14
TILES = ((0, 256), (256, 256), (512, 256), (768, 128))


def dot(a, b):
    return jnp.dot(a, b, preferred_element_type=F32)


def dot_nt(a, b):
    return lax.dot_general(a, b, (((1,), (1,)), ((), ())), preferred_element_type=F32)


def dot_tn(a, b):
    return lax.dot_general(a, b, (((0,), (0,)), ((), ())), preferred_element_type=F32)


def piece_rows():
    rows = np.full((2, PADDED), -1, np.int32)
    n = 0
    for core in range(2):
        for first in range(4):
            for second in range(4):
                for low in range(2):
                    for r in range(16):
                        if r < PIECE:
                            rows[0, n] = (((first * 4 + second) * 2 + low) * 2 + core) * PIECE + r
                            rows[1, n] = (((second * 4 + first) * 2 + low) * 2 + core) * PIECE + r
                        n += 1
    return rows


def pair_blocks(kv_ref, c, j, low, high):
    rows = slice(c * CH, (c + 1) * CH)
    k = kv_ref[rows, pl.ds(pl.multiple_of(j * PAIR, PAIR), PAIR)]
    v = kv_ref[rows, pl.ds(pl.multiple_of(DE + j * PAIR, PAIR), PAIR)]
    return (
        jnp.concatenate([k * low, k * high], axis=0),
        jnp.concatenate([v * low, v * high], axis=0),
    )


def mega(
    slot_ref,
    rows_ref,
    pos_ref,
    alt_ref,
    list_ref,
    table_ref,
    states_ref,
    wspan_ref,
    q_ref,
    og_ref,
    wq_own_ref,
    wo_own_ref,
    wd_ref,
    wqo_ref,
    att_out,
    cross_out,
    rq_ref,
    ro_ref,
    picked_ref,
    sent_ref,
    got_ref,
    emb_ref,
    kvp_ref,
    kvg_ref,
    kv_ref,
    qo_ref,
    ogo_ref,
    wb_ref,
    sb_ref,
    wq_ref,
    wo_ref,
    eq_ref,
    att_ref,
    probs_ref,
    enc_ref,
    dkv_ref,
    gkv_ref,
    sum_ref,
    pad_ref,
    pad_emb_ref,
    cross_ref,
    all_ref,
    slots_ref,
    g_ref,
    core_ref,
    acc1_ref,
    first_ref,
    acc2_ref,
    second_ref,
    acc3_ref,
    last_ref,
    emb_sems,
    swap_sems,
    weight_sems,
    slot_sems,
    sum_sems,
    local_sems,
):
    span, dp, half = lax.axis_index("span"), lax.axis_index("dp"), lax.axis_index("mp")
    z, y, x_low, core = span // 4, span % 4, dp // 2, dp % 2
    partner = {"span": span, "dp": dp, "mp": 1 - half}
    peer = {"span": span, "dp": x_low * 2 + 1 - core, "mp": half}
    where = (z, y)

    offsets = ((0, 1), (1, 0), (0, 3), (3, 0), (2, 1), (1, 2), (2, 3), (3, 2), (1, 1), (3, 3), (1, 3), (3, 1), (2, 0), (0, 2), (2, 2))

    def span_at(k):
        return lax.rem(z + offsets[k][0], 4) * 4 + lax.rem(y + offsets[k][1], 4)

    def in_span(k):
        return {"span": span_at(k), "dp": dp, "mp": half}

    def along(axis, by):
        if axis == 0:
            return {"span": lax.rem(z + by + 4, 4) * 4 + y, "dp": dp, "mp": half}
        return {"span": z * 4 + lax.rem(y + by + 4, 4), "dp": dp, "mp": half}

    others = [
        {"span": span, "dp": (1 - x_low) * 2 + core, "mp": half},
        partner,
        {"span": span, "dp": (1 - x_low) * 2 + core, "mp": 1 - half},
    ]
    def area(i):
        return (dkv_ref, gkv_ref)[i // 4].at[(i // 2) % 2, :, pl.ds((i % 2) * 1024, DE)]

    vocab = table_ref.shape[0]
    sizes = [min(512, vocab - at) for at in range(0, vocab, 512)]
    table_in = [
        pltpu.make_async_copy(
            table_ref.at[pl.ds(i * 512, size)], area(i).at[pl.ds(0, size)], local_sems.at[5 + i]
        )
        for i, size in enumerate(sizes)
    ]
    spans_in = [
        pltpu.make_async_copy(
            wspan_ref.at[pl.ds(i * 512, 512)],
            (dkv_ref, gkv_ref)[i // 2].at[i % 2, :, pl.ds(0, 2 * DE)],
            local_sems.at[i],
        )
        for i in range(4)
    ]
    alt_in = pltpu.make_async_copy(alt_ref, eq_ref, local_sems.at[4])
    for copy in table_in:
        copy.start()
    alt_in.start()

    barrier = pltpu.get_barrier_semaphore()
    friends = [in_span(k) for k in range(15)] + [peer] + others
    for friend in friends:
        pl.semaphore_signal(barrier, inc=1, device_id=friend, device_id_type=pl.DeviceIdType.MESH)
    pl.semaphore_wait(barrier, len(friends))

    def send(src, dst, sems, device):
        copy = pltpu.make_async_remote_copy(
            src_ref=src,
            dst_ref=dst,
            send_sem=sems.at[0],
            recv_sem=sems.at[1],
            device_id=device,
            device_id_type=pl.DeviceIdType.MESH,
        )
        copy.start()
        return copy

    def add(*parts):
        total = parts[0].astype(F32)
        for part in parts[1:]:
            total = total + part.astype(F32)
        return total

    def mod(v):
        return lax.rem(v + 4, 4)

    ranks = ((z, y), (y, z))

    def at(kind, r, group, piece, count):
        n = core * 2 + r
        if kind:
            return wb_ref.at[
                pl.ds(pl.multiple_of(n * 224, 224), 224),
                pl.ds(pl.multiple_of(group * 512 + piece * 128, 128), count * 128),
            ]
        return sb_ref.at[pl.ds(group * 4 + piece, count), pl.ds(pl.multiple_of(n * 112, 112), 112)]

    def weight_steps(kind):
        sems = weight_sems.at[kind]
        copies = []
        for r in range(2):
            s = ranks[r][1]
            n = core * 2 + r
            if kind:
                src = wd_ref.at[
                    pl.ds(pl.multiple_of(n * 224, 224), 224), pl.ds(pl.multiple_of(s * 512, 512), 512)
                ]
            else:
                src = wqo_ref.at[r]
            copies.append([send(src, at(kind, r, s, 0, 4), sems.at[r, 0], others[2])])
        yield
        for r in range(2):
            s = ranks[r][1]
            for copy in copies[r]:
                copy.wait()
            whole = at(kind, r, s, 0, 4)
            copies[r] = [
                send(whole, whole, sems.at[r, 1 + i], along(1 - r, by)) for i, by in enumerate((1, -1))
            ]
        yield
        for r in range(2):
            s = ranks[r][1]
            for copy in copies[r]:
                copy.wait()
            copies[r] = []
            for i, by in enumerate((1, -1)):
                part = at(kind, r, mod(s - by), 2 * i, 2)
                copies[r].append(send(part, part, sems.at[r, 3 + i], along(1 - r, by)))
        yield
        for r in range(2):
            for copy in copies[r]:
                copy.wait()
            n = core * 2 + r
            if kind:
                mine = wb_ref.at[pl.ds(pl.multiple_of(n * 224, 224), 224)]
            else:
                mine = sb_ref.at[:, pl.ds(pl.multiple_of(n * 112, 112), 112)]
            copies[r] = [send(mine, mine, sems.at[r, 5], peer)]
        yield
        for r in range(2):
            for copy in copies[r]:
                copy.wait()
        yield

    small_steps, wide_steps = weight_steps(0), weight_steps(1)
    next(small_steps)
    next(wide_steps)

    rank = lax.broadcasted_iota(jnp.int32, (1, 512), 1)
    for i, size in enumerate(sizes):
        table_in[i].wait()
        chosen = (list_ref[...] == rank + i * 512).astype(F32).astype(BF16)
        part = dot(chosen[:, :size], area(i)[:size, :])
        if i == 0:
            sum_ref[...], picked_ref[...] = part[:TOK], part[TOK:]
        else:
            sum_ref[...] += part[:TOK]
            picked_ref[...] += part[TOK:]
        if i == 4:
            next(small_steps)
    picked = jnp.concatenate([sum_ref[...], picked_ref[...]], axis=0)
    sent_ref[...] = picked.astype(BF16).reshape(16, ROOM, DE)
    for copy in spans_in:
        copy.start()
    embs = [
        send(sent_ref.at[span_at(k)], got_ref.at[span], emb_sems.at[k], in_span(k))
        for k in range(15)
    ]
    got_ref[span] = sent_ref[span]
    next(small_steps)
    next(wide_steps)

    for copy in spans_in:
        copy.wait()

    def project_span(i, _):
        cols = pl.ds(pl.multiple_of(i * 256, 256), 256)
        total = jnp.zeros((2 * SPANS * CH, 256), F32)
        for n in range(4):
            total += dot(states_ref[:, n * 512 : (n + 1) * 512], (dkv_ref, gkv_ref)[n // 2][n % 2, :, cols])
        total = total.astype(BF16)
        kvp_ref[0, :, cols] = total[: SPANS * CH]
        kvp_ref[1, :, cols] = total[SPANS * CH :]
        return 0

    lax.fori_loop(0, 2 * DE // 256, project_span, 0)
    kv_swap = send(kvp_ref.at[1 - half], kvg_ref, swap_sems.at[0], partner)
    q_swap = send(q_ref.at[1 - half], qo_ref, swap_sems.at[1], partner)
    og_swap = send(og_ref.at[1 - half], ogo_ref, swap_sems.at[2], partner)

    next(small_steps)
    next(small_steps)

    place = lax.broadcasted_iota(jnp.int32, (HALF, 256), 0)
    wide = lax.broadcasted_iota(jnp.int32, (512, 256), 0)
    wide = jnp.where(wide < 384, wide, jnp.where(wide >= 448, wide - 64, -DE))
    col = lax.broadcasted_iota(jnp.int32, (HALF, 256), 1)
    wide_col = lax.broadcasted_iota(jnp.int32, (512, 256), 1)
    for lane_at, size in TILES:
        mine = (place + half * HALF == col + lane_at).astype(F32).astype(BF16)[:, :size]
        his = (wide + (1 - half) * HALF == wide_col + lane_at).astype(F32).astype(BF16)[:, :size]
        for up in range(2):
            rows = slice(up * HALF, (up + 1) * HALF)
            other = jnp.concatenate([sb_ref[up * 4 + i] for i in range(4)], axis=1)
            wq_ref[rows, lane_at : lane_at + size] = (dot(wq_own_ref[rows, :], mine) + dot(other, his)).astype(BF16)
    wo_ref[pl.ds(pl.multiple_of(half * HALF, HALF), HALF), :] = wo_own_ref[...]
    for i in range(7):
        wo_ref[pl.ds(pl.multiple_of((1 - half) * HALF, HALF), HALF), i * 128 : (i + 1) * 128] = sb_ref[8 + i if i < 4 else 9 + i]

    for copy in embs:
        copy.wait()
    next(wide_steps)
    alt_in.wait()
    slot_of = lax.broadcasted_iota(jnp.int32, (1, 16 * ROOM), 1)
    pick = (pos_ref[...] == slot_of).astype(F32).astype(BF16)
    over = slot_ref[2, 0] > 0
    for lane_at, size in TILES:
        cols = slice(lane_at, lane_at + size)
        rows = jnp.concatenate([got_ref[i, :, cols] for i in range(16)], axis=0)
        emb_ref[:, cols] = jnp.where(over, eq_ref[:, cols].astype(F32), dot(pick, rows)).astype(BF16)

    lane = lax.broadcasted_iota(jnp.int32, (1, PAIR), 1)
    is_low = lane < EHD
    low = is_low.astype(F32).astype(BF16)
    high = (lane >= EHD).astype(F32).astype(BF16)

    def pad(to_ref, ref, order):
        for lane_at in range(0, PADDED, 256):
            spread = (
                lax.broadcasted_iota(jnp.int32, (DE, 256), 0)
                == rows_ref[order : order + 1, lane_at : lane_at + 256]
            )
            to_ref[:, lane_at : lane_at + 256] = dot(ref[...], spread.astype(F32).astype(BF16)).astype(BF16)

    for lane_at, size in TILES:
        cols = slice(lane_at, lane_at + size)
        eq_ref[:, cols] = dot(emb_ref[...], wq_ref[:, cols]).astype(BF16)

    def forward(j, _):
        cols = pl.ds(pl.multiple_of(j * PAIR, PAIR), PAIR)
        for c in range(SPANS):
            rows = slice(c * NB * R, (c + 1) * NB * R)
            kbd, vbd = pair_blocks(kv_ref, c, j, low, high)
            s = dot_nt(eq_ref[rows, cols], kbd) * (1.0 / math.sqrt(EHD))
            top0 = jnp.max(jnp.where(is_low, s, -jnp.inf), axis=1, keepdims=True)
            top1 = jnp.max(jnp.where(is_low, -jnp.inf, s), axis=1, keepdims=True)
            p = jnp.exp(s - jnp.where(is_low, top0, top1))
            sum0 = jnp.sum(jnp.where(is_low, p, 0.0), axis=1, keepdims=True)
            sum1 = jnp.sum(jnp.where(is_low, 0.0, p), axis=1, keepdims=True)
            p = p * jnp.where(is_low, 1.0 / sum0, 1.0 / sum1)
            probs_ref[c, j] = p
            att_ref[rows, cols] = dot(p.astype(BF16), vbd).astype(BF16)
        return 0

    kv_swap.wait()
    kv_ref[...] = add(kvp_ref[half], kvg_ref[...]).astype(BF16)
    lax.fori_loop(0, PAIRS, forward, 0)
    next(wide_steps)

    feature = lax.broadcasted_iota(jnp.int32, (DE, HALF), 0)
    column = lax.broadcasted_iota(jnp.int32, (DE, HALF), 1)

    def half_of(which):
        chosen = (feature == column + which * HALF).astype(F32).astype(BF16)
        return dot(att_ref[...], chosen).astype(BF16)

    slots_ref[0:4] = half_of(1 - half).reshape(4, R, HALF)
    att_swap = send(slots_ref.at[pl.ds(0, 4)], all_ref.at[half], swap_sems.at[3], partner)
    all_ref[half] = half_of(half).reshape(4, R, HALF)

    for lane_at, size in TILES:
        cols = slice(lane_at, lane_at + size)
        enc_ref[:, cols] = (emb_ref[:, cols].astype(F32) + dot(att_ref[...], wo_ref[:, cols])).astype(BF16)

    def project_own(i, _):
        cols = pl.ds(pl.multiple_of(i * 256, 256), 256)
        dkv_ref[0, :, cols] = dot(enc_ref[...], wd_ref[:, cols]).astype(BF16)
        return 0

    def project_other(i, _):
        cols = pl.ds(pl.multiple_of(i * 256, 256), 256)
        dkv_ref[1, :, cols] = dot(enc_ref[...], wb_ref[:, cols]).astype(BF16)
        return 0

    lax.fori_loop(0, DEC // 256, project_own, 0)
    pad(pad_emb_ref, emb_ref, 0)
    next(wide_steps)
    lax.fori_loop(0, DEC // 256, project_other, 0)

    att_swap.wait()
    for e in range(16):
        unit, there = slot_ref[0, e], slot_ref[1, e]
        slots_ref[e] = all_ref[unit // 4, unit % 4] * there.astype(F32).astype(BF16)
    waiting = [
        send(slots_ref.at[span_at(k)], att_out.at[span], slot_sems.at[k], in_span(k))
        for k in range(15)
    ]
    stay = pltpu.make_async_copy(slots_ref.at[span], att_out.at[span], local_sems.at[0])
    stay.start()
    q_swap.wait()
    og_swap.wait()
    scale = 1.0 / math.sqrt(HD)

    def decode(h, _):
        kcols = pl.ds(pl.multiple_of(h * HD, HD), HD)
        vcols = pl.ds(pl.multiple_of(DEC // 2 + h * HD, HD), HD)
        for g in range(2):
            for c in range(SPANS):
                few = slice(c * CH, (c + 1) * CH)
                rows = slice(c * NB * R, (c + 1) * NB * R)
                q = q_ref[half, few, kcols] if g == 0 else qo_ref[few, kcols]
                og = og_ref[half, few, kcols] if g == 0 else ogo_ref[few, kcols]
                k, v = dkv_ref[g, rows, kcols], dkv_ref[g, rows, vcols]
                s = dot_nt(q, k) * scale
                p = jnp.exp(s - jnp.max(s, axis=1, keepdims=True))
                p = p * (1.0 / jnp.sum(p, axis=1, keepdims=True))
                pb = p.astype(BF16)
                cross = dot(pb, v).astype(BF16)
                cross_ref[g, few, kcols] = cross
                gkv_ref[g, rows, vcols] = dot_tn(pb, og).astype(BF16)
                row = jnp.sum(og.astype(F32) * cross.astype(F32), axis=1, keepdims=True)
                ds = (p * (dot_nt(og, v) - row) * scale).astype(BF16)
                gkv_ref[g, rows, kcols] = dot_tn(ds, q).astype(BF16)
        return 0

    lax.fori_loop(0, 8, decode, 0)
    waiting.append(send(cross_ref.at[1], cross_out.at[half], swap_sems.at[4], partner))
    mine = pltpu.make_async_copy(cross_ref.at[0], cross_out.at[half], local_sems.at[1])
    mine.start()
    sum_ref[...] = jnp.zeros_like(sum_ref)

    def collect(i, _):
        cols = pl.ds(pl.multiple_of(i * 256, 256), 256)
        sum_ref[...] += dot_nt(gkv_ref[0, :, cols], wd_ref[:, cols]) + dot_nt(
            gkv_ref[1, :, cols], wb_ref[:, cols]
        )
        return 0

    lax.fori_loop(0, DEC // 256, collect, 0)
    enc_ref[...] = sum_ref[...].astype(BF16)

    def steps(job):
        k, lanes = ((0, slice(0, 512)), (0, slice(512, DE)), (1, slice(0, DE)))[job]
        wide = pl.ds(lanes.start, lanes.stop - lanes.start)
        axis = (0, 1, 1)[job]
        flip = job == 1
        p, q = where[axis], where[1 - axis]
        sems = sum_sems.at[job]
        copies = [
            send(g_ref.at[k, 1 - core, :, :, :, :, wide], core_ref.at[k, :, :, :, :, wide], sems.at[0], peer)
        ]
        yield
        copies[0].wait()
        for i in range(4):
            acc1_ref[k, i, :, :, :, lanes] = add(
                g_ref[k, core, i, :, :, :, lanes], core_ref[k, i, :, :, :, lanes]
            ).astype(BF16)
        copies = []
        for j in range(1, 4):
            to = mod(p + j)
            block = acc1_ref.at[k, :, to, :, :, wide] if flip else acc1_ref.at[k, to, :, :, :, wide]
            copies.append(send(block, first_ref.at[k, j - 1, :, :, :, wide], sems.at[j], along(axis, j)))
        yield
        for copy in copies:
            copy.wait()
        own = acc1_ref[k, :, p, :, :, lanes] if flip else acc1_ref[k, p, :, :, :, lanes]
        acc2_ref[k, :, :, :, lanes] = add(own, *[first_ref[k, j, :, :, :, lanes] for j in range(3)]).astype(BF16)
        copies = [
            send(
                acc2_ref.at[k, mod(q + j), :, :, wide],
                second_ref.at[k, j - 1, :, :, wide],
                sems.at[3 + j],
                along(1 - axis, j),
            )
            for j in range(1, 4)
        ]
        yield
        for copy in copies:
            copy.wait()
        acc3_ref[k, :, :, lanes] = add(
            acc2_ref[k, q, :, :, lanes], *[second_ref[k, j, :, :, lanes] for j in range(3)]
        ).astype(BF16)
        copies = []
        for n, other in enumerate(others):
            to_low = x_low if n == 1 else 1 - x_low
            copies.append(
                send(acc3_ref.at[k, to_low, :, wide], last_ref.at[k, n, :, wide], sems.at[7 + n], other)
            )
        yield
        for copy in copies:
            copy.wait()
        (rq_ref, ro_ref)[k][:, lanes] = add(
            acc3_ref[k, x_low, :, lanes], *[last_ref[k, n, :, lanes] for n in range(3)]
        )
        yield

    def outer(k, padded_ref, ref, lanes):
        def tile(i, _):
            cols = pl.ds(pl.multiple_of(i * 256, 256), 256)
            g_ref[k, i // 2, pl.ds((i % 2) * 2, 2), :, :, :, lanes] = (
                dot_tn(padded_ref[:, cols], ref[:, lanes]).astype(BF16).reshape(2, 4, 2, 16, -1)
            )
            return 0

        lax.fori_loop(0, PADDED // 256, tile, 0)

    pad(pad_ref, enc_ref, 1)
    outer(1, pad_ref, att_ref, slice(0, DE))
    out_sum = steps(2)
    next(out_sum)
    for lane_at, size in TILES:
        cols = slice(lane_at, lane_at + size)
        eq_ref[:, cols] = dot_nt(enc_ref[...], wo_ref[cols, :]).astype(BF16)
    next(out_sum)

    def backward(j, _):
        cols = pl.ds(pl.multiple_of(j * PAIR, PAIR), PAIR)
        for c in range(SPANS):
            rows = slice(c * NB * R, (c + 1) * NB * R)
            kbd, vbd = pair_blocks(kv_ref, c, j, low, high)
            ga = eq_ref[rows, cols]
            prod = ga.astype(F32) * att_ref[rows, cols].astype(F32)
            row0 = jnp.sum(jnp.where(is_low, prod, 0.0), axis=1, keepdims=True)
            row1 = jnp.sum(jnp.where(is_low, 0.0, prod), axis=1, keepdims=True)
            diff = dot_nt(ga, vbd) - jnp.where(is_low, row0, row1)
            ds = (probs_ref[c, j] * diff * (1.0 / math.sqrt(EHD))).astype(BF16)
            eq_ref[rows, cols] = dot(ds, kbd).astype(BF16)
        return 0

    lax.fori_loop(0, 4, backward, 0)
    outer(0, pad_emb_ref, eq_ref, slice(0, 512))
    low_sum = steps(0)
    next(low_sum)
    lax.fori_loop(4, PAIRS, backward, 0)
    next(low_sum)
    next(out_sum)
    outer(0, pad_emb_ref, eq_ref, slice(512, DE))
    high_sum = steps(1)
    next(high_sum)
    next(high_sum)
    next(low_sum)
    next(out_sum)
    next(high_sum)
    next(low_sum)
    next(out_sum)
    next(high_sum)
    next(low_sum)
    next(high_sum)
    for copy in waiting:
        copy.wait()
    mine.wait()
    stay.wait()


def run(slot, pos, alt, rows, table, states, w_span, q, og, w_q, w_o, w_d, wqo):
    vmem = pl.BlockSpec(memory_space=pltpu.VMEM)
    anywhere = pl.BlockSpec(memory_space=pl.ANY)
    dma = pltpu.SemaphoreType.DMA
    return pl.pallas_call(
        mega,
        out_shape=(
            jax.ShapeDtypeStruct((16, R, HALF), BF16),
            jax.ShapeDtypeStruct((2, SPANS * CH, DEC // 2), BF16),
            jax.ShapeDtypeStruct((16, DE), F32),
            jax.ShapeDtypeStruct((16, DE), F32),
        ),
        in_specs=[pl.BlockSpec(memory_space=pltpu.SMEM), vmem, vmem, anywhere, vmem, anywhere, vmem, anywhere]
        + [vmem] * 6,
        out_specs=(anywhere, anywhere, vmem, vmem),
        scratch_shapes=[
            pltpu.VMEM((16 * ROOM - TOK, DE), F32),
            pltpu.VMEM((16, ROOM, DE), BF16),
            pltpu.VMEM((16, ROOM, DE), BF16),
            pltpu.VMEM((TOK, DE), BF16),
            pltpu.VMEM((2, SPANS * CH, 2 * DE), BF16),
            pltpu.VMEM((SPANS * CH, 2 * DE), BF16),
            pltpu.VMEM((SPANS * CH, 2 * DE), BF16),
            pltpu.VMEM((SPANS * CH, DEC // 2), BF16),
            pltpu.VMEM((SPANS * CH, DEC // 2), BF16),
            pltpu.VMEM((DE, DEC), BF16),
            pltpu.VMEM((16, HALF, 128), BF16),
            pltpu.VMEM((DE, DE), BF16),
            pltpu.VMEM((DE, DE), BF16),
            pltpu.VMEM((TOK, DE), BF16),
            pltpu.VMEM((TOK, DE), BF16),
            pltpu.VMEM((SPANS, PAIRS, NB * R, PAIR), F32),
            pltpu.VMEM((TOK, DE), BF16),
            pltpu.VMEM((2, TOK, DEC), BF16),
            pltpu.VMEM((2, TOK, DEC), BF16),
            pltpu.VMEM((TOK, DE), F32),
            pltpu.VMEM((TOK, PADDED), BF16),
            pltpu.VMEM((TOK, PADDED), BF16),
            pltpu.VMEM((2, SPANS * CH, DEC // 2), BF16),
            pltpu.VMEM((2, 4, R, HALF), BF16),
            pltpu.VMEM((16, R, HALF), BF16),
            pltpu.VMEM((2, 2, 4, 4, 2, 16, DE), BF16),
            pltpu.VMEM((2, 4, 4, 2, 16, DE), BF16),
            pltpu.VMEM((2, 4, 4, 2, 16, DE), BF16),
            pltpu.VMEM((2, 3, 4, 2, 16, DE), BF16),
            pltpu.VMEM((2, 4, 2, 16, DE), BF16),
            pltpu.VMEM((2, 3, 2, 16, DE), BF16),
            pltpu.VMEM((2, 2, 16, DE), BF16),
            pltpu.VMEM((2, 3, 16, DE), BF16),
            dma((15, 2)),
            dma((5, 2)),
            dma((2, 2, 6, 2)),
            dma((15, 2)),
            dma((3, 10, 2)),
            dma((13,)),
        ],
        compiler_params=pltpu.CompilerParams(
            vmem_limit_bytes=63 * 2**20, collective_id=1, has_side_effects=True
        ),
        cost_estimate=pl.CostEstimate(
            flops=16 * 10**9, bytes_accessed=30 * 2**20, transcendentals=10**6
        ),
    )(slot, jnp.asarray(piece_rows()), pos, alt, rows, table, states, w_span, q, og, w_q, w_o, w_d, wqo)


def body(
    span_states,
    queries,
    out_grad,
    neighbour_ids,
    assignment,
    embed_table,
    w_span_kv,
    w_query_enc,
    w_out_enc,
    w_dec_kv,
):
    bf16 = jnp.bfloat16
    n_span = lax.axis_size("span")
    span_index = lax.axis_index("span")
    half_index = lax.axis_index("mp")
    seq_count, local_tokens, half_width = span_states.shape
    spans = local_tokens // CH
    units = spans * NB
    dec_cols = 2 * queries.shape[2]
    vocab_rows = embed_table.shape[0]
    tokens = units * R

    ids_m = lax.dynamic_index_in_dim(
        neighbour_ids.reshape(seq_count, n_span, tokens), half_index, 0, keepdims=False
    )
    rows, pos, over = lists(ids_m, span_index, vocab_rows, n_span)

    def whole_gather():
        shifted = ids_m.reshape(-1) - span_index * vocab_rows
        inside = (shifted >= 0) & (shifted < vocab_rows)
        found = jnp.take(embed_table, jnp.clip(shifted, 0, vocab_rows - 1), axis=0)
        found = jnp.where(inside[:, None], found, jnp.zeros_like(found))
        found = lax.all_to_all(
            found.reshape(n_span, tokens, DE), "span", split_axis=0, concat_axis=0, tiled=True
        )
        return jnp.sum(found.astype(F32), axis=0).astype(bf16)

    alt = lax.cond(over, whole_gather, lambda: jnp.zeros((tokens, DE), bf16))

    core = lax.axis_index("dp") % 2
    wqo = []
    for r in range(2):
        group = span_index % 4 if r == 0 else span_index // 4
        start = (core * 2 + r) * 112
        from_q = lax.dynamic_slice(w_query_enc, (group * HALF + start, 0), (112, HALF))
        from_o = lax.dynamic_slice(w_out_enc, (start, (group - 2) * 512), (112, 512))
        from_q = jnp.concatenate([from_q[:, :384], from_q[:, HALF - 128 :]], axis=1)
        wqo.append(jnp.where(group < 2, from_q, from_o))
    wqo = jnp.transpose(jnp.stack(wqo).reshape(2, 112, 4, 128), (0, 2, 1, 3))

    dest = lax.dynamic_index_in_dim(assignment[0, :, :, 0], span_index, 0, keepdims=False)
    at = dest[None, :] == jnp.arange(n_span, dtype=jnp.int32)[:, None]
    numbers = jnp.arange(seq_count * units, dtype=jnp.int32)
    slot = jnp.stack(
        [
            jnp.sum(jnp.where(at, numbers[None, :], 0), axis=1),
            jnp.sum(at.astype(jnp.int32), axis=1),
            jnp.full((n_span,), over.astype(jnp.int32)),
        ]
    )
    attended_out, cross_out, rq, ro = run(
        slot,
        pos[:, None],
        alt,
        rows.reshape(-1, 1),
        embed_table,
        span_states.reshape(-1, half_width),
        w_span_kv,
        queries,
        out_grad,
        w_query_enc,
        w_out_enc,
        w_dec_kv.reshape(DE, dec_cols),
        wqo,
    )
    grad_query_enc = lax.dynamic_slice_in_dim(rq[:PIECE], half_index * HALF, HALF, 1)
    grad_out_enc = lax.dynamic_slice_in_dim(ro[:PIECE], half_index * HALF, HALF, 1).T
    return (
        cross_out,
        attended_out.reshape(1, 1, n_span, 1, R, HALF),
        grad_query_enc,
        grad_out_enc,
    )


def solution(mesh):
    return jax.shard_map(
        body,
        mesh=mesh,
        in_specs=(
            P("dp", "span", "mp"),
            P("dp", "span", "mp"),
            P("dp", "span", "mp"),
            P("dp", None, None, None),
            P("dp", None, None, None),
            P("span", None),
            P("mp", None),
            P(None, "mp"),
            P("mp", None),
            P(None, None, "mp"),
        ),
        out_specs=(
            P("dp", "span", "mp"),
            P("dp", "span", None, None, None, "mp"),
            P(("span", "dp"), "mp"),
            P("mp", ("span", "dp")),
        ),
        check_vma=False,
    )
```
